32 devices in a mesh: imgs: 8 (over z, core), rows: 4 (over y, x).
Axes of the slice: x: 2, y: 2, z: 4, core: 2. Of those that a mesh axis runs over, the one named last changes fastest.
Arguments:
- image_in: bfloat16 [32, 32, 32, 512], P('imgs', 'rows')
- panel_kind: int32 [32], P('imgs'), may hold values from 0 to 3, as said below
- owner_slot: int32 [22], replicated, may hold values from 0 to 31, as said below
- out_grad: bfloat16 [32, 32, 32, 512], P('imgs', 'rows'), may hold values from -6 to 6
- master: float32 [32, 512, 512], P('imgs', 'rows')
- first_moment: float32 [32, 512, 512], P('imgs', 'rows')
- second_moment: float32 [32, 512, 512], P('imgs', 'rows'), as said below
- vec_master: float32 [11, 512], replicated
- vec_first: float32 [11, 512], replicated
- vec_second: float32 [11, 512], replicated, as said below
Outputs:
- block_out: bfloat16 [32, 32, 32, 512], P('imgs', 'rows')
- input_grad: bfloat16 [32, 32, 32, 512], P('imgs', 'rows')
- new_first: float32 [32, 512, 512], P('imgs', 'rows')
- new_second: float32 [32, 512, 512], P('imgs', 'rows')
- new_master: float32 [32, 512, 512], P('imgs', 'rows')
- vec_first_new: float32 [11, 512], replicated
- vec_second_new: float32 [11, 512], replicated
- vec_master_new: float32 [11, 512], replicated
The draws below stay inside these ranges and needn't reach their ends.
Inputs may be any that keep to these rules, and one draw needn't show every extreme that they name: `panel_kind`: kind 0: one image of 32 x 32; kind 1: one image of 24 rows and columns at the top left; kind 2: four images of 16 in the quadrants; kind 3: empty. Every aligned block of 4 panels holds a panel of kind 0. `owner_slot`: slots k * 4 to k * 4 + 3 belong to index k of imgs; no slot is named twice; some index of imgs owns 4 matrices. `second_moment`: positive. `vec_second`: positive.
All inputs are finite; a program needn't handle non-finite values.
Results may differ from the reference program's by a relative error of at most 0.025.
Values may be sent and summed in bfloat16 or wider, within the bound.
No kernel may reach another device: no remote copies, remote signals or barrier semaphores. Data moves between devices by JAX's collectives and lax.ppermute only.
A program may use at most 320 MiB of HBM per device.

```python
import math
import jax
import jax.numpy as jnp
from jax import lax

C = 512
GROUPS = 32
HMAX = 32
PANELS = 4
OWN_SLOTS = 4
MATS = 22
VECS = 11
STEP = 5
NPAN = 32
OWN_TOTAL = 32


def owner_pick(key):
    key_a, key_b, key_c = jax.random.split(jax.random.fold_in(key, 101), 3)
    groups_total = OWN_TOTAL // OWN_SLOTS
    full_group = jax.random.randint(key_a, (), 0, groups_total)
    shuffled = jax.random.permutation(key_b, OWN_TOTAL).astype(jnp.int32)
    ordering = jnp.argsort((shuffled // OWN_SLOTS != full_group).astype(jnp.int32), stable=True)
    chosen = shuffled[ordering][:MATS]
    return chosen[jax.random.permutation(key_c, MATS)].astype(jnp.int32)


def slot_table(owner_list, table_vals, fallback):
    placing = owner_list[None, :] == jnp.arange(OWN_TOTAL, dtype=jnp.int32)[:, None]
    filled = jnp.any(placing, axis=1)
    picked = jnp.sum(jnp.where(placing, table_vals[None, :], 0.0), axis=1)
    return jnp.where(filled, picked, fallback)


def weight_scales():
    conv_scale = 1.0 / math.sqrt(9 * C)
    attn_scale = 1.0 / math.sqrt(C)
    proj_scale = math.sqrt(16.0 / C)
    return jnp.array([conv_scale] * 18 + [attn_scale] * 3 + [proj_scale], jnp.float32)


def grad_scales():
    base_size = math.sqrt(NPAN * HMAX * HMAX * 0.6)
    return jnp.array([0.5 * base_size] * 18 + [0.25 * base_size] * 3 + [0.1 * base_size], jnp.float32)


def signed_sizes(key, shape_in, sizes):
    key_sign, key_mag = jax.random.split(key)
    signs = jnp.where(jax.random.bernoulli(key_sign, 0.5, shape_in), 1.0, -1.0)
    magnitude = jnp.exp(jax.random.uniform(key_mag, shape_in, jnp.float32, math.log(0.5), math.log(2.0)))
    return signs * magnitude * sizes


def square_sizes(key, shape_in, sizes):
    factor = jnp.exp(jax.random.uniform(key, shape_in, jnp.float32, 0.0, math.log(4.0)))
    return factor * sizes * sizes


def draw_owner_slot(key, part):
    return owner_pick(key)


def draw_master(key, part):
    owner_list = owner_pick(key)
    key = jax.random.fold_in(key, 1)
    scales = slot_table(owner_list, weight_scales(), 1.0 / math.sqrt(C))
    noise = jax.random.normal(key, (OWN_TOTAL, C, C), jnp.float32)
    return noise * scales[:, None, None]


def draw_first_moment(key, part):
    owner_list = owner_pick(key)
    key = jax.random.fold_in(key, 2)
    sizes = slot_table(owner_list, grad_scales(), 0.3 * math.sqrt(NPAN * HMAX * HMAX * 0.6))
    return signed_sizes(key, (OWN_TOTAL, C, C), sizes[:, None, None])


def draw_second_moment(key, part):
    owner_list = owner_pick(key)
    key = jax.random.fold_in(key, 3)
    sizes = slot_table(owner_list, grad_scales(), 0.3 * math.sqrt(NPAN * HMAX * HMAX * 0.6))
    return square_sizes(key, (OWN_TOTAL, C, C), sizes[:, None, None])


def draw_panel_kind(key, part):
    key = jax.random.fold_in(key, 5)
    key_a, key_b = jax.random.split(key)
    kinds_drawn = jax.random.randint(key_a, (NPAN,), 0, 4).astype(jnp.int32)
    forced = jax.random.randint(key_b, (NPAN // PANELS,), 0, PANELS).astype(jnp.int32)
    position = jnp.arange(NPAN, dtype=jnp.int32)
    return jnp.where(position % PANELS == jnp.repeat(forced, PANELS), 0, kinds_drawn).astype(jnp.int32)


def draw_image_in(key, part):
    key = jax.random.fold_in(key, 11)
    row_pos = jnp.arange(HMAX, dtype=jnp.float32) / (HMAX - 1)
    shape_in = (NPAN, HMAX, HMAX, C)
    noise = jax.random.normal(key, shape_in, jnp.float32)
    scale_rows = 0.6 + 1.2 * row_pos
    return (noise * scale_rows[None, :, None, None]).astype(jnp.bfloat16)


def draw_vec_master(key, part):
    key = jax.random.fold_in(key, 7)
    key_a, key_b = jax.random.split(key)
    row_num = jnp.arange(VECS, dtype=jnp.int32)[:, None]
    is_gain = (row_num % 3 == 0) & (row_num < 9)
    base_vals = 0.3 * jax.random.normal(key_a, (VECS, C), jnp.float32)
    gain_vals = jnp.exp(jax.random.uniform(key_b, (VECS, C), jnp.float32, math.log(0.7), math.log(1.4)))
    return jnp.where(is_gain, gain_vals, base_vals)


def draw_vec_first(key, part):
    key = jax.random.fold_in(key, 8)
    return signed_sizes(key, (VECS, C), math.sqrt(NPAN * HMAX * HMAX * 0.6))


def draw_vec_second(key, part):
    key = jax.random.fold_in(key, 9)
    return square_sizes(key, (VECS, C), math.sqrt(NPAN * HMAX * HMAX * 0.6))


def shard_levels(key, shape, shards, smallest, high):
    factor_of = 1.0
    for dim, blocks in shards:
        heights = jax.random.uniform(jax.random.fold_in(jax.random.fold_in(key, 6), dim), (blocks,), jnp.float32, smallest / len(shards), high / len(shards))
        factor_of = factor_of * jnp.repeat(jnp.exp(heights), shape[dim] // blocks).reshape((-1,) + (1,) * (len(shape) - 1 - dim))
    return factor_of


def scatter_about(stream_key, dims, scale, bound, cuts=(), kind=jnp.bfloat16):
    drawn = scale * jax.random.normal(stream_key, dims, jnp.float32)
    if cuts:
        drawn = drawn * shard_levels(stream_key, dims, cuts, -0.22, 0.18)
    return jnp.clip(drawn, -bound, bound).astype(kind)


def setup_inputs(seed: int = 0) -> dict:
    streams_of = jax.random.split(jax.random.key(seed), 11)
    image_in = draw_image_in(jax.random.fold_in(streams_of[10], 71), 0)
    panel_kind = draw_panel_kind(jax.random.fold_in(streams_of[10], 71), 0)
    owner_slot = draw_owner_slot(jax.random.fold_in(streams_of[10], 71), 0)
    out_grad = scatter_about(streams_of[3], (NPAN, HMAX, HMAX, C), 1.0, 6.0, ((0, 8), (1, 4)))
    master = draw_master(jax.random.fold_in(streams_of[10], 71), 0)
    first_moment = draw_first_moment(jax.random.fold_in(streams_of[10], 71), 0)
    second_moment = draw_second_moment(jax.random.fold_in(streams_of[10], 71), 0)
    vec_master = draw_vec_master(jax.random.fold_in(streams_of[10], 71), 0)
    vec_first = draw_vec_first(jax.random.fold_in(streams_of[10], 71), 0)
    vec_second = draw_vec_second(jax.random.fold_in(streams_of[10], 71), 0)
    return dict(image_in=image_in, panel_kind=panel_kind, owner_slot=owner_slot, out_grad=out_grad, master=master, first_moment=first_moment, second_moment=second_moment, vec_master=vec_master, vec_first=vec_first, vec_second=vec_second)


@jax.custom_vjp
def reduced_dtype(v):
    return lax.optimization_barrier(v.astype(jnp.bfloat16)).astype(jnp.float32)

@jax.custom_vjp
def reduced_backward(v):
    return v

def low_keep(v):
    return (reduced_dtype(v), None)

def low_pass(kept, grad):
    return (grad,)

def back_keep(v):
    return (v, None)

def back_low(kept, grad):
    return (reduced_dtype(grad),)
reduced_dtype.defvjp(low_keep, low_pass)
reduced_backward.defvjp(back_keep, back_low)
EXACT_PRECISION = lax.Precision.HIGHEST
NORM_EPS = 1e-06
LEARN_RATE = 0.05
VEC_RATE = 0.2
BETA_ONE = 0.5
BETA_TWO = 0.5
ADAM_EPS = 1e-08
WEIGHT_DECAY = 0.01
MASK_FILL = -1000000000.0

def panel_ids(kind_list, row_index, col_index, panel_side):
    row_grid = row_index.astype(jnp.int32)[None, :, None]
    col_grid = col_index.astype(jnp.int32)[None, None, :]
    kind_grid = kind_list.astype(jnp.int32)[:, None, None]
    half_side = panel_side // 2
    part_side = 3 * panel_side // 4
    inside = (row_grid >= 0) & (row_grid < panel_side) & (col_grid >= 0) & (col_grid < panel_side)
    quarter = 2 * (row_grid >= half_side).astype(jnp.int32) + (col_grid >= half_side).astype(jnp.int32)
    zero_grid = jnp.zeros_like(quarter)
    corner = jnp.where((row_grid < part_side) & (col_grid < part_side), zero_grid, zero_grid - 1)
    labels = jnp.where(kind_grid == 0, zero_grid, jnp.where(kind_grid == 1, corner, jnp.where(kind_grid == 2, quarter, zero_grid - 1)))
    return jnp.where(inside & (labels >= 0), labels, -1).astype(jnp.int32)

def group_norm(value_rows, onehot, counts, gain_row, shift_row):
    panel_count, row_count, col_count, channel_count = value_rows.shape
    grouped = value_rows.reshape(panel_count, row_count, col_count, GROUPS, channel_count // GROUPS)
    first_sums = jnp.einsum('bhwi,bhwgc->big', onehot, grouped, precision=EXACT_PRECISION)
    group_mean = first_sums / counts[:, :, None]
    mean_pix = jnp.einsum('bhwi,big->bhwg', onehot, group_mean, precision=EXACT_PRECISION)
    centred = grouped - mean_pix[..., None]
    spread = jnp.einsum('bhwi,bhwgc->big', onehot, centred * centred, precision=EXACT_PRECISION) / counts[:, :, None]
    scale_pix = jnp.einsum('bhwi,big->bhwg', onehot, lax.rsqrt(spread + NORM_EPS), precision=EXACT_PRECISION)
    normal_val = (centred * scale_pix[..., None]).reshape(value_rows.shape)
    return normal_val * gain_row + shift_row

def conv_apply(hidden, weight_set, tap_masks):
    panel_count, row_count, col_count, channel_count = hidden.shape
    padded = jnp.pad(hidden, ((0, 0), (1, 1), (1, 1), (0, 0)))
    columns = jnp.concatenate([padded[:, tap_index // 3:tap_index // 3 + row_count, tap_index % 3:tap_index % 3 + col_count, :] * tap_masks[tap_index] for tap_index in range(9)], axis=-1)
    result = jnp.dot(columns.reshape(-1, 9 * channel_count), weight_set.reshape(9 * channel_count, channel_count), preferred_element_type=jnp.float32, precision=EXACT_PRECISION)
    return result.reshape(hidden.shape)

def forward(image_vals, matrices, vectors, kind_list):
    panel_count, row_count, col_count, channel_count = image_vals.shape
    labels = panel_ids(kind_list, jnp.arange(row_count), jnp.arange(col_count), row_count)
    outer_labels = panel_ids(kind_list, jnp.arange(-1, row_count + 1), jnp.arange(-1, col_count + 1), row_count)
    onehot = (labels[..., None] == jnp.arange(4, dtype=jnp.int32)).astype(jnp.float32)
    validity = (labels >= 0).astype(jnp.float32)[..., None]
    counts = jnp.maximum(lax.optimization_barrier(jnp.sum(onehot, axis=(1, 2))) * (channel_count // GROUPS), 1.0)
    tap_masks = [((outer_labels[:, tap_index // 3:tap_index // 3 + row_count, tap_index % 3:tap_index % 3 + col_count] == labels) & (labels >= 0)).astype(jnp.float32)[..., None] for tap_index in range(9)]
    hidden_one = reduced_dtype(jax.nn.silu(group_norm(image_vals, onehot, counts, vectors[0], vectors[1])))
    middle = reduced_backward(conv_apply(hidden_one, matrices[0:9], tap_masks) + vectors[2])
    hidden_two = reduced_dtype(jax.nn.silu(group_norm(middle, onehot, counts, vectors[3], vectors[4])))
    residual = image_vals + reduced_backward(conv_apply(hidden_two, matrices[9:18], tap_masks) + vectors[5])
    normed = reduced_dtype(group_norm(residual, onehot, counts, vectors[6], vectors[7])).reshape(-1, channel_count)
    query_matrix = reduced_backward(reduced_dtype(jnp.dot(normed, matrices[18], preferred_element_type=jnp.float32, precision=EXACT_PRECISION) + vectors[8])).reshape(panel_count, -1, channel_count)
    key_rows = reduced_backward(reduced_dtype(jnp.dot(normed, matrices[19], preferred_element_type=jnp.float32, precision=EXACT_PRECISION))).reshape(panel_count, -1, channel_count)
    value_rows = reduced_backward(reduced_dtype(jnp.dot(normed, matrices[20], preferred_element_type=jnp.float32, precision=EXACT_PRECISION) + vectors[9])).reshape(panel_count, -1, channel_count)
    flat_labels = labels.reshape(panel_count, -1)
    same_image = (flat_labels[:, :, None] == flat_labels[:, None, :]) & (flat_labels[:, None, :] >= 0)
    attention_scores = jnp.einsum('szt,swt->szw', query_matrix, key_rows, precision=EXACT_PRECISION) / math.sqrt(channel_count)
    attention_scores = reduced_backward(jnp.where(same_image, attention_scores, MASK_FILL))
    softmax_weights = jax.nn.softmax(attention_scores, axis=-1)
    attended_values = reduced_backward(reduced_dtype(jnp.einsum('itp,ipy->ity', reduced_dtype(softmax_weights), value_rows, precision=EXACT_PRECISION))).reshape(-1, channel_count)
    projected = jnp.dot(attended_values, matrices[21], preferred_element_type=jnp.float32, precision=EXACT_PRECISION) + vectors[10]
    output = residual + projected.reshape(image_vals.shape)
    return output * validity

def adam_update(weight, first_old, second, gradient, step_rate):
    new_first = BETA_ONE * first_old + (1.0 - BETA_ONE) * gradient
    new_second = BETA_TWO * second + (1.0 - BETA_TWO) * gradient * gradient
    first_hat = new_first / (1.0 - BETA_ONE ** STEP)
    second_hat = new_second / (1.0 - BETA_TWO ** STEP)
    new_weight = weight - step_rate * (first_hat / (jnp.sqrt(second_hat) + ADAM_EPS) + WEIGHT_DECAY * weight)
    return (new_first, new_second, new_weight)

def reference(image_in, panel_kind, owner_slot, out_grad, master, first_moment, second_moment, vec_master, vec_first, vec_second):
    placing = (owner_slot[None, :] == jnp.arange(OWN_TOTAL, dtype=jnp.int32)[:, None]).astype(jnp.float32)
    rounded = master.astype(jnp.bfloat16).astype(jnp.float32)
    matrices = jnp.einsum('sm,sij->mij', placing, rounded, precision=EXACT_PRECISION)
    block_size = math.gcd(NPAN, 4)
    block_count = NPAN // block_size
    image_blocks = image_in.reshape(block_count, block_size, HMAX, HMAX, C)
    grad_blocks = out_grad.reshape(block_count, block_size, HMAX, HMAX, C)
    kind_blocks = panel_kind.reshape(block_count, block_size)

    def block_step(carried, block_item):
        grad_mats, grad_vecs = carried
        image_blk, cotan_blk, kind_blk = block_item

        def local_forward(image_vals, mats_in, vecs_in):
            return forward(image_vals, mats_in, vecs_in, kind_blk)
        output, pullback = jax.vjp(local_forward, image_blk.astype(jnp.float32), matrices, vec_master)
        image_grad, mats_grad, vecs_grad = pullback(cotan_blk.astype(jnp.float32))
        return ((grad_mats + mats_grad, grad_vecs + vecs_grad), (output.astype(jnp.bfloat16), image_grad.astype(jnp.bfloat16)))
    initial = (jnp.zeros(matrices.shape, jnp.float32), jnp.zeros(vec_master.shape, jnp.float32))
    (grad_mats, grad_vecs), (outputs, image_grads) = lax.scan(block_step, initial, (image_blocks, grad_blocks, kind_blocks))
    slot_grads = jnp.einsum('sm,mij->sij', placing, grad_mats, precision=EXACT_PRECISION)
    new_first, new_second, new_master = adam_update(master, first_moment, second_moment, slot_grads, LEARN_RATE)
    vec_first_new, vec_second_new, vec_master_new = adam_update(vec_master, vec_first, vec_second, grad_vecs, VEC_RATE)
    return (outputs.reshape(image_in.shape), image_grads.reshape(image_in.shape), new_first, new_second, new_master, vec_first_new, vec_second_new, vec_master_new)
```

```python
import functools
import math

import jax
import jax.numpy as jnp
from jax import lax
from jax.experimental import pallas as pl
from jax.experimental.pallas import tpu as pltpu
from jax.sharding import PartitionSpec as P

GROUPS = 32
STEP = 5


EXACT_PRECISION = lax.Precision.HIGHEST
NORM_EPS = 1e-06
LEARN_RATE = 0.05
VEC_RATE = 0.2
BETA_ONE = 0.5
BETA_TWO = 0.5
ADAM_EPS = 1e-08
WEIGHT_DECAY = 0.01
MASK_FILL = -1000000000.0


def extended(cells, sides, width):
    for axis, dim in sides:
        count = lax.axis_size(axis)
        ends = count - 1
        head = lax.slice_in_dim(cells, 0, width, axis=dim)
        tail = lax.slice_in_dim(cells, cells.shape[dim] - width, cells.shape[dim], axis=dim)
        cells = jnp.concatenate(
            [
                lax.ppermute(tail, axis, [(i, (i + 1) % count) for i in range(ends)]),
                cells,
                lax.ppermute(head, axis, [((i + 1) % count, i) for i in range(ends)]),
            ],
            axis=dim,
        )
    return cells


def panel_ids(kind_list, row_index, col_index, panel_side):
    row_grid = row_index[None, :, None]
    col_grid = col_index[None, None, :]
    kind_grid = kind_list[:, None, None]
    half_side = panel_side // 2
    part_side = 3 * panel_side // 4
    inside = (row_grid >= 0) & (row_grid < panel_side) & (col_grid >= 0) & (col_grid < panel_side)
    quarter = 2 * (row_grid >= half_side).astype(jnp.int32) + (col_grid >= half_side).astype(
        jnp.int32
    )
    zero_grid = jnp.zeros_like(quarter)
    corner = jnp.where((row_grid < part_side) & (col_grid < part_side), zero_grid, zero_grid - 1)
    labels = jnp.where(
        kind_grid == 0,
        zero_grid,
        jnp.where(kind_grid == 1, corner, jnp.where(kind_grid == 2, quarter, zero_grid - 1)),
    )
    return jnp.where(inside & (labels >= 0), labels, -1)


def spread_pix(onehot, per_group):
    return jnp.einsum("prwi,pig->prwg", onehot, per_group, precision=EXACT_PRECISION)


def group_stats(value_rows, onehot, counts):
    panel_count, row_count, col_count, channel_count = value_rows.shape
    grouped = value_rows.reshape(panel_count, row_count, col_count, GROUPS, channel_count // GROUPS)
    first_sums = lax.psum(
        jnp.einsum("prwi,prwgc->pig", onehot, grouped, precision=EXACT_PRECISION), "rows"
    )
    group_mean = first_sums / counts[:, :, None]
    centred = grouped - spread_pix(onehot, group_mean)[..., None]
    square_sums = jnp.einsum(
        "prwi,prwgc->pig", onehot, centred * centred, precision=EXACT_PRECISION
    )
    spread = lax.psum(square_sums, "rows") / counts[:, :, None]
    scale_pix = spread_pix(onehot, lax.rsqrt(spread + NORM_EPS))
    normal_val = (centred * scale_pix[..., None]).reshape(value_rows.shape)
    return (normal_val, scale_pix)


def group_back(gradient, normal_val, scale_pix, gain_row, onehot, counts):
    panel_count, row_count, col_count, channel_count = gradient.shape
    grad_gain = jnp.sum(gradient * normal_val, axis=(0, 1, 2))
    grad_shift = jnp.sum(gradient, axis=(0, 1, 2))
    scaled = (gradient * gain_row).reshape(
        panel_count, row_count, col_count, GROUPS, channel_count // GROUPS
    )
    normal_grp = normal_val.reshape(scaled.shape)
    plain_sums = jnp.einsum("prwi,prwgc->pig", onehot, scaled, precision=EXACT_PRECISION)
    cross_sums = jnp.einsum(
        "prwi,prwgc->pig", onehot, scaled * normal_grp, precision=EXACT_PRECISION
    )
    plain_sums, cross_sums = lax.psum((plain_sums, cross_sums), "rows")
    plain_pix = spread_pix(onehot, plain_sums / counts[:, :, None])
    cross_pix = spread_pix(onehot, cross_sums / counts[:, :, None])
    result = scale_pix[..., None] * (
        scaled - plain_pix[..., None] - normal_grp * cross_pix[..., None]
    )
    return (result.reshape(gradient.shape), grad_gain, grad_shift)


def silu_slope(pre_act):
    sigmoid_val = jax.nn.sigmoid(pre_act)
    return sigmoid_val * (1.0 + pre_act * (1.0 - sigmoid_val))


def conv_forward(hidden, weight_cat, tap_masks):
    panel_count, row_count, col_count, channel_count = hidden.shape
    padded = extended(hidden, (("rows", 1),), 1)
    padded = jnp.pad(padded, ((0, 0), (0, 0), (1, 1), (0, 0)))
    columns = jnp.concatenate(
        [
            padded[
                :,
                tap_index // 3 : tap_index // 3 + row_count,
                tap_index % 3 : tap_index % 3 + col_count,
                :,
            ]
            * tap_masks[tap_index]
            for tap_index in range(9)
        ],
        axis=-1,
    )
    columns = columns.reshape(-1, 9 * channel_count)
    result = jnp.dot(columns, weight_cat, preferred_element_type=jnp.float32)
    return (result.reshape(hidden.shape), columns)


def conv_backward(gradient, columns, weight_cat, tap_masks):
    panel_count, row_count, col_count, channel_count = gradient.shape
    grad_flat = gradient.reshape(-1, channel_count)
    weight_grad = jnp.einsum("mk,mc->kc", columns, grad_flat, preferred_element_type=jnp.float32)
    col_grads = jnp.einsum("mc,kc->mk", grad_flat, weight_cat, preferred_element_type=jnp.float32)
    col_grads = col_grads.reshape(panel_count, row_count, col_count, 9, channel_count)
    padded_grad = jnp.zeros((panel_count, row_count + 2, col_count + 2, channel_count), jnp.float32)
    for tap_index in range(9):
        tap_row = tap_index // 3
        tap_col = tap_index % 3
        padded_grad = padded_grad.at[
            :, tap_row : tap_row + row_count, tap_col : tap_col + col_count, :
        ].add(col_grads[:, :, :, tap_index, :] * tap_masks[tap_index])
    padded_grad = padded_grad[:, :, 1 : col_count + 1, :]
    edge_rows = jnp.concatenate(
        [padded_grad[:, 0:1], padded_grad[:, row_count + 1 : row_count + 2]], axis=1
    )
    arrived = extended(edge_rows.astype(jnp.bfloat16), (("rows", 1),), 1).astype(edge_rows.dtype)
    inner = padded_grad[:, 1 : row_count + 1]
    inner = inner.at[:, 0].add(arrived[:, 0])
    inner = inner.at[:, row_count - 1].add(arrived[:, 3])
    return (inner, weight_grad)


def adam_update(weight, first_old, second, gradient, step_rate):
    new_first = BETA_ONE * first_old + (1.0 - BETA_ONE) * gradient
    new_second = BETA_TWO * second + (1.0 - BETA_TWO) * gradient * gradient
    first_hat = new_first / (1.0 - BETA_ONE**STEP)
    second_hat = new_second / (1.0 - BETA_TWO**STEP)
    new_weight = weight - step_rate * (
        first_hat / (jnp.sqrt(second_hat) + ADAM_EPS) + WEIGHT_DECAY * weight
    )
    return (new_first, new_second, new_weight)


def on_device(
    image_in,
    panel_kind,
    owner_slot,
    out_grad,
    master,
    first_moment,
    second_moment,
    vec_master,
    vec_first,
    vec_second,
):
    panel_count, row_count, col_count, channel_count = image_in.shape
    height_all = row_count * lax.axis_size("rows")
    group_width = channel_count // GROUPS
    pixel_count = panel_count * row_count * col_count
    local_pix = row_count * col_count
    slot_total = master.shape[0] * lax.axis_size("imgs")
    inv_root = 1.0 / math.sqrt(channel_count)
    placing = owner_slot[None, :] == jnp.arange(slot_total, dtype=jnp.int32)[:, None]
    slot_weights = lax.all_gather(master.astype(jnp.bfloat16), "imgs", axis=0, tiled=True)
    picked = jnp.einsum(
        "sm,sij->mij",
        placing.astype(jnp.bfloat16),
        slot_weights,
        preferred_element_type=jnp.float32,
    ).astype(jnp.bfloat16)
    weights = lax.all_gather(picked, "rows", axis=1, tiled=True)
    conv_first = weights[0:9].reshape(9 * channel_count, channel_count)
    conv_second = weights[9:18].reshape(9 * channel_count, channel_count)
    attn_in = jnp.concatenate([weights[18], weights[19], weights[20]], axis=1)
    attn_out = weights[21]
    first_row = lax.axis_index("rows") * row_count
    col_range = jnp.arange(col_count, dtype=jnp.int32)
    labels = panel_ids(
        panel_kind, first_row + jnp.arange(row_count, dtype=jnp.int32), col_range, height_all
    )
    outer_labels = panel_ids(
        panel_kind,
        first_row + jnp.arange(-1, row_count + 1, dtype=jnp.int32),
        jnp.arange(-1, col_count + 1, dtype=jnp.int32),
        height_all,
    )
    whole_labels = panel_ids(
        panel_kind, jnp.arange(height_all, dtype=jnp.int32), col_range, height_all
    )
    label_range = jnp.arange(4, dtype=jnp.int32)
    onehot = (labels[..., None] == label_range).astype(jnp.float32)
    validity = (labels >= 0).astype(jnp.float32)[..., None]
    counts = jnp.maximum(
        jnp.sum((whole_labels[..., None] == label_range).astype(jnp.float32), axis=(1, 2))
        * group_width,
        1.0,
    )
    tap_masks = [
        (
            (
                outer_labels[
                    :,
                    tap_index // 3 : tap_index // 3 + row_count,
                    tap_index % 3 : tap_index % 3 + col_count,
                ]
                == labels
            )
            & (labels >= 0)
        ).astype(jnp.bfloat16)[..., None]
        for tap_index in range(9)
    ]
    image_vals = image_in.astype(jnp.float32)
    normal_one, scale_one = group_stats(image_vals, onehot, counts)
    pre_one = normal_one * vec_master[0] + vec_master[1]
    hidden_one = jax.nn.silu(pre_one).astype(jnp.bfloat16)
    conv_out, columns_one = conv_forward(hidden_one, conv_first, tap_masks)
    middle = conv_out + vec_master[2]
    normal_two, scale_two = group_stats(middle, onehot, counts)
    pre_two = normal_two * vec_master[3] + vec_master[4]
    hidden_two = jax.nn.silu(pre_two).astype(jnp.bfloat16)
    conv_out_two, columns_two = conv_forward(hidden_two, conv_second, tap_masks)
    residual = image_vals + conv_out_two + vec_master[5]
    normal_three, scale_three = group_stats(residual, onehot, counts)
    normed = (
        (normal_three * vec_master[6] + vec_master[7])
        .astype(jnp.bfloat16)
        .reshape(pixel_count, channel_count)
    )
    qkv_vals = jnp.dot(normed, attn_in, preferred_element_type=jnp.float32)
    query_matrix = (
        (qkv_vals[:, :channel_count] + vec_master[8])
        .astype(jnp.bfloat16)
        .reshape(panel_count, local_pix, channel_count)
    )
    key_loc = (
        qkv_vals[:, channel_count : 2 * channel_count]
        .astype(jnp.bfloat16)
        .reshape(panel_count, row_count, col_count, channel_count)
    )
    values_loc = (
        (qkv_vals[:, 2 * channel_count :] + vec_master[9])
        .astype(jnp.bfloat16)
        .reshape(panel_count, row_count, col_count, channel_count)
    )
    keys_all, values_all = (
        lax.all_gather(key_loc, "rows", axis=1, tiled=True),
        lax.all_gather(values_loc, "rows", axis=1, tiled=True),
    )
    keys_all = keys_all.reshape(panel_count, height_all * col_count, channel_count)
    values_all = values_all.reshape(panel_count, height_all * col_count, channel_count)
    query_labels = labels.reshape(panel_count, -1)
    key_labels = whole_labels.reshape(panel_count, -1)
    same_image = (query_labels[:, :, None] == key_labels[:, None, :]) & (
        key_labels[:, None, :] >= 0
    )
    attention_scores = (
        jnp.einsum("pqc,pkc->pqk", query_matrix, keys_all, preferred_element_type=jnp.float32)
        * inv_root
    )
    attention_scores = jnp.where(same_image, attention_scores, MASK_FILL)
    row_max = jnp.max(attention_scores, axis=-1, keepdims=True)
    exp_scores = jnp.exp(attention_scores - row_max)
    exp_total = jnp.sum(exp_scores, axis=-1, keepdims=True)
    softmax_weights = exp_scores / exp_total
    log_total = row_max[..., 0] + jnp.log(exp_total[..., 0])
    attended_values = jnp.einsum(
        "pqk,pkc->pqc",
        softmax_weights.astype(jnp.bfloat16),
        values_all,
        preferred_element_type=jnp.float32,
    ).astype(jnp.bfloat16)
    attended_values = attended_values.reshape(pixel_count, channel_count)
    projected = (
        jnp.dot(attended_values, attn_out, preferred_element_type=jnp.float32) + vec_master[10]
    ).reshape(image_in.shape)
    block_out = ((residual + projected) * validity).astype(jnp.bfloat16)
    grad_out = out_grad.astype(jnp.float32) * validity
    grad_flat = grad_out.astype(jnp.bfloat16).reshape(pixel_count, channel_count)
    grad_proj = jnp.einsum(
        "mc,md->cd", attended_values, grad_flat, preferred_element_type=jnp.float32
    )
    bias_proj = jnp.sum(grad_out, axis=(0, 1, 2))
    d_attended = jnp.einsum(
        "md,cd->mc", grad_flat, attn_out, preferred_element_type=jnp.float32
    ).astype(jnp.bfloat16)
    d_attended = d_attended.reshape(panel_count, local_pix, channel_count)
    again_scores = (
        jnp.einsum("pqc,pkc->pqk", query_matrix, keys_all, preferred_element_type=jnp.float32)
        * inv_root
    )
    again_scores = jnp.where(same_image, again_scores, MASK_FILL)
    again_soft = jnp.exp(again_scores - log_total[..., None])
    d_soft = jnp.einsum("pqc,pkc->pqk", d_attended, values_all, preferred_element_type=jnp.float32)
    row_delta = jnp.sum(d_soft * again_soft, axis=-1)
    d_scores = (again_soft * (d_soft - row_delta[..., None])).astype(jnp.bfloat16)
    d_queries = (
        jnp.einsum("pqk,pkc->pqc", d_scores, keys_all, preferred_element_type=jnp.float32)
        * inv_root
    ).astype(jnp.bfloat16)
    d_key_all = (
        jnp.einsum("pqk,pqc->pkc", d_scores, query_matrix, preferred_element_type=jnp.float32)
        * inv_root
    )
    d_value_all = jnp.einsum(
        "pqk,pqc->pkc",
        again_soft.astype(jnp.bfloat16),
        d_attended,
        preferred_element_type=jnp.float32,
    )
    d_key_all = d_key_all.reshape(panel_count, height_all, col_count, channel_count)
    d_value_all = d_value_all.reshape(panel_count, height_all, col_count, channel_count)
    d_keys, d_values = (
        lax.psum_scatter(
            d_key_all.astype(jnp.bfloat16), "rows", scatter_dimension=1, tiled=True
        ).astype(jnp.float32),
        lax.psum_scatter(
            d_value_all.astype(jnp.bfloat16), "rows", scatter_dimension=1, tiled=True
        ).astype(jnp.float32),
    )
    d_keys = d_keys.reshape(pixel_count, channel_count).astype(jnp.bfloat16)
    d_values = d_values.reshape(pixel_count, channel_count).astype(jnp.bfloat16)
    d_queries = d_queries.reshape(pixel_count, channel_count)
    d_qkv = jnp.concatenate([d_queries, d_keys, d_values], axis=1)
    grad_qkv = jnp.einsum("mc,md->cd", normed, d_qkv, preferred_element_type=jnp.float32)
    bias_query = jnp.sum(d_queries, axis=0, dtype=jnp.float32)
    bias_value = jnp.sum(d_values, axis=0, dtype=jnp.float32)
    d_normed = jnp.einsum("md,cd->mc", d_qkv, attn_in, preferred_element_type=jnp.float32).reshape(
        image_in.shape
    )
    d_three, gain_three, shift_three = group_back(
        d_normed, normal_three, scale_three, vec_master[6], onehot, counts
    )
    d_residual = grad_out + d_three
    d_middle_two = d_residual.astype(jnp.bfloat16)
    bias_two = jnp.sum(d_middle_two, axis=(0, 1, 2), dtype=jnp.float32)
    d_hidden_two, grad_conv_two = conv_backward(d_middle_two, columns_two, conv_second, tap_masks)
    d_middle, gain_two, shift_two = group_back(
        d_hidden_two * silu_slope(pre_two), normal_two, scale_two, vec_master[3], onehot, counts
    )
    d_middle_one = d_middle.astype(jnp.bfloat16)
    bias_one = jnp.sum(d_middle_one, axis=(0, 1, 2), dtype=jnp.float32)
    d_hidden_one, grad_conv_one = conv_backward(d_middle_one, columns_one, conv_first, tap_masks)
    d_input, gain_one, shift_one = group_back(
        d_hidden_one * silu_slope(pre_one), normal_one, scale_one, vec_master[0], onehot, counts
    )
    input_grad = (d_residual + d_input).astype(jnp.bfloat16)
    vec_grads = jnp.stack(
        [
            gain_one,
            shift_one,
            bias_one,
            gain_two,
            shift_two,
            bias_two,
            gain_three,
            shift_three,
            bias_query,
            bias_value,
            bias_proj,
        ]
    )
    vec_grads = lax.psum(vec_grads, ("imgs", "rows"))
    mat_grads = jnp.concatenate(
        [
            grad_conv_one.reshape(9, channel_count, channel_count),
            grad_conv_two.reshape(9, channel_count, channel_count),
            grad_qkv[:, :channel_count][None],
            grad_qkv[:, channel_count : 2 * channel_count][None],
            grad_qkv[:, 2 * channel_count :][None],
            grad_proj[None],
        ],
        axis=0,
    )
    row_grads = lax.psum_scatter(
        mat_grads.astype(jnp.bfloat16), "rows", scatter_dimension=1, tiled=True
    ).astype(jnp.float32)
    slot_terms = jnp.einsum(
        "sm,mij->sij", placing.astype(jnp.float32), row_grads, precision=EXACT_PRECISION
    )
    owned_grads = lax.psum_scatter(
        slot_terms.astype(jnp.bfloat16), "imgs", scatter_dimension=0, tiled=True
    ).astype(jnp.float32)
    new_first, new_second, new_master = adam_update(
        master, first_moment, second_moment, owned_grads, LEARN_RATE
    )
    vec_first_new, vec_second_new, vec_master_new = adam_update(
        vec_master, vec_first, vec_second, vec_grads, VEC_RATE
    )
    return (
        block_out,
        input_grad,
        new_first,
        new_second,
        new_master,
        vec_first_new,
        vec_second_new,
        vec_master_new,
    )


F32 = jnp.float32
B16 = jnp.bfloat16
AXES = ("imgs", "rows")
NN = (((1,), (0,)), ((), ()))
NT = (((1,), (1,)), ((), ()))
TN = (((0,), (0,)), ((), ()))
VSPEC = pl.BlockSpec(memory_space=pltpu.VMEM)
SSPEC = pl.BlockSpec(memory_space=pltpu.SMEM)
ASPEC = pl.BlockSpec(memory_space=pl.ANY)
VMEM_BYTES = 52 * 2**20
STAT = 16
M_KIND, M_CORE, M_ROW, M_Z, M_OFF, M_KEEP, M_SEND = 0, 1, 2, 3, 4, 12, 16


def dot(left, right, dims):
    return lax.dot_general(left, right, dims, preferred_element_type=F32)


def shaped(shape, dtype):
    return jax.ShapeDtypeStruct(shape, dtype)


def call(body, outs, in_specs, out_specs, scratch, args, flops=0, moved=0, grid=None):
    extra = {} if grid is None else {"grid": grid}
    return pl.pallas_call(
        body,
        out_shape=outs,
        in_specs=in_specs,
        out_specs=out_specs,
        scratch_shapes=scratch,
        compiler_params=pltpu.CompilerParams(vmem_limit_bytes=VMEM_BYTES),
        cost_estimate=pl.CostEstimate(flops=flops, bytes_accessed=moved, transcendentals=0),
        **extra,
    )(*args)


class Panel:
    def __init__(self, kind, side, channels):
        self.kind, self.side, self.channels = kind, side, channels
        self.half = side // 2
        self.width = channels // GROUPS
        part = 3 * side // 4
        self.limit = jnp.where(kind == 3, 0, jnp.where(kind == 1, part, side))
        pixels = jnp.where(
            kind == 2, self.half * self.half, jnp.where(kind == 1, part * part, side * side)
        )
        count = jnp.where(kind == 3, 1, pixels * self.width)
        self.inverse = 1.0 / count.astype(F32)
        self.four = jnp.where(kind == 2, 1.0, 0.0).astype(F32)
        self.cut = jnp.where(kind == 2, self.half, -1)

    def columns(self):
        return lax.broadcasted_iota(jnp.int32, (self.side, self.channels), 0)

    def mask(self, columns, i):
        return columns < jnp.where(i < self.limit, self.limit, 0)

    def rows(self, i):
        return pl.ds(pl.multiple_of(i * self.side, self.side), self.side)

    def same_group(self):
        shift = self.width.bit_length() - 1
        shape = (self.channels, self.channels)
        left = lax.broadcasted_iota(jnp.int32, shape, 0) >> shift
        right = lax.broadcasted_iota(jnp.int32, shape, 1) >> shift
        return jnp.where(left == right, 1.0, 0.0).astype(B16)

    def loop(self, body, init):
        found = []
        for top in range(2):
            found.append(
                lax.fori_loop(
                    0,
                    self.half,
                    lambda t, carry, top=top: body(top * self.half + t, top, carry),
                    init,
                    unroll=2,
                )
            )
        return found

    def spread(self, stat, top):
        shape = (self.half, self.channels)
        return jnp.concatenate(
            [
                jnp.broadcast_to(stat[2 * top : 2 * top + 1], shape),
                jnp.broadcast_to(stat[2 * top + 1 : 2 * top + 2], shape),
            ],
            axis=0,
        )

    def quadrants(self, upper, lower):
        parts = []
        for acc in (upper, lower):
            for left in range(2):
                parts.append(
                    jnp.sum(acc[left * self.half : (left + 1) * self.half], axis=0, keepdims=True)
                )
        parts.append(jnp.zeros((STAT - 4, self.channels), F32))
        return jnp.concatenate(parts, axis=0)

    def over_images(self, sums):
        total = jnp.sum(sums, axis=0, keepdims=True)
        return sums * self.four + total * (1.0 - self.four)

    def over_groups(self, sums, same):
        high = sums.astype(B16)
        rest = sums - high.astype(F32)
        middle = rest.astype(B16)
        low = (rest - middle.astype(F32)).astype(B16)
        return (dot(high, same, NN) + dot(middle, same, NN)) + dot(low, same, NN)

    def reduced(self, sums, same):
        return self.over_groups(self.over_images(sums), same) * self.inverse

    def zero(self):
        return jnp.zeros((self.side, self.channels), F32)


def norm_stats(panel, load, same):
    columns = panel.columns()

    def add_plain(i, top, carry):
        return carry + jnp.where(panel.mask(columns, i), load(i), 0.0)

    mean = panel.reduced(panel.quadrants(*panel.loop(add_plain, panel.zero())), same)
    means = [panel.spread(mean, top) for top in range(2)]

    def add_square(i, top, carry):
        centred = load(i) - means[top]
        return carry + jnp.where(panel.mask(columns, i), centred * centred, 0.0)

    spread = panel.reduced(panel.quadrants(*panel.loop(add_square, panel.zero())), same)
    return mean, lax.rsqrt(spread + NORM_EPS)


def store_shifted(panel, hb, i, top, row, columns):
    side = panel.side
    place = pl.ds(pl.multiple_of((i - top * panel.half + 1) * side, side), side)
    before = pltpu.roll(row, 1, 0)
    after = pltpu.roll(row, side - 1, 0)
    from_left = (columns != 0) & (columns != panel.cut)
    from_right = (columns != side - 1) & (columns != panel.cut - 1)
    hb[0, top, place, :] = jnp.where(from_left, before, 0.0).astype(B16)
    hb[1, top, place, :] = row.astype(B16)
    hb[2, top, place, :] = jnp.where(from_right, after, 0.0).astype(B16)


def store_edges(panel, hb):
    side, half = panel.side, panel.half
    joined = 1.0 - panel.four
    blank = jnp.zeros((side, panel.channels), B16)
    for b in range(3):
        hb[b, 0, 0:side, :] = blank
        hb[b, 1, (half + 1) * side : (half + 2) * side, :] = blank
        upper = hb[b, 0, half * side : (half + 1) * side, :].astype(F32) * joined
        lower = hb[b, 1, side : 2 * side, :].astype(F32) * joined
        hb[b, 1, 0:side, :] = upper.astype(B16)
        hb[b, 0, (half + 1) * side : (half + 2) * side, :] = lower.astype(B16)


def silu_row(panel, load, columns, mean, rstd, gain, shift, i):
    mask = panel.mask(columns, i)
    normal = jnp.where(mask, (load(i) - mean) * rstd, 0.0)
    pre = normal * gain + shift
    return jnp.where(mask, pre / (1.0 + jnp.exp(-pre)), 0.0)


def silu_shifted(panel, load, mean, rstd, gain, shift, hb):
    columns = panel.columns()
    means = [panel.spread(mean, top) for top in range(2)]
    rstds = [panel.spread(rstd, top) for top in range(2)]

    def step(i, top, carry):
        row = silu_row(panel, load, columns, means[top], rstds[top], gain, shift, i)
        store_shifted(panel, hb, i, top, row, columns)
        return carry

    panel.loop(step, 0)
    store_edges(panel, hb)


def weight_copies(meta, pieces, held, sems, m):
    block = pieces[0].shape[1]
    return [
        pltpu.make_async_copy(
            piece.at[m],
            held.at[m, pl.ds(pl.multiple_of(meta[M_OFF + t], block), block), :],
            sems.at[m, t],
        )
        for t, piece in enumerate(pieces)
    ]


def start_weights(meta, pieces, held, sems):
    for m in range(held.shape[0]):
        for copy in weight_copies(meta, pieces, held, sems, m):
            copy.start()


def wait_weights(meta, pieces, held, sems):
    for m in range(held.shape[0]):
        for copy in weight_copies(meta, pieces, held, sems, m):
            copy.wait()


def conv_taps(panel, hb, held, top, dims, flip):
    side, pixels = panel.side, panel.half * panel.side
    total = jnp.zeros((pixels, panel.channels), F32)
    for a in range(3):
        for b in range(3):
            row, col = (2 - a, 2 - b) if flip else (a, b)
            total = total + dot(
                hb[col, top, row * side : row * side + pixels, :], held[3 * a + b], dims
            )
    return total


def cast_kernel(meta, master, mine, send):
    block = mine.shape[1]
    core = meta[M_CORE]
    mine[...] = master[:, pl.ds(pl.multiple_of(core * block, block), block), :].astype(B16)
    send[...] = master[:, pl.ds(pl.multiple_of((1 - core) * block, block), block), :].astype(B16)


def pick_kernel(sizes, count, *refs):
    table = refs[0]
    sources = refs[1 : 1 + count]
    outs = refs[1 + count : 1 + count + len(sizes)]
    sems = refs[-1]
    places = [(g, k) for g, size in enumerate(sizes) for k in range(size)]
    for m, (g, k) in enumerate(places):
        for t in range(count):

            @pl.when(table[0, m] == t)
            def _(m=m, g=g, k=k, t=t):
                pltpu.make_async_copy(
                    sources[t].at[table[1, m]], outs[g].at[k], sems.at[m]
                ).start()

    for m, (g, k) in enumerate(places):
        pltpu.make_async_copy(sources[0].at[0], outs[g].at[k], sems.at[m]).wait()


def first_kernel(side, meta, image, vec, hb, stats):
    panel = Panel(meta[M_KIND], side, image.shape[1])

    def load(i):
        return image[panel.rows(i), :].astype(F32)

    mean, rstd = norm_stats(panel, load, panel.same_group())
    stats[0:STAT, :] = mean
    stats[STAT:, :] = rstd
    silu_shifted(panel, load, mean, rstd, vec[0:1, :], vec[1:2, :], hb)


def middle_kernel(side, meta, hb, vec, *refs):
    pieces, (middle, stats, hb_two, held, sems) = refs[:8], refs[8:]
    panel = Panel(meta[M_KIND], side, middle.shape[1])
    start_weights(meta, pieces, held, sems)
    same = panel.same_group()
    wait_weights(meta, pieces, held, sems)
    pixels = panel.half * side
    for top in range(2):
        middle[top * pixels : (top + 1) * pixels, :] = (
            conv_taps(panel, hb, held, top, NN, False) + vec[2:3, :]
        )

    def load(i):
        return middle[panel.rows(i), :]

    mean, rstd = norm_stats(panel, load, same)
    stats[0:STAT, :] = mean
    stats[STAT:, :] = rstd
    silu_shifted(panel, load, mean, rstd, vec[3:4, :], vec[4:5, :], hb_two)


def residual_kernel(side, meta, hb, image, vec, *refs):
    pieces, (residual, stats, normed, held, sems) = refs[:8], refs[8:]
    panel = Panel(meta[M_KIND], side, residual.shape[1])
    start_weights(meta, pieces, held, sems)
    same = panel.same_group()
    wait_weights(meta, pieces, held, sems)
    pixels = panel.half * side
    for top in range(2):
        span = slice(top * pixels, (top + 1) * pixels)
        residual[span, :] = (
            image[span, :].astype(F32) + conv_taps(panel, hb, held, top, NN, False) + vec[5:6, :]
        )

    def load(i):
        return residual[panel.rows(i), :]

    mean, rstd = norm_stats(panel, load, same)
    stats[0:STAT, :] = mean
    stats[STAT:, :] = rstd
    columns = panel.columns()
    means = [panel.spread(mean, top) for top in range(2)]
    rstds = [panel.spread(rstd, top) for top in range(2)]

    def step(i, top, carry):
        normal = jnp.where(panel.mask(columns, i), (load(i) - means[top]) * rstds[top], 0.0)
        normed[panel.rows(i), :] = (normal * vec[6:7, :] + vec[7:8, :]).astype(B16)
        return carry

    panel.loop(step, 0)


def norm_back(panel, load, stats, gain, same, gradient, emit, extra):
    columns = panel.columns()
    means = [panel.spread(stats[0:STAT], top) for top in range(2)]
    rstds = [panel.spread(stats[STAT:], top) for top in range(2)]

    def normal_of(i, top, mask):
        return jnp.where(mask, (load(i) - means[top]) * rstds[top], 0.0)

    def add(i, top, carry):
        mask = panel.mask(columns, i)
        normal = normal_of(i, top, mask)
        grad = gradient(i, mask, normal)
        return carry[0] + grad, carry[1] + grad * normal

    upper, lower = panel.loop(add, (panel.zero(), panel.zero()))
    plain = panel.quadrants(upper[0], lower[0])
    cross = panel.quadrants(upper[1], lower[1])
    plain_mean = panel.reduced(plain * gain, same)
    cross_mean = panel.reduced(cross * gain, same)
    plains = [panel.spread(plain_mean, top) for top in range(2)]
    crosses = [panel.spread(cross_mean, top) for top in range(2)]

    def finish(i, top, carry):
        mask = panel.mask(columns, i)
        normal = normal_of(i, top, mask)
        scaled = gradient(i, mask, None) * gain
        value = rstds[top] * (scaled - plains[top] - normal * crosses[top])
        return emit(i, top, jnp.where(mask, value, 0.0), carry, columns)

    found = panel.loop(finish, extra)
    grad_gain = jnp.sum(cross, axis=0, keepdims=True)
    grad_shift = jnp.sum(plain, axis=0, keepdims=True)
    return grad_gain, grad_shift, found


def attention_kernel(side, meta, residual, stats, normed, out_grad, vec, *refs):
    pieces = refs[:8]
    (block_out, d_residual, d_middle, eb, keep, send, rows_out) = refs[8:15]
    (held, sems, queries, keys, values, soft, soft_low, d_scores, attended, d_attended,
     d_queries, d_keys, d_values, gout, d_normed, staged) = refs[15:]
    channels = residual.shape[1]
    panel = Panel(meta[M_KIND], side, channels)
    start_weights(meta, pieces, held, sems)
    same = panel.same_group()
    total = side * side
    block = total // 4
    inv_root = 1.0 / math.sqrt(channels)
    shift = side.bit_length() - 1

    def labels(pixel):
        i, j = pixel >> shift, pixel & (side - 1)
        quarter = jnp.where(i >= panel.half, 2, 0) + jnp.where(j >= panel.half, 1, 0)
        four = jnp.where(panel.kind == 2, 1, 0)
        lab = quarter * four
        return jnp.where((i < panel.limit) & (j < panel.limit), lab, -1)

    key_labels = labels(lax.broadcasted_iota(jnp.int32, (1, total), 1))

    def block_labels(n):
        return labels(lax.broadcasted_iota(jnp.int32, (block, 1), 0) + n * block)

    wait_weights(meta, pieces, held, sems)
    for n in range(4):
        span = slice(n * block, (n + 1) * block)
        rows = normed[span, :]
        queries[span, :] = (dot(rows, held[0], NN) + vec[8:9, :]).astype(B16)
        keys[span, :] = dot(rows, held[1], NN).astype(B16)
        values[span, :] = (dot(rows, held[2], NN) + vec[9:10, :]).astype(B16)
    gout_sum = jnp.zeros((1, channels), F32)
    for n in range(4):
        span = slice(n * block, (n + 1) * block)
        lab = block_labels(n)
        scores = dot(queries[span, :], keys[...], NT) * inv_root
        scores = jnp.where((lab == key_labels) & (key_labels >= 0), scores, MASK_FILL)
        top = jnp.max(scores, axis=-1, keepdims=True)
        grown = jnp.exp(scores - top)
        weights = grown / jnp.sum(grown, axis=-1, keepdims=True)
        soft[span, :] = weights
        soft_low[span, :] = weights.astype(B16)
        attended[span, :] = dot(soft_low[span, :], values[...], NN).astype(B16)
        projected = dot(attended[span, :], held[3], NN) + vec[10:11, :]
        valid = lab >= 0
        block_out[span, :] = jnp.where(valid, residual[span, :] + projected, 0.0).astype(B16)
        grad = jnp.where(valid, out_grad[span, :].astype(F32), 0.0)
        gout_sum = gout_sum + jnp.sum(grad, axis=0, keepdims=True)
        gout[span, :] = grad.astype(B16)
        d_attended[span, :] = dot(gout[span, :], held[3], NT).astype(B16)
    for n in range(4):
        span = slice(n * block, (n + 1) * block)
        d_soft = dot(d_attended[span, :], values[...], NT)
        weights = soft[span, :]
        delta = jnp.sum(d_soft * weights, axis=-1, keepdims=True)
        d_scores[span, :] = (weights * (d_soft - delta)).astype(B16)
        d_queries[span, :] = (dot(d_scores[span, :], keys[...], NN) * inv_root).astype(B16)
    d_keys[...] = (dot(d_scores[...], queries[...], TN) * inv_root).astype(B16)
    d_values[...] = dot(soft_low[...], d_attended[...], TN).astype(B16)
    pairs = ((normed, d_queries), (normed, d_keys), (normed, d_values), (attended, gout))
    for m, (left, right) in enumerate(pairs):
        staged[...] = dot(left[...], right[...], TN)
        store_parts(meta, staged, keep, send, m)
    for n in range(4):
        span = slice(n * block, (n + 1) * block)
        d_normed[span, :] = (
            dot(d_queries[span, :], held[0], NT)
            + dot(d_keys[span, :], held[1], NT)
            + dot(d_values[span, :], held[2], NT)
        )

    def load(i):
        return residual[panel.rows(i), :]

    def gradient(i, mask, normal):
        return jnp.where(mask, d_normed[panel.rows(i), :], 0.0)

    def emit(i, top, value, carry, columns):
        place = panel.rows(i)
        full = gout[place, :].astype(F32) + value
        d_residual[place, :] = full
        low = full.astype(B16)
        d_middle[place, :] = low
        row = low.astype(F32)
        store_shifted(panel, eb, i, top, row, columns)
        return (
            carry[0] + row,
            carry[1] + d_queries[place, :].astype(F32),
            carry[2] + d_values[place, :].astype(F32),
        )

    zero = panel.zero()
    grad_gain, grad_shift, found = norm_back(
        panel, load, stats, vec[6:7, :], same, gradient, emit, (zero, zero, zero)
    )
    store_edges(panel, eb)
    sums = [jnp.sum(found[0][k] + found[1][k], axis=0, keepdims=True) for k in range(3)]
    rows_out[0:1, :] = sums[0]
    rows_out[1:2, :] = grad_gain
    rows_out[2:3, :] = grad_shift
    rows_out[3:4, :] = sums[1]
    rows_out[4:5, :] = sums[2]
    rows_out[5:6, :] = gout_sum
    rows_out[6:8, :] = jnp.zeros((2, channels), F32)


def store_parts(meta, staged, keep, send, m):
    block = keep.shape[2]
    for k in range(4):
        keep[k, m] = staged[pl.ds(pl.multiple_of(meta[M_KEEP + k], block), block), :].astype(B16)
        send[k, m] = staged[pl.ds(pl.multiple_of(meta[M_SEND + k], block), block), :].astype(B16)


def tap_kernel(side, meta, hb, grad, keep, send, staged):
    pixels = side * side // 2
    tap = pl.program_id(0)
    start = pl.multiple_of((tap // 3) * side, side)
    col = tap % 3
    staged[...] = dot(hb[col, 0, pl.ds(start, pixels), :], grad[0:pixels, :], TN) + dot(
        hb[col, 1, pl.ds(start, pixels), :], grad[pixels:, :], TN
    )
    store_parts(meta, staged, keep, send, 0)


def back_kernel(side, last, meta, eb, source, stats, vec, *refs):
    if last:
        d_residual, pieces, refs = refs[0], refs[1:9], refs[9:]
        out, rows_out, held, sems, slope = refs
        first = 0
    else:
        pieces, refs = refs[:8], refs[8:]
        out, eb_out, rows_out, held, sems, slope = refs
        first = 3
    panel = Panel(meta[M_KIND], side, source.shape[1])
    start_weights(meta, pieces, held, sems)
    same = panel.same_group()
    gain, shift = vec[first : first + 1, :], vec[first + 1 : first + 2, :]
    wait_weights(meta, pieces, held, sems)
    pixels = panel.half * side
    for top in range(2):
        slope[top * pixels : (top + 1) * pixels, :] = conv_taps(panel, eb, held, top, NT, True)

    def load(i):
        return source[panel.rows(i), :].astype(F32)

    def gradient(i, mask, normal):
        place = panel.rows(i)
        if normal is None:
            return slope[place, :]
        pre = normal * gain + shift
        sig = 1.0 / (1.0 + jnp.exp(-pre))
        value = jnp.where(mask, slope[place, :] * (sig * (1.0 + pre * (1.0 - sig))), 0.0)
        slope[place, :] = value
        return value

    def emit(i, top, value, carry, columns):
        place = panel.rows(i)
        if last:
            out[place, :] = (d_residual[place, :] + value).astype(B16)
            return carry
        low = value.astype(B16)
        out[place, :] = low
        row = low.astype(F32)
        store_shifted(panel, eb_out, i, top, row, columns)
        return carry + row

    grad_gain, grad_shift, found = norm_back(
        panel, load, stats, gain, same, gradient, emit, 0 if last else panel.zero()
    )
    channels = panel.channels
    rows_out[0:1, :] = grad_gain
    rows_out[1:2, :] = grad_shift
    if last:
        rows_out[2:8, :] = jnp.zeros((6, channels), F32)
    else:
        store_edges(panel, eb_out)
        rows_out[2:3, :] = jnp.sum(found[0] + found[1], axis=0, keepdims=True)
        rows_out[3:8, :] = jnp.zeros((5, channels), F32)


def slot_kernel(sizes, chips, table, *refs):
    parts, (mine, send) = refs[: len(sizes) * chips], refs[len(sizes) * chips : -len(sizes)]
    whole = refs[-len(sizes) :]
    for g in range(len(sizes)):
        for d in range(chips):
            part = parts[g * chips + d]
            rows = part.shape[0]
            whole[g][pl.ds(pl.multiple_of(table[8 + d] * rows, 16), rows), :] = part[...]
    count, block = mine.shape[0], mine.shape[1]
    for out, base in ((mine, 0), (send, count)):
        for k in range(count):
            m = table[base + k]

            @pl.when(m < 0)
            def _(out=out, k=k):
                out[k] = jnp.zeros(out.shape[1:], out.dtype)

            low = 0
            for g, size in enumerate(sizes):

                @pl.when((m >= low) & (m < low + size))
                def _(out=out, k=k, g=g, low=low, m=m):
                    out[k] = whole[g][pl.ds(pl.multiple_of((m - low) * block, block), block), :]

                low += size


def adam_kernel(meta, master, first, second, mine, other, new_first, new_second, new_master, grad):
    block = mine.shape[1]
    core = meta[M_CORE]
    grad[pl.ds(pl.multiple_of(core * block, block), block), :] = mine[0].astype(F32)
    grad[pl.ds(pl.multiple_of((1 - core) * block, block), block), :] = other[0].astype(F32)
    results = adam_update(master[0], first[0], second[0], grad[...], LEARN_RATE)
    new_first[0], new_second[0], new_master[0] = results


def on_panel(
    image_in,
    panel_kind,
    owner_slot,
    out_grad,
    master,
    first_moment,
    second_moment,
    vec_master,
    vec_first,
    vec_second,
):
    side, channels = image_in.shape[2], image_in.shape[3]
    imgs = lax.axis_size("imgs")
    chips = imgs // 2
    own, depth = master.shape[0], master.shape[1]
    block = depth // 2
    total = side * side
    group, row = lax.axis_index("imgs"), lax.axis_index("rows")
    core, chip = group % 2, group // 2

    def permutation(target):
        pairs = []
        for i in range(imgs):
            for r in range(4):
                to_i, to_r = target(i, r)
                pairs.append((i * 4 + r, to_i * 4 + to_r))
        return pairs

    to_core = permutation(lambda i, r: (i ^ 1, r))
    to_near = [permutation(lambda i, r, k=k: (i, r ^ k)) for k in range(4)]
    to_first = permutation(lambda i, r: (i, r ^ (1 + i % 2)))
    to_second = permutation(lambda i, r: (i, r ^ (2 - i % 2)))
    to_chip = [permutation(lambda i, r, d=d: ((i + 2 * d) % imgs, r)) for d in range(chips)]

    def move(value, pairs):
        return lax.ppermute(value, AXES, pairs)

    near_first, near_second = row ^ (1 + core), row ^ (2 - core)
    quarters = [row, near_first, near_second, row ^ 3, row, near_second, near_first, row ^ 3]
    halves = [core] * 4 + [1 - core] * 4
    kind = lax.dynamic_index_in_dim(panel_kind, row, keepdims=False)
    meta = jnp.stack(
        [kind, core, row, chip]
        + [q * depth + h * block for q, h in zip(quarters, halves)]
        + [(row ^ k) * depth + core * block for k in range(4)]
        + [(row ^ k) * depth + (1 - core) * block for k in range(4)]
    ).astype(jnp.int32)

    low = shaped((own, block, channels), B16)
    mine, send = call(
        cast_kernel, (low, low), [SSPEC, VSPEC], (VSPEC, VSPEC), [], (meta, master)
    )
    other = move(send, to_core)
    sources = [mine] + [move(mine, to_chip[d]) for d in range(1, chips)]
    sources += [other] + [move(other, to_chip[d]) for d in range(1, chips)]
    slot_chip, slot_core = owner_slot // (2 * own), (owner_slot // own) % 2
    which = (chip - slot_chip) % chips + jnp.where(slot_core == core, 0, chips)
    table = jnp.stack([which, owner_slot % own]).astype(jnp.int32)
    sizes = (9, 9, 4)
    picked = call(
        functools.partial(pick_kernel, sizes, 2 * chips),
        tuple(shaped((n, block, channels), B16) for n in sizes),
        [SSPEC] + [ASPEC] * (2 * chips),
        (ASPEC,) * 3,
        [pltpu.SemaphoreType.DMA((sum(sizes),))],
        [table] + sources,
        moved=2 * sum(sizes) * block * channels * 2,
    )

    def all_pieces(own_part):
        near = move(own_part, to_first)
        far = move(own_part, to_second)
        corner = move(near, to_second)
        here = [own_part, near, far, corner]
        return here + [move(part, to_core) for part in here]

    pieces = [all_pieces(part) for part in picked]

    def weight_scratch(n):
        return [pltpu.VMEM((n, channels, channels), B16), pltpu.SemaphoreType.DMA((n, 8))]

    conv_flops = 2 * total * 9 * channels * channels
    conv_bytes = 9 * channels * channels * 2 + 8 * total * channels
    wide = shaped((total, channels), F32)
    narrow = shaped((total, channels), B16)
    stat = shaped((2 * STAT, channels), F32)
    shifted = shaped((3, 2, (side // 2 + 2) * side, channels), B16)
    vec_rows = shaped((8, channels), F32)

    image = lax.all_to_all(image_in, "rows", 0, 0, tiled=True).reshape(total, channels)
    cotangent = lax.all_to_all(out_grad, "rows", 0, 0, tiled=True).reshape(total, channels)
    hb_one, stats_one = call(
        functools.partial(first_kernel, side),
        (shifted, stat),
        [SSPEC, VSPEC, VSPEC],
        (VSPEC, VSPEC),
        [],
        (meta, image, vec_master),
        moved=5 * total * channels * 2,
    )
    middle, stats_two, hb_two = call(
        functools.partial(middle_kernel, side),
        (wide, stat, shifted),
        [SSPEC, VSPEC, VSPEC] + [ASPEC] * 8,
        (VSPEC,) * 3,
        weight_scratch(9),
        [meta, hb_one, vec_master] + pieces[0],
        flops=conv_flops,
        moved=conv_bytes,
    )
    residual, stats_three, normed = call(
        functools.partial(residual_kernel, side),
        (wide, stat, narrow),
        [SSPEC, VSPEC, VSPEC, VSPEC] + [ASPEC] * 8,
        (VSPEC,) * 3,
        weight_scratch(9),
        [meta, hb_two, image, vec_master] + pieces[1],
        flops=conv_flops,
        moved=conv_bytes,
    )
    parts_of = lambda n: shaped((4, n, block, channels), B16)
    low_scratch = pltpu.VMEM((total, channels), B16)
    (block_out, d_residual, d_middle_two, eb_two, keep_attn, send_attn, rows_attn) = call(
        functools.partial(attention_kernel, side),
        (narrow, wide, narrow, shifted, parts_of(4), parts_of(4), vec_rows),
        [SSPEC] + [VSPEC] * 5 + [ASPEC] * 8,
        (VSPEC,) * 7,
        weight_scratch(4)
        + [low_scratch] * 3
        + [pltpu.VMEM((total, total), F32)]
        + [pltpu.VMEM((total, total), B16)] * 2
        + [low_scratch] * 6
        + [pltpu.VMEM((total, channels), F32), pltpu.VMEM((channels, channels), F32)],
        [meta, residual, stats_three, normed, cotangent, vec_master] + pieces[2],
        flops=3 * conv_flops,
        moved=2 * conv_bytes,
    )

    def tap_grads(hb, grad):
        whole = lambda *shape: pl.BlockSpec(shape, lambda t: (0,) * len(shape))
        part = pl.BlockSpec((4, 1, block, channels), lambda t: (0, t, 0, 0))
        return call(
            functools.partial(tap_kernel, side),
            (parts_of(9), parts_of(9)),
            [SSPEC, whole(*hb.shape), whole(*grad.shape)],
            (part, part),
            [pltpu.VMEM((channels, channels), F32)],
            (meta, hb, grad),
            flops=conv_flops,
            moved=conv_bytes,
            grid=(9,),
        )

    def sum_chips(keep, send):
        got = move(send, to_core)
        both = [(keep[k].astype(F32) + got[k].astype(F32)).astype(B16) for k in range(4)]
        arrived = [move(both[k], to_near[k]) for k in range(1, 4)]
        summed = sum((v.astype(F32) for v in arrived), both[0].astype(F32)).astype(B16)
        rows = summed.shape[0] * block // chips
        blocks = summed.reshape(chips, rows, channels)
        terms = [lax.dynamic_index_in_dim(blocks, chip, keepdims=False)]
        for d in range(1, chips):
            there = lax.dynamic_index_in_dim(blocks, (chip + d) % chips, keepdims=False)
            terms.append(move(there, to_chip[d]))
        own_sum = sum((v.astype(F32) for v in terms[1:]), terms[0].astype(F32)).astype(B16)
        return [own_sum] + [move(own_sum, to_chip[d]) for d in range(1, chips)]

    sums_attn = sum_chips(keep_attn, send_attn)
    sums_two = sum_chips(*tap_grads(hb_two, d_middle_two))
    d_middle_one, eb_one, rows_two = call(
        functools.partial(back_kernel, side, False),
        (narrow, shifted, vec_rows),
        [SSPEC] + [VSPEC] * 4 + [ASPEC] * 8,
        (VSPEC,) * 3,
        weight_scratch(9) + [pltpu.VMEM((total, channels), F32)],
        [meta, eb_two, middle, stats_two, vec_master] + pieces[1],
        flops=conv_flops,
        moved=conv_bytes,
    )
    sums_one = sum_chips(*tap_grads(hb_one, d_middle_one))
    d_image, rows_one = call(
        functools.partial(back_kernel, side, True),
        (narrow, vec_rows),
        [SSPEC] + [VSPEC] * 5 + [ASPEC] * 8,
        (VSPEC,) * 2,
        weight_scratch(9) + [pltpu.VMEM((total, channels), F32)],
        [meta, eb_one, image, stats_one, vec_master, d_residual] + pieces[0],
        flops=conv_flops,
        moved=conv_bytes,
    )

    def to_rows(value):
        split = value.reshape(4, side // 4, side, channels)
        return lax.all_to_all(split, "rows", 0, 0, tiled=True)

    block_out, input_grad = to_rows(block_out), to_rows(d_image)

    vec_grads = jnp.concatenate(
        [
            rows_one[0:2],
            rows_two[2:3],
            rows_two[0:2],
            rows_attn[0:6],
        ]
    )
    for pairs in (to_core, to_near[1], to_near[2]):
        vec_grads = vec_grads + move(vec_grads, pairs)
    step = 1
    while step < chips:
        vec_grads = vec_grads + move(
            vec_grads, permutation(lambda i, r, step=step: (i ^ (2 * step), r))
        )
        step *= 2

    def matrix_of(first_slot):
        slots = first_slot + jnp.arange(own, dtype=jnp.int32)
        placing = owner_slot[None, :] == slots[:, None]
        found = jnp.sum(jnp.where(placing, jnp.arange(owner_slot.shape[0])[None, :] + 1, 0), axis=1)
        return found - 1

    slots_table = jnp.concatenate(
        [
            matrix_of(group * own),
            matrix_of((group ^ 1) * own),
            (chip - jnp.arange(chips)) % chips,
        ]
    ).astype(jnp.int32)
    all_sums = sums_one + sums_two + sums_attn
    mine, send = call(
        functools.partial(slot_kernel, sizes, chips),
        (low, low),
        [SSPEC] + [VSPEC] * len(all_sums),
        (VSPEC, VSPEC),
        [pltpu.VMEM((n * block, channels), B16) for n in sizes],
        [slots_table] + all_sums,
    )
    other = move(send, to_core)
    deep = pl.BlockSpec((1, depth, channels), lambda t: (t, 0, 0))
    flat = pl.BlockSpec((1, block, channels), lambda t: (t, 0, 0))
    slot_shape = shaped(master.shape, F32)
    new_first, new_second, new_master = call(
        adam_kernel,
        (slot_shape,) * 3,
        [SSPEC, deep, deep, deep, flat, flat],
        (deep,) * 3,
        [pltpu.VMEM((depth, channels), F32)],
        (meta, master, first_moment, second_moment, mine, other),
        moved=6 * own * depth * channels * 4,
        grid=(own,),
    )
    vec_results = adam_update(vec_master, vec_first, vec_second, vec_grads, VEC_RATE)
    return (block_out, input_grad, new_first, new_second, new_master) + vec_results


def on_slice(*args):
    image_in = args[0]
    panels, row_count, col_count, channels = image_in.shape
    rows, imgs = lax.axis_size("rows"), lax.axis_size("imgs")
    chips = imgs // 2
    whole_panels = (
        rows == 4
        and panels == rows
        and row_count * rows == col_count == 32
        and channels == 512
        and args[4].shape[0] == 4
        and imgs == 2 * chips
        and chips in (1, 2, 4)
    )
    return on_panel(*args) if whole_panels else on_device(*args)


def solution(mesh):
    in_specs = (
        P("imgs", "rows", None, None),
        P("imgs"),
        P(),
        P("imgs", "rows", None, None),
        P("imgs", "rows", None),
        P("imgs", "rows", None),
        P("imgs", "rows", None),
        P(),
        P(),
        P(),
    )
    out_specs = (
        P("imgs", "rows", None, None),
        P("imgs", "rows", None, None),
        P("imgs", "rows", None),
        P("imgs", "rows", None),
        P("imgs", "rows", None),
        P(),
        P(),
        P(),
    )
    return jax.shard_map(
        on_slice, mesh=mesh, in_specs=in_specs, out_specs=out_specs, check_vma=False
    )
```

```python
import functools
import math

import jax
import jax.numpy as jnp
from jax import lax
from jax.experimental import pallas as pl
from jax.experimental.pallas import tpu as pltpu
from jax.sharding import PartitionSpec as P

GROUPS = 32
MATS = 22
STEP = 5


EXACT_PRECISION = lax.Precision.HIGHEST
NORM_EPS = 1e-06
LEARN_RATE = 0.05
VEC_RATE = 0.2
BETA_ONE = 0.5
BETA_TWO = 0.5
ADAM_EPS = 1e-08
WEIGHT_DECAY = 0.01
MASK_FILL = -1000000000.0


def extended(cells, sides, width):
    for axis, dim in sides:
        count = lax.axis_size(axis)
        ends = count - 1
        head = lax.slice_in_dim(cells, 0, width, axis=dim)
        tail = lax.slice_in_dim(cells, cells.shape[dim] - width, cells.shape[dim], axis=dim)
        cells = jnp.concatenate(
            [
                lax.ppermute(tail, axis, [(i, (i + 1) % count) for i in range(ends)]),
                cells,
                lax.ppermute(head, axis, [((i + 1) % count, i) for i in range(ends)]),
            ],
            axis=dim,
        )
    return cells


def panel_ids(kind_list, row_index, col_index, panel_side):
    row_grid = row_index[None, :, None]
    col_grid = col_index[None, None, :]
    kind_grid = kind_list[:, None, None]
    half_side = panel_side // 2
    part_side = 3 * panel_side // 4
    inside = (row_grid >= 0) & (row_grid < panel_side) & (col_grid >= 0) & (col_grid < panel_side)
    quarter = 2 * (row_grid >= half_side).astype(jnp.int32) + (col_grid >= half_side).astype(
        jnp.int32
    )
    zero_grid = jnp.zeros_like(quarter)
    corner = jnp.where((row_grid < part_side) & (col_grid < part_side), zero_grid, zero_grid - 1)
    labels = jnp.where(
        kind_grid == 0,
        zero_grid,
        jnp.where(kind_grid == 1, corner, jnp.where(kind_grid == 2, quarter, zero_grid - 1)),
    )
    return jnp.where(inside & (labels >= 0), labels, -1)


def spread_pix(onehot, per_group):
    return jnp.einsum("prwi,pig->prwg", onehot, per_group, precision=EXACT_PRECISION)


def group_stats(value_rows, onehot, counts):
    panel_count, row_count, col_count, channel_count = value_rows.shape
    grouped = value_rows.reshape(panel_count, row_count, col_count, GROUPS, channel_count // GROUPS)
    first_sums = lax.psum(
        jnp.einsum("prwi,prwgc->pig", onehot, grouped, precision=EXACT_PRECISION), "rows"
    )
    group_mean = first_sums / counts[:, :, None]
    centred = grouped - spread_pix(onehot, group_mean)[..., None]
    square_sums = jnp.einsum(
        "prwi,prwgc->pig", onehot, centred * centred, precision=EXACT_PRECISION
    )
    spread = lax.psum(square_sums, "rows") / counts[:, :, None]
    scale_pix = spread_pix(onehot, lax.rsqrt(spread + NORM_EPS))
    normal_val = (centred * scale_pix[..., None]).reshape(value_rows.shape)
    return (normal_val, scale_pix)


def group_back(gradient, normal_val, scale_pix, gain_row, onehot, counts):
    panel_count, row_count, col_count, channel_count = gradient.shape
    grad_gain = jnp.sum(gradient * normal_val, axis=(0, 1, 2))
    grad_shift = jnp.sum(gradient, axis=(0, 1, 2))
    scaled = (gradient * gain_row).reshape(
        panel_count, row_count, col_count, GROUPS, channel_count // GROUPS
    )
    normal_grp = normal_val.reshape(scaled.shape)
    plain_sums = jnp.einsum("prwi,prwgc->pig", onehot, scaled, precision=EXACT_PRECISION)
    cross_sums = jnp.einsum(
        "prwi,prwgc->pig", onehot, scaled * normal_grp, precision=EXACT_PRECISION
    )
    plain_sums, cross_sums = lax.psum((plain_sums, cross_sums), "rows")
    plain_pix = spread_pix(onehot, plain_sums / counts[:, :, None])
    cross_pix = spread_pix(onehot, cross_sums / counts[:, :, None])
    result = scale_pix[..., None] * (
        scaled - plain_pix[..., None] - normal_grp * cross_pix[..., None]
    )
    return (result.reshape(gradient.shape), grad_gain, grad_shift)


def silu_slope(pre_act):
    sigmoid_val = jax.nn.sigmoid(pre_act)
    return sigmoid_val * (1.0 + pre_act * (1.0 - sigmoid_val))


def conv_forward(hidden, weight_cat, tap_masks):
    panel_count, row_count, col_count, channel_count = hidden.shape
    padded = extended(hidden, (("rows", 1),), 1)
    padded = jnp.pad(padded, ((0, 0), (0, 0), (1, 1), (0, 0)))
    columns = jnp.concatenate(
        [
            padded[
                :,
                tap_index // 3 : tap_index // 3 + row_count,
                tap_index % 3 : tap_index % 3 + col_count,
                :,
            ]
            * tap_masks[tap_index]
            for tap_index in range(9)
        ],
        axis=-1,
    )
    columns = columns.reshape(-1, 9 * channel_count)
    result = jnp.dot(columns, weight_cat, preferred_element_type=jnp.float32)
    return (result.reshape(hidden.shape), columns)


def conv_backward(gradient, columns, weight_cat, tap_masks):
    panel_count, row_count, col_count, channel_count = gradient.shape
    grad_flat = gradient.reshape(-1, channel_count)
    weight_grad = jnp.einsum("mk,mc->kc", columns, grad_flat, preferred_element_type=jnp.float32)
    col_grads = jnp.einsum("mc,kc->mk", grad_flat, weight_cat, preferred_element_type=jnp.float32)
    col_grads = col_grads.reshape(panel_count, row_count, col_count, 9, channel_count)
    padded_grad = jnp.zeros((panel_count, row_count + 2, col_count + 2, channel_count), jnp.float32)
    for tap_index in range(9):
        tap_row = tap_index // 3
        tap_col = tap_index % 3
        padded_grad = padded_grad.at[
            :, tap_row : tap_row + row_count, tap_col : tap_col + col_count, :
        ].add(col_grads[:, :, :, tap_index, :] * tap_masks[tap_index])
    padded_grad = padded_grad[:, :, 1 : col_count + 1, :]
    edge_rows = jnp.concatenate(
        [padded_grad[:, 0:1], padded_grad[:, row_count + 1 : row_count + 2]], axis=1
    )
    arrived = extended(edge_rows.astype(jnp.bfloat16), (("rows", 1),), 1).astype(edge_rows.dtype)
    inner = padded_grad[:, 1 : row_count + 1]
    inner = inner.at[:, 0].add(arrived[:, 0])
    inner = inner.at[:, row_count - 1].add(arrived[:, 3])
    return (inner, weight_grad)


def adam_update(weight, first_old, second, gradient, step_rate):
    new_first = BETA_ONE * first_old + (1.0 - BETA_ONE) * gradient
    new_second = BETA_TWO * second + (1.0 - BETA_TWO) * gradient * gradient
    first_hat = new_first / (1.0 - BETA_ONE**STEP)
    second_hat = new_second / (1.0 - BETA_TWO**STEP)
    new_weight = weight - step_rate * (
        first_hat / (jnp.sqrt(second_hat) + ADAM_EPS) + WEIGHT_DECAY * weight
    )
    return (new_first, new_second, new_weight)


def on_device(
    image_in,
    panel_kind,
    owner_slot,
    out_grad,
    master,
    first_moment,
    second_moment,
    vec_master,
    vec_first,
    vec_second,
):
    panel_count, row_count, col_count, channel_count = image_in.shape
    height_all = row_count * lax.axis_size("rows")
    group_width = channel_count // GROUPS
    pixel_count = panel_count * row_count * col_count
    local_pix = row_count * col_count
    slot_total = master.shape[0] * lax.axis_size("imgs")
    inv_root = 1.0 / math.sqrt(channel_count)
    placing = owner_slot[None, :] == jnp.arange(slot_total, dtype=jnp.int32)[:, None]
    slot_weights = lax.all_gather(master.astype(jnp.bfloat16), "imgs", axis=0, tiled=True)
    picked = jnp.einsum(
        "sm,sij->mij",
        placing.astype(jnp.bfloat16),
        slot_weights,
        preferred_element_type=jnp.float32,
    ).astype(jnp.bfloat16)
    weights = lax.all_gather(picked, "rows", axis=1, tiled=True)
    conv_first = weights[0:9].reshape(9 * channel_count, channel_count)
    conv_second = weights[9:18].reshape(9 * channel_count, channel_count)
    attn_in = jnp.concatenate([weights[18], weights[19], weights[20]], axis=1)
    attn_out = weights[21]
    first_row = lax.axis_index("rows") * row_count
    col_range = jnp.arange(col_count, dtype=jnp.int32)
    labels = panel_ids(
        panel_kind, first_row + jnp.arange(row_count, dtype=jnp.int32), col_range, height_all
    )
    outer_labels = panel_ids(
        panel_kind,
        first_row + jnp.arange(-1, row_count + 1, dtype=jnp.int32),
        jnp.arange(-1, col_count + 1, dtype=jnp.int32),
        height_all,
    )
    whole_labels = panel_ids(
        panel_kind, jnp.arange(height_all, dtype=jnp.int32), col_range, height_all
    )
    label_range = jnp.arange(4, dtype=jnp.int32)
    onehot = (labels[..., None] == label_range).astype(jnp.float32)
    validity = (labels >= 0).astype(jnp.float32)[..., None]
    counts = jnp.maximum(
        jnp.sum((whole_labels[..., None] == label_range).astype(jnp.float32), axis=(1, 2))
        * group_width,
        1.0,
    )
    tap_masks = [
        (
            (
                outer_labels[
                    :,
                    tap_index // 3 : tap_index // 3 + row_count,
                    tap_index % 3 : tap_index % 3 + col_count,
                ]
                == labels
            )
            & (labels >= 0)
        ).astype(jnp.bfloat16)[..., None]
        for tap_index in range(9)
    ]
    image_vals = image_in.astype(jnp.float32)
    normal_one, scale_one = group_stats(image_vals, onehot, counts)
    pre_one = normal_one * vec_master[0] + vec_master[1]
    hidden_one = jax.nn.silu(pre_one).astype(jnp.bfloat16)
    conv_out, columns_one = conv_forward(hidden_one, conv_first, tap_masks)
    middle = conv_out + vec_master[2]
    normal_two, scale_two = group_stats(middle, onehot, counts)
    pre_two = normal_two * vec_master[3] + vec_master[4]
    hidden_two = jax.nn.silu(pre_two).astype(jnp.bfloat16)
    conv_out_two, columns_two = conv_forward(hidden_two, conv_second, tap_masks)
    residual = image_vals + conv_out_two + vec_master[5]
    normal_three, scale_three = group_stats(residual, onehot, counts)
    normed = (
        (normal_three * vec_master[6] + vec_master[7])
        .astype(jnp.bfloat16)
        .reshape(pixel_count, channel_count)
    )
    qkv_vals = jnp.dot(normed, attn_in, preferred_element_type=jnp.float32)
    query_matrix = (
        (qkv_vals[:, :channel_count] + vec_master[8])
        .astype(jnp.bfloat16)
        .reshape(panel_count, local_pix, channel_count)
    )
    key_loc = (
        qkv_vals[:, channel_count : 2 * channel_count]
        .astype(jnp.bfloat16)
        .reshape(panel_count, row_count, col_count, channel_count)
    )
    values_loc = (
        (qkv_vals[:, 2 * channel_count :] + vec_master[9])
        .astype(jnp.bfloat16)
        .reshape(panel_count, row_count, col_count, channel_count)
    )
    keys_all, values_all = (
        lax.all_gather(key_loc, "rows", axis=1, tiled=True),
        lax.all_gather(values_loc, "rows", axis=1, tiled=True),
    )
    keys_all = keys_all.reshape(panel_count, height_all * col_count, channel_count)
    values_all = values_all.reshape(panel_count, height_all * col_count, channel_count)
    query_labels = labels.reshape(panel_count, -1)
    key_labels = whole_labels.reshape(panel_count, -1)
    same_image = (query_labels[:, :, None] == key_labels[:, None, :]) & (
        key_labels[:, None, :] >= 0
    )
    attention_scores = (
        jnp.einsum("pqc,pkc->pqk", query_matrix, keys_all, preferred_element_type=jnp.float32)
        * inv_root
    )
    attention_scores = jnp.where(same_image, attention_scores, MASK_FILL)
    row_max = jnp.max(attention_scores, axis=-1, keepdims=True)
    exp_scores = jnp.exp(attention_scores - row_max)
    exp_total = jnp.sum(exp_scores, axis=-1, keepdims=True)
    softmax_weights = exp_scores / exp_total
    log_total = row_max[..., 0] + jnp.log(exp_total[..., 0])
    attended_values = jnp.einsum(
        "pqk,pkc->pqc",
        softmax_weights.astype(jnp.bfloat16),
        values_all,
        preferred_element_type=jnp.float32,
    ).astype(jnp.bfloat16)
    attended_values = attended_values.reshape(pixel_count, channel_count)
    projected = (
        jnp.dot(attended_values, attn_out, preferred_element_type=jnp.float32) + vec_master[10]
    ).reshape(image_in.shape)
    block_out = ((residual + projected) * validity).astype(jnp.bfloat16)
    grad_out = out_grad.astype(jnp.float32) * validity
    grad_flat = grad_out.astype(jnp.bfloat16).reshape(pixel_count, channel_count)
    grad_proj = jnp.einsum(
        "mc,md->cd", attended_values, grad_flat, preferred_element_type=jnp.float32
    )
    bias_proj = jnp.sum(grad_out, axis=(0, 1, 2))
    d_attended = jnp.einsum(
        "md,cd->mc", grad_flat, attn_out, preferred_element_type=jnp.float32
    ).astype(jnp.bfloat16)
    d_attended = d_attended.reshape(panel_count, local_pix, channel_count)
    again_scores = (
        jnp.einsum("pqc,pkc->pqk", query_matrix, keys_all, preferred_element_type=jnp.float32)
        * inv_root
    )
    again_scores = jnp.where(same_image, again_scores, MASK_FILL)
    again_soft = jnp.exp(again_scores - log_total[..., None])
    d_soft = jnp.einsum("pqc,pkc->pqk", d_attended, values_all, preferred_element_type=jnp.float32)
    row_delta = jnp.sum(d_soft * again_soft, axis=-1)
    d_scores = (again_soft * (d_soft - row_delta[..., None])).astype(jnp.bfloat16)
    d_queries = (
        jnp.einsum("pqk,pkc->pqc", d_scores, keys_all, preferred_element_type=jnp.float32)
        * inv_root
    ).astype(jnp.bfloat16)
    d_key_all = (
        jnp.einsum("pqk,pqc->pkc", d_scores, query_matrix, preferred_element_type=jnp.float32)
        * inv_root
    )
    d_value_all = jnp.einsum(
        "pqk,pqc->pkc",
        again_soft.astype(jnp.bfloat16),
        d_attended,
        preferred_element_type=jnp.float32,
    )
    d_key_all = d_key_all.reshape(panel_count, height_all, col_count, channel_count)
    d_value_all = d_value_all.reshape(panel_count, height_all, col_count, channel_count)
    d_keys, d_values = (
        lax.psum_scatter(
            d_key_all.astype(jnp.bfloat16), "rows", scatter_dimension=1, tiled=True
        ).astype(jnp.float32),
        lax.psum_scatter(
            d_value_all.astype(jnp.bfloat16), "rows", scatter_dimension=1, tiled=True
        ).astype(jnp.float32),
    )
    d_keys = d_keys.reshape(pixel_count, channel_count).astype(jnp.bfloat16)
    d_values = d_values.reshape(pixel_count, channel_count).astype(jnp.bfloat16)
    d_queries = d_queries.reshape(pixel_count, channel_count)
    d_qkv = jnp.concatenate([d_queries, d_keys, d_values], axis=1)
    grad_qkv = jnp.einsum("mc,md->cd", normed, d_qkv, preferred_element_type=jnp.float32)
    bias_query = jnp.sum(d_queries, axis=0, dtype=jnp.float32)
    bias_value = jnp.sum(d_values, axis=0, dtype=jnp.float32)
    d_normed = jnp.einsum("md,cd->mc", d_qkv, attn_in, preferred_element_type=jnp.float32).reshape(
        image_in.shape
    )
    d_three, gain_three, shift_three = group_back(
        d_normed, normal_three, scale_three, vec_master[6], onehot, counts
    )
    d_residual = grad_out + d_three
    d_middle_two = d_residual.astype(jnp.bfloat16)
    bias_two = jnp.sum(d_middle_two, axis=(0, 1, 2), dtype=jnp.float32)
    d_hidden_two, grad_conv_two = conv_backward(d_middle_two, columns_two, conv_second, tap_masks)
    d_middle, gain_two, shift_two = group_back(
        d_hidden_two * silu_slope(pre_two), normal_two, scale_two, vec_master[3], onehot, counts
    )
    d_middle_one = d_middle.astype(jnp.bfloat16)
    bias_one = jnp.sum(d_middle_one, axis=(0, 1, 2), dtype=jnp.float32)
    d_hidden_one, grad_conv_one = conv_backward(d_middle_one, columns_one, conv_first, tap_masks)
    d_input, gain_one, shift_one = group_back(
        d_hidden_one * silu_slope(pre_one), normal_one, scale_one, vec_master[0], onehot, counts
    )
    input_grad = (d_residual + d_input).astype(jnp.bfloat16)
    vec_grads = jnp.stack(
        [
            gain_one,
            shift_one,
            bias_one,
            gain_two,
            shift_two,
            bias_two,
            gain_three,
            shift_three,
            bias_query,
            bias_value,
            bias_proj,
        ]
    )
    vec_grads = lax.psum(vec_grads, ("imgs", "rows"))
    mat_grads = jnp.concatenate(
        [
            grad_conv_one.reshape(9, channel_count, channel_count),
            grad_conv_two.reshape(9, channel_count, channel_count),
            grad_qkv[:, :channel_count][None],
            grad_qkv[:, channel_count : 2 * channel_count][None],
            grad_qkv[:, 2 * channel_count :][None],
            grad_proj[None],
        ],
        axis=0,
    )
    row_grads = lax.psum_scatter(
        mat_grads.astype(jnp.bfloat16), "rows", scatter_dimension=1, tiled=True
    ).astype(jnp.float32)
    slot_terms = jnp.einsum(
        "sm,mij->sij", placing.astype(jnp.float32), row_grads, precision=EXACT_PRECISION
    )
    owned_grads = lax.psum_scatter(
        slot_terms.astype(jnp.bfloat16), "imgs", scatter_dimension=0, tiled=True
    ).astype(jnp.float32)
    new_first, new_second, new_master = adam_update(
        master, first_moment, second_moment, owned_grads, LEARN_RATE
    )
    vec_first_new, vec_second_new, vec_master_new = adam_update(
        vec_master, vec_first, vec_second, vec_grads, VEC_RATE
    )
    return (
        block_out,
        input_grad,
        new_first,
        new_second,
        new_master,
        vec_first_new,
        vec_second_new,
        vec_master_new,
    )


F32 = jnp.float32
B16 = jnp.bfloat16
AXES = ("imgs", "rows")
NN = (((1,), (0,)), ((), ()))
NT = (((1,), (1,)), ((), ()))
TN = (((0,), (0,)), ((), ()))
VSPEC = pl.BlockSpec(memory_space=pltpu.VMEM)
SSPEC = pl.BlockSpec(memory_space=pltpu.SMEM)
ASPEC = pl.BlockSpec(memory_space=pl.ANY)
VMEM_BYTES = 52 * 2**20
STAT = 16
M_KIND, M_CORE, M_OFF, M_KEEP, M_SEND, M_FROM = 0, 1, 2, 10, 14, 18
LANES = 128


def dot(left, right, dims):
    return lax.dot_general(left, right, dims, preferred_element_type=F32)


def shaped(shape, dtype):
    return jax.ShapeDtypeStruct(shape, dtype)


def call(body, outs, in_specs, out_specs, scratch, args, flops=0, moved=0, grid=None):
    extra = {} if grid is None else {"grid": grid}
    return pl.pallas_call(
        body,
        out_shape=outs,
        in_specs=in_specs,
        out_specs=out_specs,
        scratch_shapes=scratch,
        compiler_params=pltpu.CompilerParams(vmem_limit_bytes=VMEM_BYTES),
        cost_estimate=pl.CostEstimate(flops=flops, bytes_accessed=moved, transcendentals=0),
        **extra,
    )(*args)


class Panel:
    def __init__(self, kind, side, channels):
        self.kind, self.side, self.channels = kind, side, channels
        self.half = side // 2
        self.width = channels // GROUPS
        part = 3 * side // 4
        self.limit = jnp.where(kind == 3, 0, jnp.where(kind == 1, part, side))
        pixels = jnp.where(
            kind == 2, self.half * self.half, jnp.where(kind == 1, part * part, side * side)
        )
        count = jnp.where(kind == 3, 1, pixels * self.width)
        self.inverse = 1.0 / count.astype(F32)
        self.four = jnp.where(kind == 2, 1.0, 0.0).astype(F32)
        self.cut = jnp.where(kind == 2, self.half, -1)

    def columns(self):
        return lax.broadcasted_iota(jnp.int32, (self.side, self.channels), 0)

    def mask(self, columns, i):
        return columns < jnp.where(i < self.limit, self.limit, 0)

    def rows(self, i):
        return pl.ds(pl.multiple_of(i * self.side, self.side), self.side)

    def same_group(self):
        shift = self.width.bit_length() - 1
        shape = (LANES, LANES)
        left = lax.broadcasted_iota(jnp.int32, shape, 0) >> shift
        right = lax.broadcasted_iota(jnp.int32, shape, 1) >> shift
        return jnp.where(left == right, 1.0, 0.0).astype(B16)

    def loop(self, body, init):
        found = []
        for top in range(2):
            found.append(
                lax.fori_loop(
                    0,
                    self.half,
                    lambda t, carry, top=top: body(top * self.half + t, top, carry),
                    init,
                    unroll=2,
                )
            )
        return found

    def spread(self, stat, top):
        shape = (self.half, self.channels)
        return jnp.concatenate(
            [
                jnp.broadcast_to(stat[2 * top : 2 * top + 1], shape),
                jnp.broadcast_to(stat[2 * top + 1 : 2 * top + 2], shape),
            ],
            axis=0,
        )

    def quadrants(self, upper, lower):
        parts = []
        for acc in (upper, lower):
            for left in range(2):
                parts.append(
                    jnp.sum(acc[left * self.half : (left + 1) * self.half], axis=0, keepdims=True)
                )
        parts.append(jnp.zeros((STAT - 4, self.channels), F32))
        return jnp.concatenate(parts, axis=0)

    def over_images(self, sums):
        total = jnp.sum(sums, axis=0, keepdims=True)
        return sums * self.four + total * (1.0 - self.four)

    def over_groups(self, sums, same):
        high = sums.astype(B16)
        rest = sums - high.astype(F32)
        middle = rest.astype(B16)
        low = (rest - middle.astype(F32)).astype(B16)
        cuts = range(0, self.channels, LANES)
        stacked = jnp.concatenate(
            [part[:, c : c + LANES] for part in (high, middle, low) for c in cuts], axis=0
        )
        found = dot(stacked, same, NN)
        third = len(cuts) * STAT
        found = found[0:third] + found[third : 2 * third] + found[2 * third :]
        return jnp.concatenate(
            [found[k * STAT : (k + 1) * STAT] for k in range(len(cuts))], axis=1
        )

    def reduced(self, sums, same):
        return self.over_groups(self.over_images(sums), same) * self.inverse

    def zero(self):
        return jnp.zeros((self.side, self.channels), F32)


def norm_stats(panel, load, same):
    columns = panel.columns()

    def add_plain(i, top, carry):
        return carry + jnp.where(panel.mask(columns, i), load(i), 0.0)

    mean = panel.reduced(panel.quadrants(*panel.loop(add_plain, panel.zero())), same)
    means = [panel.spread(mean, top) for top in range(2)]

    def add_square(i, top, carry):
        centred = load(i) - means[top]
        return carry + jnp.where(panel.mask(columns, i), centred * centred, 0.0)

    spread = panel.reduced(panel.quadrants(*panel.loop(add_square, panel.zero())), same)
    return mean, lax.rsqrt(spread + NORM_EPS)


def store_shifted(panel, hb, i, top, row, columns):
    side = panel.side
    place = pl.ds(pl.multiple_of((i - top * panel.half + 1) * side, side), side)
    before = pltpu.roll(row, 1, 0)
    after = pltpu.roll(row, side - 1, 0)
    from_left = (columns != 0) & (columns != panel.cut)
    from_right = (columns != side - 1) & (columns != panel.cut - 1)
    hb[0, top, place, :] = jnp.where(from_left, before, 0.0).astype(B16)
    hb[1, top, place, :] = row.astype(B16)
    hb[2, top, place, :] = jnp.where(from_right, after, 0.0).astype(B16)


def store_edges(panel, hb):
    side, half = panel.side, panel.half
    joined = 1.0 - panel.four
    blank = jnp.zeros((side, panel.channels), B16)
    for b in range(3):
        hb[b, 0, 0:side, :] = blank
        hb[b, 1, (half + 1) * side : (half + 2) * side, :] = blank
        upper = hb[b, 0, half * side : (half + 1) * side, :].astype(F32) * joined
        lower = hb[b, 1, side : 2 * side, :].astype(F32) * joined
        hb[b, 1, 0:side, :] = upper.astype(B16)
        hb[b, 0, (half + 1) * side : (half + 2) * side, :] = lower.astype(B16)


def silu_row(panel, load, columns, mean, rstd, gain, shift, i):
    mask = panel.mask(columns, i)
    normal = jnp.where(mask, (load(i) - mean) * rstd, 0.0)
    pre = normal * gain + shift
    return jnp.where(mask, pre / (1.0 + jnp.exp(-pre)), 0.0)


def silu_shifted(panel, load, mean, rstd, gain, shift, hb):
    columns = panel.columns()
    means = [panel.spread(mean, top) for top in range(2)]
    rstds = [panel.spread(rstd, top) for top in range(2)]

    def step(i, top, carry):
        row = silu_row(panel, load, columns, means[top], rstds[top], gain, shift, i)
        store_shifted(panel, hb, i, top, row, columns)
        return carry

    panel.loop(step, 0)
    store_edges(panel, hb)


PIECES = 8


def weight_copies(meta, pieces, first, held, sems, m):
    block = pieces[0].shape[1]
    slot = meta[M_FROM + MATS + first + m]
    other_slot = meta[M_FROM + 2 * MATS + first + m]
    copies = []
    for t in range(8):
        source = pieces[t].at[slot if t < 4 else other_slot]
        place = pl.ds(pl.multiple_of(meta[M_OFF + t], block), block)
        copies.append(pltpu.make_async_copy(source, held.at[m, place, :], sems.at[m, t]))
    return copies


class Weights:
    def __init__(self, meta, pieces, first, held, sems):
        self.copies = lambda e, m: weight_copies(
            meta, pieces[PIECES * e : PIECES * (e + 1)], first, held, sems, m
        )
        self.held = held
        for m in range(held.shape[0]):
            for e in range(len(pieces) // PIECES):

                @pl.when(meta[M_FROM + first + m] == e)
                def _(e=e, m=m):
                    for copy in self.copies(e, m):
                        copy.start()

    def wait(self, m):
        for copy in self.copies(0, m):
            copy.wait()


def conv_taps(panel, hb, weights, top, dims, flip):
    side, pixels = panel.side, panel.half * panel.side
    total = jnp.zeros((pixels, panel.channels), F32)
    for a in range(3):
        if top == 0:
            for b in range(3):
                weights.wait(3 * a + b)
        for b in range(3):
            row, col = (2 - a, 2 - b) if flip else (a, b)
            total = total + dot(
                hb[col, top, row * side : row * side + pixels, :], weights.held[3 * a + b], dims
            )
    return total


def cast_kernel(meta, master, mine, send):
    block = mine.shape[1]
    for out, half in ((mine, meta[M_CORE]), (send, 1 - meta[M_CORE])):
        place = pl.ds(pl.multiple_of(half * block, block), block)
        out[...] = master[:, place, :].astype(B16)


def first_kernel(side, meta, image, vec, hb, stats):
    panel = Panel(meta[M_KIND], side, image.shape[1])

    def load(i):
        return image[panel.rows(i), :].astype(F32)

    mean, rstd = norm_stats(panel, load, panel.same_group())
    stats[0:STAT, :] = mean
    stats[STAT:, :] = rstd
    silu_shifted(panel, load, mean, rstd, vec[0:1, :], vec[1:2, :], hb)


def middle_kernel(side, count, first_mat, meta, hb, vec, *refs):
    pieces, (middle, stats, hb_two, held, sems) = refs[:count], refs[count:]
    panel = Panel(meta[M_KIND], side, middle.shape[1])
    weights = Weights(meta, pieces, first_mat, held, sems)
    same = panel.same_group()
    pixels = panel.half * side
    for top in range(2):
        middle[top * pixels : (top + 1) * pixels, :] = (
            conv_taps(panel, hb, weights, top, NN, False) + vec[2:3, :]
        )

    def load(i):
        return middle[panel.rows(i), :]

    mean, rstd = norm_stats(panel, load, same)
    stats[0:STAT, :] = mean
    stats[STAT:, :] = rstd
    silu_shifted(panel, load, mean, rstd, vec[3:4, :], vec[4:5, :], hb_two)


def residual_kernel(side, count, first_mat, meta, hb, image, vec, *refs):
    pieces, (residual, stats, normed, held, sems) = refs[:count], refs[count:]
    panel = Panel(meta[M_KIND], side, residual.shape[1])
    weights = Weights(meta, pieces, first_mat, held, sems)
    same = panel.same_group()
    pixels = panel.half * side
    for top in range(2):
        span = slice(top * pixels, (top + 1) * pixels)
        residual[span, :] = (
            image[span, :].astype(F32) + conv_taps(panel, hb, weights, top, NN, False) + vec[5:6, :]
        )

    def load(i):
        return residual[panel.rows(i), :]

    mean, rstd = norm_stats(panel, load, same)
    stats[0:STAT, :] = mean
    stats[STAT:, :] = rstd
    columns = panel.columns()
    means = [panel.spread(mean, top) for top in range(2)]
    rstds = [panel.spread(rstd, top) for top in range(2)]

    def step(i, top, carry):
        normal = jnp.where(panel.mask(columns, i), (load(i) - means[top]) * rstds[top], 0.0)
        normed[panel.rows(i), :] = (normal * vec[6:7, :] + vec[7:8, :]).astype(B16)
        return carry

    panel.loop(step, 0)


def norm_back(panel, load, stats, gain, same, gradient, emit, extra):
    columns = panel.columns()
    means = [panel.spread(stats[0:STAT], top) for top in range(2)]
    rstds = [panel.spread(stats[STAT:], top) for top in range(2)]

    def normal_of(i, top, mask):
        return jnp.where(mask, (load(i) - means[top]) * rstds[top], 0.0)

    def add(i, top, carry):
        mask = panel.mask(columns, i)
        normal = normal_of(i, top, mask)
        grad = gradient(i, mask, normal)
        return carry[0] + grad, carry[1] + grad * normal

    upper, lower = panel.loop(add, (panel.zero(), panel.zero()))
    plain = panel.quadrants(upper[0], lower[0])
    cross = panel.quadrants(upper[1], lower[1])
    plain_mean = panel.reduced(plain * gain, same)
    cross_mean = panel.reduced(cross * gain, same)
    plains = [panel.spread(plain_mean, top) for top in range(2)]
    crosses = [panel.spread(cross_mean, top) for top in range(2)]

    def finish(i, top, carry):
        mask = panel.mask(columns, i)
        normal = normal_of(i, top, mask)
        scaled = gradient(i, mask, None) * gain
        value = rstds[top] * (scaled - plains[top] - normal * crosses[top])
        return emit(i, top, jnp.where(mask, value, 0.0), carry, columns)

    found = panel.loop(finish, extra)
    grad_gain = jnp.sum(cross, axis=0, keepdims=True)
    grad_shift = jnp.sum(plain, axis=0, keepdims=True)
    return grad_gain, grad_shift, found


def attention_kernel(side, count, first_mat, meta, residual, stats, normed, out_grad, vec, *refs):
    pieces, refs = refs[:count], refs[count:]
    (block_out, d_residual, d_middle, eb, keep, send, rows_out) = refs[:7]
    (held, sems, queries, keys, values, soft, soft_low, d_scores, attended, d_attended,
     d_queries, d_keys, d_values, gout, d_normed, staged) = refs[7:]
    channels = residual.shape[1]
    panel = Panel(meta[M_KIND], side, channels)
    weights = Weights(meta, pieces, first_mat, held, sems)
    same = panel.same_group()
    total = side * side
    block = total // 4
    inv_root = 1.0 / math.sqrt(channels)
    shift = side.bit_length() - 1

    def labels(pixel):
        i, j = pixel >> shift, pixel & (side - 1)
        quarter = jnp.where(i >= panel.half, 2, 0) + jnp.where(j >= panel.half, 1, 0)
        four = jnp.where(panel.kind == 2, 1, 0)
        lab = quarter * four
        return jnp.where((i < panel.limit) & (j < panel.limit), lab, -1)

    key_labels = labels(lax.broadcasted_iota(jnp.int32, (1, total), 1))

    def block_labels(n):
        return labels(lax.broadcasted_iota(jnp.int32, (block, 1), 0) + n * block)

    for m in range(4):
        weights.wait(m)
    for n in range(4):
        span = slice(n * block, (n + 1) * block)
        rows = normed[span, :]
        queries[span, :] = (dot(rows, held[0], NN) + vec[8:9, :]).astype(B16)
        keys[span, :] = dot(rows, held[1], NN).astype(B16)
        values[span, :] = (dot(rows, held[2], NN) + vec[9:10, :]).astype(B16)
    gout_sum = jnp.zeros((1, channels), F32)
    for n in range(4):
        span = slice(n * block, (n + 1) * block)
        lab = block_labels(n)
        scores = dot(queries[span, :], keys[...], NT) * inv_root
        scores = jnp.where((lab == key_labels) & (key_labels >= 0), scores, MASK_FILL)
        top = jnp.max(scores, axis=-1, keepdims=True)
        grown = jnp.exp(scores - top)
        chances = grown / jnp.sum(grown, axis=-1, keepdims=True)
        soft[span, :] = chances
        soft_low[span, :] = chances.astype(B16)
        attended[span, :] = dot(soft_low[span, :], values[...], NN).astype(B16)
        projected = dot(attended[span, :], held[3], NN) + vec[10:11, :]
        valid = lab >= 0
        block_out[span, :] = jnp.where(valid, residual[span, :] + projected, 0.0).astype(B16)
        grad = jnp.where(valid, out_grad[span, :].astype(F32), 0.0)
        gout_sum = gout_sum + jnp.sum(grad, axis=0, keepdims=True)
        gout[span, :] = grad.astype(B16)
        d_attended[span, :] = dot(gout[span, :], held[3], NT).astype(B16)
    for n in range(4):
        span = slice(n * block, (n + 1) * block)
        d_soft = dot(d_attended[span, :], values[...], NT)
        chances = soft[span, :]
        delta = jnp.sum(d_soft * chances, axis=-1, keepdims=True)
        d_scores[span, :] = (chances * (d_soft - delta)).astype(B16)
        d_queries[span, :] = (dot(d_scores[span, :], keys[...], NN) * inv_root).astype(B16)
    d_keys[...] = (dot(d_scores[...], queries[...], TN) * inv_root).astype(B16)
    d_values[...] = dot(soft_low[...], d_attended[...], TN).astype(B16)
    pairs = ((normed, d_queries), (normed, d_keys), (normed, d_values), (attended, gout))
    for m, (left, right) in enumerate(pairs):
        staged[...] = dot(left[...], right[...], TN)
        store_parts(meta, staged, keep, send, m)
    for n in range(4):
        span = slice(n * block, (n + 1) * block)
        d_normed[span, :] = (
            dot(d_queries[span, :], held[0], NT)
            + dot(d_keys[span, :], held[1], NT)
            + dot(d_values[span, :], held[2], NT)
        )

    def load(i):
        return residual[panel.rows(i), :]

    def gradient(i, mask, normal):
        return jnp.where(mask, d_normed[panel.rows(i), :], 0.0)

    def emit(i, top, value, carry, columns):
        place = panel.rows(i)
        full = gout[place, :].astype(F32) + value
        d_residual[place, :] = full
        low = full.astype(B16)
        d_middle[place, :] = low
        row = low.astype(F32)
        store_shifted(panel, eb, i, top, row, columns)
        return (
            carry[0] + row,
            carry[1] + d_queries[place, :].astype(F32),
            carry[2] + d_values[place, :].astype(F32),
        )

    zero = panel.zero()
    grad_gain, grad_shift, found = norm_back(
        panel, load, stats, vec[6:7, :], same, gradient, emit, (zero, zero, zero)
    )
    store_edges(panel, eb)
    sums = [jnp.sum(found[0][k] + found[1][k], axis=0, keepdims=True) for k in range(3)]
    rows_out[0:1, :] = sums[0]
    rows_out[1:2, :] = grad_gain
    rows_out[2:3, :] = grad_shift
    rows_out[3:4, :] = sums[1]
    rows_out[4:5, :] = sums[2]
    rows_out[5:6, :] = gout_sum
    rows_out[6:8, :] = jnp.zeros((2, channels), F32)


def store_parts(meta, staged, keep, send, m):
    block = keep.shape[2]
    for k in range(4):
        keep[k, m] = staged[pl.ds(pl.multiple_of(meta[M_KEEP + k], block), block), :].astype(B16)
        send[k, m] = staged[pl.ds(pl.multiple_of(meta[M_SEND + k], block), block), :].astype(B16)


def tap_kernel(side, meta, hb, grad, keep, send, staged):
    pixels = side * side // 2
    tap = pl.program_id(0)
    start = pl.multiple_of((tap // 3) * side, side)
    col = tap % 3
    staged[...] = dot(hb[col, 0, pl.ds(start, pixels), :], grad[0:pixels, :], TN) + dot(
        hb[col, 1, pl.ds(start, pixels), :], grad[pixels:, :], TN
    )
    store_parts(meta, staged, keep, send, 0)


def back_kernel(side, last, count, first_mat, meta, eb, source, stats, vec, *refs):
    if last:
        d_residual, pieces, refs = refs[0], refs[1 : 1 + count], refs[1 + count :]
        out, rows_out, held, sems, slope = refs
        first = 0
    else:
        pieces, refs = refs[:count], refs[count:]
        out, eb_out, rows_out, held, sems, slope = refs
        first = 3
    panel = Panel(meta[M_KIND], side, source.shape[1])
    weights = Weights(meta, pieces, first_mat, held, sems)
    same = panel.same_group()
    gain, shift = vec[first : first + 1, :], vec[first + 1 : first + 2, :]
    pixels = panel.half * side
    for top in range(2):
        slope[top * pixels : (top + 1) * pixels, :] = conv_taps(panel, eb, weights, top, NT, True)

    def load(i):
        return source[panel.rows(i), :].astype(F32)

    def gradient(i, mask, normal):
        place = panel.rows(i)
        if normal is None:
            return slope[place, :]
        pre = normal * gain + shift
        sig = 1.0 / (1.0 + jnp.exp(-pre))
        value = jnp.where(mask, slope[place, :] * (sig * (1.0 + pre * (1.0 - sig))), 0.0)
        slope[place, :] = value
        return value

    def emit(i, top, value, carry, columns):
        place = panel.rows(i)
        if last:
            out[place, :] = (d_residual[place, :] + value).astype(B16)
            return carry
        low = value.astype(B16)
        out[place, :] = low
        row = low.astype(F32)
        store_shifted(panel, eb_out, i, top, row, columns)
        return carry + row

    grad_gain, grad_shift, found = norm_back(
        panel, load, stats, gain, same, gradient, emit, 0 if last else panel.zero()
    )
    channels = panel.channels
    rows_out[0:1, :] = grad_gain
    rows_out[1:2, :] = grad_shift
    if last:
        rows_out[2:8, :] = jnp.zeros((6, channels), F32)
    else:
        store_edges(panel, eb_out)
        rows_out[2:3, :] = jnp.sum(found[0] + found[1], axis=0, keepdims=True)
        rows_out[3:8, :] = jnp.zeros((5, channels), F32)


def slot_kernel(sizes, chips, table, *refs):
    groups = len(sizes)
    parts, (mine, send), whole = refs[: groups * chips], refs[groups * chips : -groups], refs[-groups:]
    count, block = mine.shape[0], mine.shape[1]
    for g in range(groups):
        for d in range(chips):
            part = parts[g * chips + d]
            rows = part.shape[0]
            place = pl.ds(pl.multiple_of(table[2 * count + d] * rows, 16), rows)
            whole[g][place, :] = part[...]
    for out, base in ((mine, 0), (send, count)):
        for k in range(count):
            m = table[base + k]

            @pl.when(m < 0)
            def _(out=out, k=k):
                out[k] = jnp.zeros(out.shape[1:], out.dtype)

            low = 0
            for g, size in enumerate(sizes):

                @pl.when((m >= low) & (m < low + size))
                def _(out=out, k=k, g=g, low=low, m=m):
                    out[k] = whole[g][pl.ds(pl.multiple_of((m - low) * block, block), block), :]

                low += size


def adam_kernel(meta, master, first, second, mine, other, new_first, new_second, new_master, grad):
    block = mine.shape[1]
    core = meta[M_CORE]
    grad[pl.ds(pl.multiple_of(core * block, block), block), :] = mine[0].astype(F32)
    grad[pl.ds(pl.multiple_of((1 - core) * block, block), block), :] = other[0].astype(F32)
    results = adam_update(master[0], first[0], second[0], grad[...], LEARN_RATE)
    new_first[0], new_second[0], new_master[0] = results


def on_panel(
    image_in,
    panel_kind,
    owner_slot,
    out_grad,
    master,
    first_moment,
    second_moment,
    vec_master,
    vec_first,
    vec_second,
):
    side, channels = image_in.shape[2], image_in.shape[3]
    imgs = lax.axis_size("imgs")
    chips = imgs // 2
    own, depth = master.shape[0], master.shape[1]
    block = depth // 2
    total = side * side
    group, row = lax.axis_index("imgs"), lax.axis_index("rows")
    core, chip = group % 2, group // 2

    def permutation(target):
        pairs = []
        for i in range(imgs):
            for r in range(4):
                to_i, to_r = target(i, r)
                pairs.append((i * 4 + r, to_i * 4 + to_r))
        return pairs

    to_core = permutation(lambda i, r: (i ^ 1, r))
    to_near = [permutation(lambda i, r, k=k: (i, r ^ k)) for k in range(4)]
    to_first = permutation(lambda i, r: (i, r ^ (1 + i % 2)))
    to_second = permutation(lambda i, r: (i, r ^ (2 - i % 2)))
    to_chip = [permutation(lambda i, r, d=d: ((i + 2 * d) % imgs, r)) for d in range(chips)]
    across_chip = [permutation(lambda i, r, e=e: (i ^ (2 * e), r)) for e in range(chips)]

    def move(value, pairs):
        return lax.ppermute(value, AXES, pairs)

    tie = lax.optimization_barrier
    wide = shaped((total, channels), F32)
    narrow = shaped((total, channels), B16)
    stat = shaped((2 * STAT, channels), F32)
    shifted = shaped((3, 2, (side // 2 + 2) * side, channels), B16)
    vec_rows = shaped((8, channels), F32)
    near_first, near_second = row ^ (1 + core), row ^ (2 - core)
    quarters = [row, near_first, near_second, row ^ 3, row, near_second, near_first, row ^ 3]
    halves = [core] * 4 + [1 - core] * 4
    kind = lax.dynamic_index_in_dim(panel_kind, row, keepdims=False)
    slot_chip, slot_core = owner_slot // (2 * own), (owner_slot // own) % 2
    place = owner_slot % own + jnp.where(slot_core == core, 0, own)
    meta = jnp.stack(
        [kind, core]
        + [q * depth + h * block for q, h in zip(quarters, halves)]
        + [q * depth + core * block for q in (row, near_second, near_first, row ^ 3)]
        + [q * depth + (1 - core) * block for q in (row, near_first, near_second, row ^ 3)]
    ).astype(jnp.int32)
    meta = jnp.concatenate([meta, chip ^ slot_chip, place, place ^ own]).astype(jnp.int32)
    image = lax.all_to_all(image_in, "rows", 0, 0, tiled=True).reshape(total, channels)

    low = shaped((own, block, channels), B16)
    mine, send = call(
        cast_kernel, (low, low), [SSPEC, VSPEC], (VSPEC, VSPEC), [], (meta, master)
    )
    here = jnp.concatenate([mine, move(send, to_core)], axis=0)

    arrived = [here] + [move(here, across_chip[e]) for e in range(1, chips)]
    pieces, tied = [], None
    for e in range(chips):
        part = arrived[e]
        if e > 0:
            part, tied = tie((part, tied))
        if e == 1:
            part, image = tie((part, image))
            hb_one, stats_one = call(
                functools.partial(first_kernel, side),
                (shifted, stat),
                [SSPEC, VSPEC, VSPEC],
                (VSPEC, VSPEC),
                [],
                (meta, image, vec_master),
                moved=5 * total * channels * 2,
            )
        if e == 2:
            part, hb_one = tie((part, hb_one))
        near = move(part, to_first)
        far = move(part, to_second)
        tied = near
        held = [part, near, far, move(near, to_second)]
        pieces += held + [move(piece, to_core) for piece in held]
    count = len(pieces)

    def weight_scratch(n):
        return [pltpu.VMEM((n, channels, channels), B16), pltpu.SemaphoreType.DMA((n, 8))]

    conv_flops = 2 * total * 9 * channels * channels
    conv_bytes = 9 * channels * channels * 2 + 8 * total * channels

    out_grad, pieces[-1] = tie((out_grad, pieces[-1]))
    cotangent = lax.all_to_all(out_grad, "rows", 0, 0, tiled=True).reshape(total, channels)
    middle, stats_two, hb_two = call(
        functools.partial(middle_kernel, side, count, 0),
        (wide, stat, shifted),
        [SSPEC, VSPEC, VSPEC] + [ASPEC] * count,
        (VSPEC,) * 3,
        weight_scratch(9),
        [meta, hb_one, vec_master] + pieces,
        flops=conv_flops,
        moved=conv_bytes,
    )
    residual, stats_three, normed = call(
        functools.partial(residual_kernel, side, count, 9),
        (wide, stat, narrow),
        [SSPEC, VSPEC, VSPEC, VSPEC] + [ASPEC] * count,
        (VSPEC,) * 3,
        weight_scratch(9),
        [meta, hb_two, image, vec_master] + pieces,
        flops=conv_flops,
        moved=conv_bytes,
    )
    parts_of = lambda n: shaped((4, n, block, channels), B16)
    low_scratch = pltpu.VMEM((total, channels), B16)
    (block_out, d_residual, d_middle_two, eb_two, keep_attn, send_attn, rows_attn) = call(
        functools.partial(attention_kernel, side, count, 18),
        (narrow, wide, narrow, shifted, parts_of(4), parts_of(4), vec_rows),
        [SSPEC] + [VSPEC] * 5 + [ASPEC] * count,
        (VSPEC,) * 7,
        weight_scratch(4)
        + [low_scratch] * 3
        + [pltpu.VMEM((total, total), F32)]
        + [pltpu.VMEM((total, total), B16)] * 2
        + [low_scratch] * 6
        + [pltpu.VMEM((total, channels), F32), pltpu.VMEM((channels, channels), F32)],
        [meta, residual, stats_three, normed, cotangent, vec_master] + pieces,
        flops=3 * conv_flops,
        moved=2 * conv_bytes,
    )

    def tap_grads(hb, grad):
        whole = lambda *shape: pl.BlockSpec(shape, lambda t: (0,) * len(shape))
        part = pl.BlockSpec((4, 1, block, channels), lambda t: (0, t, 0, 0))
        return call(
            functools.partial(tap_kernel, side),
            (parts_of(9), parts_of(9)),
            [SSPEC, whole(*hb.shape), whole(*grad.shape)],
            (part, part),
            [pltpu.VMEM((channels, channels), F32)],
            (meta, hb, grad),
            flops=conv_flops,
            moved=conv_bytes,
            grid=(9,),
        )

    def to_rows(value):
        split = value.reshape(4, side // 4, side, channels)
        return lax.all_to_all(split, "rows", 0, 0, tiled=True)

    def added(*terms):
        return sum((v.astype(F32) for v in terms[1:]), terms[0].astype(F32)).astype(B16)

    chip_groups = [list(range(c, imgs, 2)) for c in range(2)]

    def to_pair(keeps, gots):
        both = [added(keep[2:4], got[2:4]) for keep, got in zip(keeps, gots)]
        return both[0] if len(both) == 1 else jnp.concatenate(both, axis=1)

    def to_quarter(keeps, gots, arrived, k):
        both = [keep[k].astype(F32) + got[k].astype(F32) for keep, got in zip(keeps, gots)]
        both = both[0] if len(both) == 1 else jnp.concatenate(both, axis=0)
        return (both + arrived[k].astype(F32)).astype(B16)

    def over_chips(value):
        rows = value.shape[0] * block // chips
        parts = lax.all_to_all(
            value.reshape(chips, rows, channels),
            "imgs",
            0,
            0,
            tiled=True,
            axis_index_groups=chip_groups,
        )
        return added(*[parts[d] for d in range(chips)])

    def whole_sums(part):
        return [part] + [move(part, to_chip[d]) for d in range(1, chips)]

    got_attn = move(send_attn, to_core)
    block_out = to_rows(block_out)
    keep_two, send_two = tap_grads(hb_two, d_middle_two)
    got_two = move(send_two, to_core)
    eb_two, send_two = tie((eb_two, send_two))
    d_middle_one, eb_one, rows_two = call(
        functools.partial(back_kernel, side, False, count, 9),
        (narrow, shifted, vec_rows),
        [SSPEC] + [VSPEC] * 4 + [ASPEC] * count,
        (VSPEC,) * 3,
        weight_scratch(9) + [pltpu.VMEM((total, channels), F32)],
        [meta, eb_two, middle, stats_two, vec_master] + pieces,
        flops=conv_flops,
        moved=conv_bytes,
    )
    got_attn, got_two, d_middle_one, block_out = tie((got_attn, got_two, d_middle_one, block_out))
    keeps_a, gots_a = (keep_two, keep_attn), (got_two, got_attn)
    pair_a, d_middle_one = tie((to_pair(keeps_a, gots_a), d_middle_one))
    arrived_a = move(pair_a, to_first)
    keep_one, send_one = tap_grads(hb_one, d_middle_one)
    got_one = move(send_one, to_core)
    eb_one, send_one = tie((eb_one, send_one))
    d_image, rows_one = call(
        functools.partial(back_kernel, side, True, count, 0),
        (narrow, vec_rows),
        [SSPEC] + [VSPEC] * 5 + [ASPEC] * count,
        (VSPEC,) * 2,
        weight_scratch(9) + [pltpu.VMEM((total, channels), F32)],
        [meta, eb_one, image, stats_one, vec_master, d_residual] + pieces,
        flops=conv_flops,
        moved=conv_bytes,
    )
    vec_grads = jnp.concatenate([rows_one[0:2], rows_two[2:3], rows_two[0:2], rows_attn[0:6]])
    for pairs in [to_core, to_near[1], to_near[2]] + [
        across_chip[e] for e in (1, 2) if e < chips
    ]:
        vec_grads = vec_grads + move(vec_grads, pairs)
    got_one, d_image = tie((got_one, d_image))
    keeps_b, gots_b = (keep_one,), (got_one,)
    pair_b = to_pair(keeps_b, gots_b)
    arrived_b = move(pair_b, to_first)
    arrived_a, pair_b = tie((arrived_a, pair_b))
    quarter_a = move(to_quarter(keeps_a, gots_a, arrived_a, 1), to_second)
    quarter_b = move(to_quarter(keeps_b, gots_b, arrived_b, 1), to_second)
    part_a = over_chips(added(to_quarter(keeps_a, gots_a, arrived_a, 0), quarter_a))
    quarter_b, d_image = tie((quarter_b, d_image))
    part_b = over_chips(added(to_quarter(keeps_b, gots_b, arrived_b, 0), quarter_b))
    input_grad = to_rows(d_image)

    def matrix_of(first_slot):
        slots = first_slot + jnp.arange(own, dtype=jnp.int32)
        placing = owner_slot[None, :] == slots[:, None]
        found = jnp.sum(jnp.where(placing, jnp.arange(owner_slot.shape[0])[None, :] + 1, 0), axis=1)
        return found - 1

    slots_table = jnp.concatenate(
        [
            matrix_of(group * own),
            matrix_of((group ^ 1) * own),
            (chip - jnp.arange(chips)) % chips,
        ]
    )
    all_sums = whole_sums(part_b) + whole_sums(part_a)
    sizes = (9, MATS - 9)
    mine, send = call(
        functools.partial(slot_kernel, sizes, chips),
        (low, low),
        [SSPEC] + [VSPEC] * len(all_sums),
        (VSPEC, VSPEC),
        [pltpu.VMEM((n * block, channels), B16) for n in sizes],
        [slots_table.astype(jnp.int32)] + all_sums,
    )
    other = move(send, to_core)
    deep = pl.BlockSpec((1, depth, channels), lambda t: (t, 0, 0))
    flat = pl.BlockSpec((1, block, channels), lambda t: (t, 0, 0))
    slot_shape = shaped(master.shape, F32)
    new_first, new_second, new_master = call(
        adam_kernel,
        (slot_shape,) * 3,
        [SSPEC, deep, deep, deep, flat, flat],
        (deep,) * 3,
        [pltpu.VMEM((depth, channels), F32)],
        (meta, master, first_moment, second_moment, mine, other),
        moved=6 * own * depth * channels * 4,
        grid=(own,),
    )
    vec_results = adam_update(vec_master, vec_first, vec_second, vec_grads, VEC_RATE)
    return (block_out, input_grad, new_first, new_second, new_master) + vec_results


def on_slice(*args):
    image_in = args[0]
    panels, row_count, col_count, channels = image_in.shape
    rows, imgs = lax.axis_size("rows"), lax.axis_size("imgs")
    chips = imgs // 2
    whole_panels = (
        rows == 4
        and panels == rows
        and row_count * rows == col_count == 32
        and channels == 512
        and args[4].shape[0] == 4
        and imgs == 2 * chips
        and args[2].shape[0] == MATS
        and chips in (1, 2, 4)
    )
    return on_panel(*args) if whole_panels else on_device(*args)


def solution(mesh):
    in_specs = (
        P("imgs", "rows", None, None),
        P("imgs"),
        P(),
        P("imgs", "rows", None, None),
        P("imgs", "rows", None),
        P("imgs", "rows", None),
        P("imgs", "rows", None),
        P(),
        P(),
        P(),
    )
    out_specs = (
        P("imgs", "rows", None, None),
        P("imgs", "rows", None, None),
        P("imgs", "rows", None),
        P("imgs", "rows", None),
        P("imgs", "rows", None),
        P(),
        P(),
        P(),
    )
    return jax.shard_map(
        on_slice, mesh=mesh, in_specs=in_specs, out_specs=out_specs, check_vma=False
    )
```

```python
import functools
import math

import jax
import jax.numpy as jnp
from jax import lax
from jax.experimental import pallas as pl
from jax.experimental.pallas import tpu as pltpu
from jax.sharding import PartitionSpec as P

GROUPS = 32
MATS = 22
STEP = 5


EXACT_PRECISION = lax.Precision.HIGHEST
NORM_EPS = 1e-06
LEARN_RATE = 0.05
VEC_RATE = 0.2
BETA_ONE = 0.5
BETA_TWO = 0.5
ADAM_EPS = 1e-08
WEIGHT_DECAY = 0.01
MASK_FILL = -1000000000.0


def extended(cells, sides, width):
    for axis, dim in sides:
        count = lax.axis_size(axis)
        ends = count - 1
        head = lax.slice_in_dim(cells, 0, width, axis=dim)
        tail = lax.slice_in_dim(cells, cells.shape[dim] - width, cells.shape[dim], axis=dim)
        cells = jnp.concatenate(
            [
                lax.ppermute(tail, axis, [(i, (i + 1) % count) for i in range(ends)]),
                cells,
                lax.ppermute(head, axis, [((i + 1) % count, i) for i in range(ends)]),
            ],
            axis=dim,
        )
    return cells


def panel_ids(kind_list, row_index, col_index, panel_side):
    row_grid = row_index[None, :, None]
    col_grid = col_index[None, None, :]
    kind_grid = kind_list[:, None, None]
    half_side = panel_side // 2
    part_side = 3 * panel_side // 4
    inside = (row_grid >= 0) & (row_grid < panel_side) & (col_grid >= 0) & (col_grid < panel_side)
    quarter = 2 * (row_grid >= half_side).astype(jnp.int32) + (col_grid >= half_side).astype(
        jnp.int32
    )
    zero_grid = jnp.zeros_like(quarter)
    corner = jnp.where((row_grid < part_side) & (col_grid < part_side), zero_grid, zero_grid - 1)
    labels = jnp.where(
        kind_grid == 0,
        zero_grid,
        jnp.where(kind_grid == 1, corner, jnp.where(kind_grid == 2, quarter, zero_grid - 1)),
    )
    return jnp.where(inside & (labels >= 0), labels, -1)


def spread_pix(onehot, per_group):
    return jnp.einsum("prwi,pig->prwg", onehot, per_group, precision=EXACT_PRECISION)


def group_stats(value_rows, onehot, counts):
    panel_count, row_count, col_count, channel_count = value_rows.shape
    grouped = value_rows.reshape(panel_count, row_count, col_count, GROUPS, channel_count // GROUPS)
    first_sums = lax.psum(
        jnp.einsum("prwi,prwgc->pig", onehot, grouped, precision=EXACT_PRECISION), "rows"
    )
    group_mean = first_sums / counts[:, :, None]
    centred = grouped - spread_pix(onehot, group_mean)[..., None]
    square_sums = jnp.einsum(
        "prwi,prwgc->pig", onehot, centred * centred, precision=EXACT_PRECISION
    )
    spread = lax.psum(square_sums, "rows") / counts[:, :, None]
    scale_pix = spread_pix(onehot, lax.rsqrt(spread + NORM_EPS))
    normal_val = (centred * scale_pix[..., None]).reshape(value_rows.shape)
    return (normal_val, scale_pix)


def group_back(gradient, normal_val, scale_pix, gain_row, onehot, counts):
    panel_count, row_count, col_count, channel_count = gradient.shape
    grad_gain = jnp.sum(gradient * normal_val, axis=(0, 1, 2))
    grad_shift = jnp.sum(gradient, axis=(0, 1, 2))
    scaled = (gradient * gain_row).reshape(
        panel_count, row_count, col_count, GROUPS, channel_count // GROUPS
    )
    normal_grp = normal_val.reshape(scaled.shape)
    plain_sums = jnp.einsum("prwi,prwgc->pig", onehot, scaled, precision=EXACT_PRECISION)
    cross_sums = jnp.einsum(
        "prwi,prwgc->pig", onehot, scaled * normal_grp, precision=EXACT_PRECISION
    )
    plain_sums, cross_sums = lax.psum((plain_sums, cross_sums), "rows")
    plain_pix = spread_pix(onehot, plain_sums / counts[:, :, None])
    cross_pix = spread_pix(onehot, cross_sums / counts[:, :, None])
    result = scale_pix[..., None] * (
        scaled - plain_pix[..., None] - normal_grp * cross_pix[..., None]
    )
    return (result.reshape(gradient.shape), grad_gain, grad_shift)


def silu_slope(pre_act):
    sigmoid_val = jax.nn.sigmoid(pre_act)
    return sigmoid_val * (1.0 + pre_act * (1.0 - sigmoid_val))


def conv_forward(hidden, weight_cat, tap_masks):
    panel_count, row_count, col_count, channel_count = hidden.shape
    padded = extended(hidden, (("rows", 1),), 1)
    padded = jnp.pad(padded, ((0, 0), (0, 0), (1, 1), (0, 0)))
    columns = jnp.concatenate(
        [
            padded[
                :,
                tap_index // 3 : tap_index // 3 + row_count,
                tap_index % 3 : tap_index % 3 + col_count,
                :,
            ]
            * tap_masks[tap_index]
            for tap_index in range(9)
        ],
        axis=-1,
    )
    columns = columns.reshape(-1, 9 * channel_count)
    result = jnp.dot(columns, weight_cat, preferred_element_type=jnp.float32)
    return (result.reshape(hidden.shape), columns)


def conv_backward(gradient, columns, weight_cat, tap_masks):
    panel_count, row_count, col_count, channel_count = gradient.shape
    grad_flat = gradient.reshape(-1, channel_count)
    weight_grad = jnp.einsum("mk,mc->kc", columns, grad_flat, preferred_element_type=jnp.float32)
    col_grads = jnp.einsum("mc,kc->mk", grad_flat, weight_cat, preferred_element_type=jnp.float32)
    col_grads = col_grads.reshape(panel_count, row_count, col_count, 9, channel_count)
    padded_grad = jnp.zeros((panel_count, row_count + 2, col_count + 2, channel_count), jnp.float32)
    for tap_index in range(9):
        tap_row = tap_index // 3
        tap_col = tap_index % 3
        padded_grad = padded_grad.at[
            :, tap_row : tap_row + row_count, tap_col : tap_col + col_count, :
        ].add(col_grads[:, :, :, tap_index, :] * tap_masks[tap_index])
    padded_grad = padded_grad[:, :, 1 : col_count + 1, :]
    edge_rows = jnp.concatenate(
        [padded_grad[:, 0:1], padded_grad[:, row_count + 1 : row_count + 2]], axis=1
    )
    arrived = extended(edge_rows.astype(jnp.bfloat16), (("rows", 1),), 1).astype(edge_rows.dtype)
    inner = padded_grad[:, 1 : row_count + 1]
    inner = inner.at[:, 0].add(arrived[:, 0])
    inner = inner.at[:, row_count - 1].add(arrived[:, 3])
    return (inner, weight_grad)


def adam_update(weight, first_old, second, gradient, step_rate):
    new_first = BETA_ONE * first_old + (1.0 - BETA_ONE) * gradient
    new_second = BETA_TWO * second + (1.0 - BETA_TWO) * gradient * gradient
    first_hat = new_first / (1.0 - BETA_ONE**STEP)
    second_hat = new_second / (1.0 - BETA_TWO**STEP)
    new_weight = weight - step_rate * (
        first_hat / (jnp.sqrt(second_hat) + ADAM_EPS) + WEIGHT_DECAY * weight
    )
    return (new_first, new_second, new_weight)


def on_device(
    image_in,
    panel_kind,
    owner_slot,
    out_grad,
    master,
    first_moment,
    second_moment,
    vec_master,
    vec_first,
    vec_second,
):
    panel_count, row_count, col_count, channel_count = image_in.shape
    height_all = row_count * lax.axis_size("rows")
    group_width = channel_count // GROUPS
    pixel_count = panel_count * row_count * col_count
    local_pix = row_count * col_count
    slot_total = master.shape[0] * lax.axis_size("imgs")
    inv_root = 1.0 / math.sqrt(channel_count)
    placing = owner_slot[None, :] == jnp.arange(slot_total, dtype=jnp.int32)[:, None]
    slot_weights = lax.all_gather(master.astype(jnp.bfloat16), "imgs", axis=0, tiled=True)
    picked = jnp.einsum(
        "sm,sij->mij",
        placing.astype(jnp.bfloat16),
        slot_weights,
        preferred_element_type=jnp.float32,
    ).astype(jnp.bfloat16)
    weights = lax.all_gather(picked, "rows", axis=1, tiled=True)
    conv_first = weights[0:9].reshape(9 * channel_count, channel_count)
    conv_second = weights[9:18].reshape(9 * channel_count, channel_count)
    attn_in = jnp.concatenate([weights[18], weights[19], weights[20]], axis=1)
    attn_out = weights[21]
    first_row = lax.axis_index("rows") * row_count
    col_range = jnp.arange(col_count, dtype=jnp.int32)
    labels = panel_ids(
        panel_kind, first_row + jnp.arange(row_count, dtype=jnp.int32), col_range, height_all
    )
    outer_labels = panel_ids(
        panel_kind,
        first_row + jnp.arange(-1, row_count + 1, dtype=jnp.int32),
        jnp.arange(-1, col_count + 1, dtype=jnp.int32),
        height_all,
    )
    whole_labels = panel_ids(
        panel_kind, jnp.arange(height_all, dtype=jnp.int32), col_range, height_all
    )
    label_range = jnp.arange(4, dtype=jnp.int32)
    onehot = (labels[..., None] == label_range).astype(jnp.float32)
    validity = (labels >= 0).astype(jnp.float32)[..., None]
    counts = jnp.maximum(
        jnp.sum((whole_labels[..., None] == label_range).astype(jnp.float32), axis=(1, 2))
        * group_width,
        1.0,
    )
    tap_masks = [
        (
            (
                outer_labels[
                    :,
                    tap_index // 3 : tap_index // 3 + row_count,
                    tap_index % 3 : tap_index % 3 + col_count,
                ]
                == labels
            )
            & (labels >= 0)
        ).astype(jnp.bfloat16)[..., None]
        for tap_index in range(9)
    ]
    image_vals = image_in.astype(jnp.float32)
    normal_one, scale_one = group_stats(image_vals, onehot, counts)
    pre_one = normal_one * vec_master[0] + vec_master[1]
    hidden_one = jax.nn.silu(pre_one).astype(jnp.bfloat16)
    conv_out, columns_one = conv_forward(hidden_one, conv_first, tap_masks)
    middle = conv_out + vec_master[2]
    normal_two, scale_two = group_stats(middle, onehot, counts)
    pre_two = normal_two * vec_master[3] + vec_master[4]
    hidden_two = jax.nn.silu(pre_two).astype(jnp.bfloat16)
    conv_out_two, columns_two = conv_forward(hidden_two, conv_second, tap_masks)
    residual = image_vals + conv_out_two + vec_master[5]
    normal_three, scale_three = group_stats(residual, onehot, counts)
    normed = (
        (normal_three * vec_master[6] + vec_master[7])
        .astype(jnp.bfloat16)
        .reshape(pixel_count, channel_count)
    )
    qkv_vals = jnp.dot(normed, attn_in, preferred_element_type=jnp.float32)
    query_matrix = (
        (qkv_vals[:, :channel_count] + vec_master[8])
        .astype(jnp.bfloat16)
        .reshape(panel_count, local_pix, channel_count)
    )
    key_loc = (
        qkv_vals[:, channel_count : 2 * channel_count]
        .astype(jnp.bfloat16)
        .reshape(panel_count, row_count, col_count, channel_count)
    )
    values_loc = (
        (qkv_vals[:, 2 * channel_count :] + vec_master[9])
        .astype(jnp.bfloat16)
        .reshape(panel_count, row_count, col_count, channel_count)
    )
    keys_all, values_all = (
        lax.all_gather(key_loc, "rows", axis=1, tiled=True),
        lax.all_gather(values_loc, "rows", axis=1, tiled=True),
    )
    keys_all = keys_all.reshape(panel_count, height_all * col_count, channel_count)
    values_all = values_all.reshape(panel_count, height_all * col_count, channel_count)
    query_labels = labels.reshape(panel_count, -1)
    key_labels = whole_labels.reshape(panel_count, -1)
    same_image = (query_labels[:, :, None] == key_labels[:, None, :]) & (
        key_labels[:, None, :] >= 0
    )
    attention_scores = (
        jnp.einsum("pqc,pkc->pqk", query_matrix, keys_all, preferred_element_type=jnp.float32)
        * inv_root
    )
    attention_scores = jnp.where(same_image, attention_scores, MASK_FILL)
    row_max = jnp.max(attention_scores, axis=-1, keepdims=True)
    exp_scores = jnp.exp(attention_scores - row_max)
    exp_total = jnp.sum(exp_scores, axis=-1, keepdims=True)
    softmax_weights = exp_scores / exp_total
    log_total = row_max[..., 0] + jnp.log(exp_total[..., 0])
    attended_values = jnp.einsum(
        "pqk,pkc->pqc",
        softmax_weights.astype(jnp.bfloat16),
        values_all,
        preferred_element_type=jnp.float32,
    ).astype(jnp.bfloat16)
    attended_values = attended_values.reshape(pixel_count, channel_count)
    projected = (
        jnp.dot(attended_values, attn_out, preferred_element_type=jnp.float32) + vec_master[10]
    ).reshape(image_in.shape)
    block_out = ((residual + projected) * validity).astype(jnp.bfloat16)
    grad_out = out_grad.astype(jnp.float32) * validity
    grad_flat = grad_out.astype(jnp.bfloat16).reshape(pixel_count, channel_count)
    grad_proj = jnp.einsum(
        "mc,md->cd", attended_values, grad_flat, preferred_element_type=jnp.float32
    )
    bias_proj = jnp.sum(grad_out, axis=(0, 1, 2))
    d_attended = jnp.einsum(
        "md,cd->mc", grad_flat, attn_out, preferred_element_type=jnp.float32
    ).astype(jnp.bfloat16)
    d_attended = d_attended.reshape(panel_count, local_pix, channel_count)
    again_scores = (
        jnp.einsum("pqc,pkc->pqk", query_matrix, keys_all, preferred_element_type=jnp.float32)
        * inv_root
    )
    again_scores = jnp.where(same_image, again_scores, MASK_FILL)
    again_soft = jnp.exp(again_scores - log_total[..., None])
    d_soft = jnp.einsum("pqc,pkc->pqk", d_attended, values_all, preferred_element_type=jnp.float32)
    row_delta = jnp.sum(d_soft * again_soft, axis=-1)
    d_scores = (again_soft * (d_soft - row_delta[..., None])).astype(jnp.bfloat16)
    d_queries = (
        jnp.einsum("pqk,pkc->pqc", d_scores, keys_all, preferred_element_type=jnp.float32)
        * inv_root
    ).astype(jnp.bfloat16)
    d_key_all = (
        jnp.einsum("pqk,pqc->pkc", d_scores, query_matrix, preferred_element_type=jnp.float32)
        * inv_root
    )
    d_value_all = jnp.einsum(
        "pqk,pqc->pkc",
        again_soft.astype(jnp.bfloat16),
        d_attended,
        preferred_element_type=jnp.float32,
    )
    d_key_all = d_key_all.reshape(panel_count, height_all, col_count, channel_count)
    d_value_all = d_value_all.reshape(panel_count, height_all, col_count, channel_count)
    d_keys, d_values = (
        lax.psum_scatter(
            d_key_all.astype(jnp.bfloat16), "rows", scatter_dimension=1, tiled=True
        ).astype(jnp.float32),
        lax.psum_scatter(
            d_value_all.astype(jnp.bfloat16), "rows", scatter_dimension=1, tiled=True
        ).astype(jnp.float32),
    )
    d_keys = d_keys.reshape(pixel_count, channel_count).astype(jnp.bfloat16)
    d_values = d_values.reshape(pixel_count, channel_count).astype(jnp.bfloat16)
    d_queries = d_queries.reshape(pixel_count, channel_count)
    d_qkv = jnp.concatenate([d_queries, d_keys, d_values], axis=1)
    grad_qkv = jnp.einsum("mc,md->cd", normed, d_qkv, preferred_element_type=jnp.float32)
    bias_query = jnp.sum(d_queries, axis=0, dtype=jnp.float32)
    bias_value = jnp.sum(d_values, axis=0, dtype=jnp.float32)
    d_normed = jnp.einsum("md,cd->mc", d_qkv, attn_in, preferred_element_type=jnp.float32).reshape(
        image_in.shape
    )
    d_three, gain_three, shift_three = group_back(
        d_normed, normal_three, scale_three, vec_master[6], onehot, counts
    )
    d_residual = grad_out + d_three
    d_middle_two = d_residual.astype(jnp.bfloat16)
    bias_two = jnp.sum(d_middle_two, axis=(0, 1, 2), dtype=jnp.float32)
    d_hidden_two, grad_conv_two = conv_backward(d_middle_two, columns_two, conv_second, tap_masks)
    d_middle, gain_two, shift_two = group_back(
        d_hidden_two * silu_slope(pre_two), normal_two, scale_two, vec_master[3], onehot, counts
    )
    d_middle_one = d_middle.astype(jnp.bfloat16)
    bias_one = jnp.sum(d_middle_one, axis=(0, 1, 2), dtype=jnp.float32)
    d_hidden_one, grad_conv_one = conv_backward(d_middle_one, columns_one, conv_first, tap_masks)
    d_input, gain_one, shift_one = group_back(
        d_hidden_one * silu_slope(pre_one), normal_one, scale_one, vec_master[0], onehot, counts
    )
    input_grad = (d_residual + d_input).astype(jnp.bfloat16)
    vec_grads = jnp.stack(
        [
            gain_one,
            shift_one,
            bias_one,
            gain_two,
            shift_two,
            bias_two,
            gain_three,
            shift_three,
            bias_query,
            bias_value,
            bias_proj,
        ]
    )
    vec_grads = lax.psum(vec_grads, ("imgs", "rows"))
    mat_grads = jnp.concatenate(
        [
            grad_conv_one.reshape(9, channel_count, channel_count),
            grad_conv_two.reshape(9, channel_count, channel_count),
            grad_qkv[:, :channel_count][None],
            grad_qkv[:, channel_count : 2 * channel_count][None],
            grad_qkv[:, 2 * channel_count :][None],
            grad_proj[None],
        ],
        axis=0,
    )
    row_grads = lax.psum_scatter(
        mat_grads.astype(jnp.bfloat16), "rows", scatter_dimension=1, tiled=True
    ).astype(jnp.float32)
    slot_terms = jnp.einsum(
        "sm,mij->sij", placing.astype(jnp.float32), row_grads, precision=EXACT_PRECISION
    )
    owned_grads = lax.psum_scatter(
        slot_terms.astype(jnp.bfloat16), "imgs", scatter_dimension=0, tiled=True
    ).astype(jnp.float32)
    new_first, new_second, new_master = adam_update(
        master, first_moment, second_moment, owned_grads, LEARN_RATE
    )
    vec_first_new, vec_second_new, vec_master_new = adam_update(
        vec_master, vec_first, vec_second, vec_grads, VEC_RATE
    )
    return (
        block_out,
        input_grad,
        new_first,
        new_second,
        new_master,
        vec_first_new,
        vec_second_new,
        vec_master_new,
    )


F32 = jnp.float32
B16 = jnp.bfloat16
AXES = ("imgs", "rows")
NN = (((1,), (0,)), ((), ()))
NT = (((1,), (1,)), ((), ()))
TN = (((0,), (0,)), ((), ()))
VSPEC = pl.BlockSpec(memory_space=pltpu.VMEM)
SSPEC = pl.BlockSpec(memory_space=pltpu.SMEM)
ASPEC = pl.BlockSpec(memory_space=pl.ANY)
STAT = 16
M_KIND, M_CORE, M_OFF, M_KEEP, M_SEND, M_FROM = 0, 1, 2, 10, 14, 18
LANES = 128


def dot(left, right, dims):
    return lax.dot_general(left, right, dims, preferred_element_type=F32)


def shaped(shape, dtype):
    return jax.ShapeDtypeStruct(shape, dtype)


def call(body, outs, in_specs, out_specs, scratch, args, flops=0, moved=0, grid=None, vmem=58):
    extra = {} if grid is None else {"grid": grid}
    return pl.pallas_call(
        body,
        out_shape=outs,
        in_specs=in_specs,
        out_specs=out_specs,
        scratch_shapes=scratch,
        compiler_params=pltpu.CompilerParams(vmem_limit_bytes=vmem * 2**20),
        cost_estimate=pl.CostEstimate(flops=flops, bytes_accessed=moved, transcendentals=0),
        **extra,
    )(*args)


class Panel:
    def __init__(self, kind, side, channels):
        self.kind, self.side, self.channels = kind, side, channels
        self.half = side // 2
        self.width = channels // GROUPS
        part = 3 * side // 4
        self.limit = jnp.where(kind == 3, 0, jnp.where(kind == 1, part, side))
        pixels = jnp.where(
            kind == 2, self.half * self.half, jnp.where(kind == 1, part * part, side * side)
        )
        count = jnp.where(kind == 3, 1, pixels * self.width)
        self.inverse = 1.0 / count.astype(F32)
        self.four = jnp.where(kind == 2, 1.0, 0.0).astype(F32)
        self.cut = jnp.where(kind == 2, self.half, -1)

    def columns(self):
        return lax.broadcasted_iota(jnp.int32, (self.side, self.channels), 0)

    def mask(self, columns, i):
        return columns < jnp.where(i < self.limit, self.limit, 0)

    def rows(self, i):
        return pl.ds(pl.multiple_of(i * self.side, self.side), self.side)

    def same_group(self):
        shift = self.width.bit_length() - 1
        shape = (LANES, LANES)
        left = lax.broadcasted_iota(jnp.int32, shape, 0) >> shift
        right = lax.broadcasted_iota(jnp.int32, shape, 1) >> shift
        return jnp.where(left == right, 1.0, 0.0).astype(B16)

    def loop(self, body, init, after=None):
        found = []
        for top in range(2):
            found.append(
                lax.fori_loop(
                    0,
                    self.half,
                    lambda t, carry, top=top: body(top * self.half + t, top, carry),
                    init,
                    unroll=2,
                )
            )
            if after is not None:
                after(top)
        return found

    def spread(self, stat, top):
        shape = (self.half, self.channels)
        return jnp.concatenate(
            [
                jnp.broadcast_to(stat[2 * top : 2 * top + 1], shape),
                jnp.broadcast_to(stat[2 * top + 1 : 2 * top + 2], shape),
            ],
            axis=0,
        )

    def quadrants(self, upper, lower):
        parts = []
        for acc in (upper, lower):
            for left in range(2):
                parts.append(
                    jnp.sum(acc[left * self.half : (left + 1) * self.half], axis=0, keepdims=True)
                )
        parts.append(jnp.zeros((STAT - 4, self.channels), F32))
        return jnp.concatenate(parts, axis=0)

    def over_images(self, sums):
        total = jnp.sum(sums, axis=0, keepdims=True)
        return sums * self.four + total * (1.0 - self.four)

    def over_groups(self, sums, same):
        high = sums.astype(B16)
        rest = sums - high.astype(F32)
        middle = rest.astype(B16)
        low = (rest - middle.astype(F32)).astype(B16)
        cuts = range(0, self.channels, LANES)
        stacked = jnp.concatenate(
            [part[:, c : c + LANES] for part in (high, middle, low) for c in cuts], axis=0
        )
        found = dot(stacked, same, NN)
        third = len(cuts) * STAT
        found = found[0:third] + found[third : 2 * third] + found[2 * third :]
        return jnp.concatenate(
            [found[k * STAT : (k + 1) * STAT] for k in range(len(cuts))], axis=1
        )

    def reduced(self, sums, same):
        return self.over_groups(self.over_images(sums), same) * self.inverse

    def zero(self):
        return jnp.zeros((self.side, self.channels), F32)


def norm_stats(panel, load, same):
    columns = panel.columns()

    def add_plain(i, top, carry):
        return carry + jnp.where(panel.mask(columns, i), load(i), 0.0)

    mean = panel.reduced(panel.quadrants(*panel.loop(add_plain, panel.zero())), same)
    means = [panel.spread(mean, top) for top in range(2)]

    def add_square(i, top, carry):
        centred = load(i) - means[top]
        return carry + jnp.where(panel.mask(columns, i), centred * centred, 0.0)

    spread = panel.reduced(panel.quadrants(*panel.loop(add_square, panel.zero())), same)
    return mean, lax.rsqrt(spread + NORM_EPS)


def store_shifted(panel, hb, i, top, row, columns):
    side = panel.side
    place = pl.ds(pl.multiple_of((i - top * panel.half + 1) * side, side), side)
    before = pltpu.roll(row, 1, 0)
    after = pltpu.roll(row, side - 1, 0)
    from_left = (columns != 0) & (columns != panel.cut)
    from_right = (columns != side - 1) & (columns != panel.cut - 1)
    hb[0, top, place, :] = jnp.where(from_left, before, 0.0).astype(B16)
    hb[1, top, place, :] = row.astype(B16)
    hb[2, top, place, :] = jnp.where(from_right, after, 0.0).astype(B16)


def store_edges(panel, hb):
    side, half = panel.side, panel.half
    joined = 1.0 - panel.four
    blank = jnp.zeros((side, panel.channels), B16)
    for b in range(3):
        hb[b, 0, 0:side, :] = blank
        hb[b, 1, (half + 1) * side : (half + 2) * side, :] = blank
        upper = hb[b, 0, half * side : (half + 1) * side, :].astype(F32) * joined
        lower = hb[b, 1, side : 2 * side, :].astype(F32) * joined
        hb[b, 1, 0:side, :] = upper.astype(B16)
        hb[b, 0, (half + 1) * side : (half + 2) * side, :] = lower.astype(B16)


def silu_row(panel, load, columns, mean, rstd, gain, shift, i):
    mask = panel.mask(columns, i)
    normal = jnp.where(mask, (load(i) - mean) * rstd, 0.0)
    pre = normal * gain + shift
    half = 0.5 * pre
    return jnp.where(mask, half + half * jnp.tanh(half), 0.0)


def silu_shifted(panel, load, mean, rstd, gain, shift, hb, sender, out):
    columns = panel.columns()
    means = [panel.spread(mean, top) for top in range(2)]
    rstds = [panel.spread(rstd, top) for top in range(2)]

    def step(i, top, carry):
        row = silu_row(panel, load, columns, means[top], rstds[top], gain, shift, i)
        store_shifted(panel, hb, i, top, row, columns)
        return carry

    def after(top):
        if top == 1:
            store_edges(panel, hb)
        if sender is not None:
            send_shifted(panel, sender, hb, out, top)

    panel.loop(step, 0, after)


PIECES = 8
SENDS = 32


class Sender:
    def __init__(self, sems):
        self.sems, self.copies = sems, []

    def send(self, source, target):
        copy = pltpu.make_async_copy(source, target, self.sems.at[len(self.copies)])
        copy.start()
        self.copies.append(copy)

    def finish(self):
        for copy in self.copies:
            copy.wait()


def fetch(source, target, sem):
    copy = pltpu.make_async_copy(source, target, sem)
    copy.start()
    return copy


def send_shifted(panel, sender, hb, out, top):
    side, rows = panel.side, panel.half * panel.side
    for b in range(3):
        if top == 0:
            sender.send(hb.at[b, 0, pl.ds(side, rows), :], out.at[b, 0, pl.ds(side, rows), :])
        else:
            for start in (0, rows + side):
                place = pl.ds(start, side)
                sender.send(hb.at[b, 0, place, :], out.at[b, 0, place, :])
            sender.send(hb.at[b, 1], out.at[b, 1])


def send_half(panel, sender, source, out, top):
    rows = panel.half * panel.side
    place = pl.ds(top * rows, rows)
    sender.send(source.at[place, :], out.at[place, :])


def weight_copies(meta, pieces, first, held, sems, m):
    block = pieces[0].shape[1]
    slot = meta[M_FROM + MATS + first + m]
    other_slot = meta[M_FROM + 2 * MATS + first + m]
    copies = []
    for t in range(8):
        source = pieces[t].at[slot if t < 4 else other_slot]
        place = pl.ds(pl.multiple_of(meta[M_OFF + t], block), block)
        copies.append(pltpu.make_async_copy(source, held.at[m, place, :], sems.at[m, t]))
    return copies


class Whole:
    def __init__(self, matrices, held, sems):
        self.matrices, self.held, self.sems, self.copies = matrices, held, sems, {}

    def start(self, order):
        for m in order:
            self.copies[m] = fetch(self.matrices.at[m], self.held.at[m], self.sems.at[m, 0])

    def wait(self, m):
        self.copies[m].wait()


class Weights:
    def __init__(self, meta, pieces, first, held, sems):
        self.meta, self.pieces, self.first, self.held, self.sems = meta, pieces, first, held, sems

    def start(self, order):
        for m in order:
            for e in range(len(self.pieces) // PIECES):

                @pl.when(self.meta[M_FROM + self.first + m] == e)
                def _(e=e, m=m):
                    group = self.pieces[PIECES * e : PIECES * (e + 1)]
                    for copy in weight_copies(
                        self.meta, group, self.first, self.held, self.sems, m
                    ):
                        copy.start()

    def wait(self, m):
        block = self.pieces[0].shape[1]
        for t in range(PIECES):
            target = self.held.at[m, pl.ds(0, block), :]
            pltpu.make_async_copy(self.pieces[t].at[0], target, self.sems.at[m, t]).wait()


def start_taps(weights, shifted, hb, sems, flip):
    loads = []
    order = [tap for tap, _, _ in tap_order(flip)]
    for col in range(3):
        if shifted is not None:
            loads.append(fetch(shifted.at[col], hb.at[col], sems.at[col]))
        weights.start(order[3 * col : 3 * col + 3])
    return loads


def tap_order(flip):
    order = []
    for col in range(3):
        for row in range(3):
            a, b = (2 - row, 2 - col) if flip else (row, col)
            order.append((3 * a + b, row, col))
    return order


def conv_taps(panel, hb, loads, weights, top, dims, flip):
    side, pixels = panel.side, panel.half * panel.side
    total = jnp.zeros((pixels, panel.channels), F32)
    for tap, row, col in tap_order(flip):
        if top == 0:
            if row == 0 and loads is not None:
                loads[col].wait()
            weights.wait(tap)
        total = total + dot(
            hb[col, top, row * side : row * side + pixels, :], weights.held[tap], dims
        )
    return total


def cast_kernel(meta, master, mine, send):
    block = mine.shape[1]
    for out, half in ((mine, meta[M_CORE]), (send, 1 - meta[M_CORE])):
        place = pl.ds(pl.multiple_of(half * block, block), block)
        out[...] = master[:, place, :].astype(B16)


def first_kernel(side, meta, image, vec, hb_out, stats, hb, out_sems):
    panel = Panel(meta[M_KIND], side, image.shape[1])
    sender = Sender(out_sems)

    def load(i):
        return image[panel.rows(i), :].astype(F32)

    mean, rstd = norm_stats(panel, load, panel.same_group())
    stats[0:STAT, :] = mean
    stats[STAT:, :] = rstd
    silu_shifted(panel, load, mean, rstd, vec[0:1, :], vec[1:2, :], hb, sender, hb_out)
    sender.finish()


def norm_back(panel, load, stats, gain, same, gradient, emit, extra, after):
    columns = panel.columns()
    means = [panel.spread(stats[0:STAT], top) for top in range(2)]
    rstds = [panel.spread(stats[STAT:], top) for top in range(2)]

    def normal_of(i, top, mask):
        return jnp.where(mask, (load(i) - means[top]) * rstds[top], 0.0)

    def add(i, top, carry):
        mask = panel.mask(columns, i)
        normal = normal_of(i, top, mask)
        grad = gradient(i, mask, normal)
        return carry[0] + grad, carry[1] + grad * normal

    upper, lower = panel.loop(add, (panel.zero(), panel.zero()))
    plain = panel.quadrants(upper[0], lower[0])
    cross = panel.quadrants(upper[1], lower[1])
    plain_mean = panel.reduced(plain * gain, same)
    cross_mean = panel.reduced(cross * gain, same)
    plains = [panel.spread(plain_mean, top) for top in range(2)]
    crosses = [panel.spread(cross_mean, top) for top in range(2)]

    def finish(i, top, carry):
        mask = panel.mask(columns, i)
        normal = normal_of(i, top, mask)
        scaled = gradient(i, mask, None) * gain
        value = rstds[top] * (scaled - plains[top] - normal * crosses[top])
        return emit(i, top, jnp.where(mask, value, 0.0), carry, columns)

    found = panel.loop(finish, extra, after)
    grad_gain = jnp.sum(cross, axis=0, keepdims=True)
    grad_shift = jnp.sum(plain, axis=0, keepdims=True)
    return grad_gain, grad_shift, found


def store_parts(meta, staged, keep, send, m):
    block = keep.shape[2]
    for k in range(4):
        keep[k, m] = staged[pl.ds(pl.multiple_of(meta[M_KEEP + k], block), block), :].astype(B16)
        send[k, m] = staged[pl.ds(pl.multiple_of(meta[M_SEND + k], block), block), :].astype(B16)


TAP_SLOTS = 3


class Parts:
    def __init__(self, meta, staged, keep, send, targets, sems):
        self.meta, self.staged, self.keep, self.send = meta, staged, keep, send
        self.targets, self.sems, self.flying = targets, sems, []

    def put(self, value, m):
        n = len(self.flying)
        slot, staged = n % TAP_SLOTS, self.staged.at[n % 2]
        staged[...] = value
        if n >= TAP_SLOTS:
            for copy in self.flying[n - TAP_SLOTS]:
                copy.wait()
        store_parts(self.meta, staged, self.keep, self.send, slot)
        sources = (
            self.keep.at[:, slot],
            self.send.at[pl.ds(0, 2), slot],
            self.send.at[pl.ds(2, 2), slot],
        )
        self.flying.append(
            [
                fetch(source, target.at[:, m], self.sems.at[slot, k])
                for k, (source, target) in enumerate(zip(sources, self.targets))
            ]
        )

    def finish(self):
        for copies in self.flying[-TAP_SLOTS:]:
            for copy in copies:
                copy.wait()


def tap_grads_of(side, hb, loads, grad, parts):
    pixels = side * side // 2
    for tap, row, col in tap_order(False):
        if row == 0 and loads is not None:
            loads[col].wait()
        start = row * side
        parts.put(
            dot(hb[col, 0, start : start + pixels, :], grad[0:pixels, :], TN)
            + dot(hb[col, 1, start : start + pixels, :], grad[pixels:, :], TN),
            tap,
        )


def tap_kernel(side, meta, hb_in, grad_in, keep_to, near_to, pair_to, *refs):
    hb, grad, staged, keep, send, in_sems, out_sems = refs
    first = fetch(grad_in, grad, in_sems.at[3])
    loads = [fetch(hb_in.at[b], hb.at[b], in_sems.at[b]) for b in range(3)]
    first.wait()
    parts = Parts(meta, staged, keep, send, (keep_to, near_to, pair_to), out_sems)
    tap_grads_of(side, hb, loads, grad, parts)
    parts.finish()


def conv_kernel(side, count, meta, hb_in, image_in, vec, *refs):
    pieces, refs = refs[:count], refs[count:]
    middle_to, stats_two, hb_to, residual_to, stats, normed_to, weights_to = refs[:7]
    held_one, sems_one, held_two, sems_two, hb, middle, image, residual, normed, in_sems, out_sems = refs[7:]
    channels = residual.shape[1]
    panel = Panel(meta[M_KIND], side, channels)
    first = Weights(meta, pieces, 0, held_one, sems_one)
    second = Weights(meta, pieces, 9, held_two, sems_two)
    loads = start_taps(first, hb_in, hb, in_sems, False)
    sender = Sender(out_sems)
    same = panel.same_group()
    pixels = panel.half * side
    for top in range(2):
        middle[top * pixels : (top + 1) * pixels, :] = (
            conv_taps(panel, hb, loads, first, top, NN, False) + vec[2:3, :]
        )
        send_half(panel, sender, middle, middle_to, top)
        if top == 0:
            image_load = fetch(image_in, image, in_sems.at[3])
            start_taps(second, None, None, None, False)

    def middle_load(i):
        return middle[panel.rows(i), :]

    mean, rstd = norm_stats(panel, middle_load, same)
    stats_two[0:STAT, :] = mean
    stats_two[STAT:, :] = rstd
    silu_shifted(panel, middle_load, mean, rstd, vec[3:4, :], vec[4:5, :], hb, sender, hb_to)
    image_load.wait()
    for top in range(2):
        span = slice(top * pixels, (top + 1) * pixels)
        residual[span, :] = (
            image[span, :].astype(F32)
            + conv_taps(panel, hb, None, second, top, NN, False)
            + vec[5:6, :]
        )
        if top == 0:
            sender.send(held_two, weights_to)
        send_half(panel, sender, residual, residual_to, top)

    def residual_load(i):
        return residual[panel.rows(i), :]

    mean, rstd = norm_stats(panel, residual_load, same)
    stats[0:STAT, :] = mean
    stats[STAT:, :] = rstd
    columns = panel.columns()
    means = [panel.spread(mean, top) for top in range(2)]
    rstds = [panel.spread(rstd, top) for top in range(2)]

    def step(i, top, carry):
        value = (residual_load(i) - means[top]) * rstds[top]
        normal = jnp.where(panel.mask(columns, i), value, 0.0)
        normed[panel.rows(i), :] = (normal * vec[6:7, :] + vec[7:8, :]).astype(B16)
        return carry

    panel.loop(step, 0, lambda top: send_half(panel, sender, normed, normed_to, top))
    sender.finish()


def attention_kernel(side, count, meta, residual_in, stats, normed_in, grad_in, vec, *refs):
    pieces, refs = refs[:count], refs[count:]
    (block_to, d_residual_to, grad_to, eb_to, keep_to, near_to, pair_to, rows_out) = refs[:8]
    (held_attn, sems_attn, residual, normed, queries, keys, values, soft, soft_low, d_scores,
     attended, d_attended, d_queries, d_keys, d_values, gout, d_normed, block_out, d_residual,
     d_middle, eb, staged, keep, send, in_sems, out_sems, part_sems) = refs[8:]
    channels = residual.shape[1]
    panel = Panel(meta[M_KIND], side, channels)
    normed_load = fetch(normed_in, normed, in_sems.at[3])
    third = Weights(meta, pieces, 18, held_attn, sems_attn)
    third.start(range(4))
    grad_load = fetch(grad_in, gout, in_sems.at[4])
    residual_copy = fetch(residual_in, residual, in_sems.at[5])
    sender = Sender(out_sems)
    parts = Parts(meta, staged, keep, send, (keep_to, near_to, pair_to), part_sems)
    same = panel.same_group()

    def residual_load(i):
        return residual[panel.rows(i), :]

    normed_load.wait()
    total = side * side
    block = total // 4
    inv_root = 1.0 / math.sqrt(channels)
    shift = side.bit_length() - 1

    def labels(pixel):
        i, j = pixel >> shift, pixel & (side - 1)
        quarter = jnp.where(i >= panel.half, 2, 0) + jnp.where(j >= panel.half, 1, 0)
        four = jnp.where(panel.kind == 2, 1, 0)
        lab = quarter * four
        return jnp.where((i < panel.limit) & (j < panel.limit), lab, -1)

    key_labels = labels(lax.broadcasted_iota(jnp.int32, (1, total), 1))

    def block_labels(n):
        return labels(lax.broadcasted_iota(jnp.int32, (block, 1), 0) + n * block)

    for m in range(4):
        third.wait(m)
    for n in range(4):
        span = slice(n * block, (n + 1) * block)
        rows = normed[span, :]
        queries[span, :] = (dot(rows, held_attn[0], NN) + vec[8:9, :]).astype(B16)
        keys[span, :] = dot(rows, held_attn[1], NN).astype(B16)
        values[span, :] = (dot(rows, held_attn[2], NN) + vec[9:10, :]).astype(B16)
    gout_sum = jnp.zeros((1, channels), F32)
    grad_load.wait()
    residual_copy.wait()
    for n in range(4):
        span = slice(n * block, (n + 1) * block)
        lab = block_labels(n)
        scores = dot(queries[span, :], keys[...], NT) * inv_root
        scores = jnp.where((lab == key_labels) & (key_labels >= 0), scores, MASK_FILL)
        top = jnp.max(scores, axis=-1, keepdims=True)
        grown = jnp.exp(scores - top)
        chances = grown * (1.0 / jnp.sum(grown, axis=-1, keepdims=True))
        soft[span, :] = chances
        soft_low[span, :] = chances.astype(B16)
        attended[span, :] = dot(soft_low[span, :], values[...], NN).astype(B16)
        projected = dot(attended[span, :], held_attn[3], NN) + vec[10:11, :]
        valid = lab >= 0
        block_out[span, :] = jnp.where(valid, residual[span, :] + projected, 0.0).astype(B16)
        grad = jnp.where(valid, gout[span, :].astype(F32), 0.0)
        gout_sum = gout_sum + jnp.sum(grad, axis=0, keepdims=True)
        gout[span, :] = grad.astype(B16)
        d_attended[span, :] = dot(gout[span, :], held_attn[3], NT).astype(B16)
    sender.send(block_out, block_to)
    for n in range(4):
        span = slice(n * block, (n + 1) * block)
        d_soft = dot(d_attended[span, :], values[...], NT)
        chances = soft[span, :]
        delta = jnp.sum(d_soft * chances, axis=-1, keepdims=True)
        d_scores[span, :] = (chances * (d_soft - delta)).astype(B16)
        d_queries[span, :] = (dot(d_scores[span, :], keys[...], NN) * inv_root).astype(B16)
    d_keys[...] = (dot(d_scores[...], queries[...], TN) * inv_root).astype(B16)
    d_values[...] = dot(soft_low[...], d_attended[...], TN).astype(B16)
    pairs = ((normed, d_queries), (normed, d_keys), (normed, d_values), (attended, gout))
    for m, (left, right) in enumerate(pairs):
        parts.put(dot(left[...], right[...], TN), m)
    for n in range(4):
        span = slice(n * block, (n + 1) * block)
        d_normed[span, :] = (
            dot(d_queries[span, :], held_attn[0], NT)
            + dot(d_keys[span, :], held_attn[1], NT)
            + dot(d_values[span, :], held_attn[2], NT)
        )

    def gradient(i, mask, normal):
        return jnp.where(mask, d_normed[panel.rows(i), :], 0.0)

    def emit(i, top, value, carry, columns):
        place = panel.rows(i)
        full = gout[place, :].astype(F32) + value
        d_residual[place, :] = full
        low = full.astype(B16)
        d_middle[place, :] = low
        row = low.astype(F32)
        store_shifted(panel, eb, i, top, row, columns)
        return (
            carry[0] + row,
            carry[1] + d_queries[place, :].astype(F32),
            carry[2] + d_values[place, :].astype(F32),
        )

    def after(top):
        send_half(panel, sender, d_residual, d_residual_to, top)
        send_half(panel, sender, d_middle, grad_to, top)
        if top == 1:
            store_edges(panel, eb)
        send_shifted(panel, sender, eb, eb_to, top)

    zero = panel.zero()
    grad_gain, grad_shift, found = norm_back(
        panel, residual_load, stats, vec[6:7, :], same, gradient, emit, (zero, zero, zero), after
    )
    sums = [jnp.sum(found[0][k] + found[1][k], axis=0, keepdims=True) for k in range(3)]
    rows_out[0:1, :] = sums[0]
    rows_out[1:2, :] = grad_gain
    rows_out[2:3, :] = grad_shift
    rows_out[3:4, :] = sums[1]
    rows_out[4:5, :] = sums[2]
    rows_out[5:6, :] = gout_sum
    rows_out[6:8, :] = jnp.zeros((2, channels), F32)
    parts.finish()
    sender.finish()


def back_kernel(side, last, count, meta, eb_in, source_in, stats, vec, *refs):
    if last:
        residual_in, pieces, refs = refs[0], refs[1 : 1 + count], refs[1 + count :]
        out_to, rows_out, held, sems, eb, source, slope, out, d_residual, in_sems, out_sems = refs
        first = 0
    else:
        pieces, refs = refs[:count], refs[count:]
        out_to, rows_out, held, sems, eb, source, slope, out, in_sems, out_sems = refs
        first = 3
    panel = Panel(meta[M_KIND], side, source.shape[1])
    if last:
        given = fetch(eb_in, out, in_sems.at[0])
        weights, loads = Weights(meta, pieces, 0, held, sems), None
        start_taps(weights, None, None, None, True)
    else:
        weights = Whole(pieces[0], held, sems)
        loads = start_taps(weights, eb_in, eb, in_sems, True)
    later = [fetch(source_in, source, in_sems.at[3])]
    if last:
        later.append(fetch(residual_in, d_residual, in_sems.at[4]))
    sender = Sender(out_sems)
    same = panel.same_group()
    gain, shift = vec[first : first + 1, :], vec[first + 1 : first + 2, :]
    if last:
        columns = panel.columns()
        given.wait()

        def widen(i, top, carry):
            row = out[panel.rows(i), :].astype(F32)
            store_shifted(panel, eb, i, top, row, columns)
            return carry

        panel.loop(widen, 0)
        store_edges(panel, eb)
    pixels = panel.half * side
    for top in range(2):
        slope[top * pixels : (top + 1) * pixels, :] = conv_taps(
            panel, eb, loads, weights, top, NT, True
        )
    for copy in later:
        copy.wait()

    def load(i):
        return source[panel.rows(i), :].astype(F32)

    def gradient(i, mask, normal):
        place = panel.rows(i)
        if normal is None:
            return slope[place, :]
        pre = normal * gain + shift
        sig = 0.5 + 0.5 * jnp.tanh(0.5 * pre)
        value = jnp.where(mask, slope[place, :] * (sig * (1.0 + pre * (1.0 - sig))), 0.0)
        slope[place, :] = value
        return value

    def emit(i, top, value, carry, columns):
        place = panel.rows(i)
        if last:
            out[place, :] = (d_residual[place, :] + value).astype(B16)
            return carry
        low = value.astype(B16)
        out[place, :] = low
        return carry + low.astype(F32)

    def after(top):
        send_half(panel, sender, out, out_to, top)

    grad_gain, grad_shift, found = norm_back(
        panel, load, stats, gain, same, gradient, emit, 0 if last else panel.zero(), after
    )
    channels = panel.channels
    rows_out[0:1, :] = grad_gain
    rows_out[1:2, :] = grad_shift
    if last:
        rows_out[2:8, :] = jnp.zeros((6, channels), F32)
    else:
        rows_out[2:3, :] = jnp.sum(found[0] + found[1], axis=0, keepdims=True)
        rows_out[3:8, :] = jnp.zeros((5, channels), F32)
    sender.finish()


def slot_kernel(owner, *refs):
    terms, second, third, out = refs[:4], refs[4], refs[5], refs[6]
    out[...] = jnp.zeros(out.shape, out.dtype)
    for m in range(MATS):
        if m < 9:
            total = terms[0][0, m].astype(F32)
            for term in terms[1:]:
                total = total + term[0, m].astype(F32)
            out[owner[m]] = total.astype(out.dtype)
        else:
            out[owner[m]] = second[m - 9] if m < 18 else third[m - 18]


def adam_kernel(meta, master, first, second, mine, other, new_first, new_second, new_master, grad):
    block = mine.shape[1]
    core = meta[M_CORE]
    grad[pl.ds(pl.multiple_of(core * block, block), block), :] = mine[0].astype(F32)
    grad[pl.ds(pl.multiple_of((1 - core) * block, block), block), :] = other[0].astype(F32)
    results = adam_update(master[0], first[0], second[0], grad[...], LEARN_RATE)
    new_first[0], new_second[0], new_master[0] = results


def on_panel(
    image_in,
    panel_kind,
    owner_slot,
    out_grad,
    master,
    first_moment,
    second_moment,
    vec_master,
    vec_first,
    vec_second,
):
    side, channels = image_in.shape[2], image_in.shape[3]
    imgs = lax.axis_size("imgs")
    chips = imgs // 2
    own, depth = master.shape[0], master.shape[1]
    block = depth // 2
    total = side * side
    group, row = lax.axis_index("imgs"), lax.axis_index("rows")
    core, chip = group % 2, group // 2

    def permutation(target):
        pairs = []
        for i in range(imgs):
            for r in range(4):
                to_i, to_r = target(i, r)
                pairs.append((i * 4 + r, to_i * 4 + to_r))
        return pairs

    to_core = permutation(lambda i, r: (i ^ 1, r))
    to_near = [permutation(lambda i, r, k=k: (i, r ^ k)) for k in range(4)]
    to_first = permutation(lambda i, r: (i, r ^ (1 + i % 2)))
    to_second = permutation(lambda i, r: (i, r ^ (2 - i % 2)))
    to_chip = [permutation(lambda i, r, d=d: ((i + 2 * d) % imgs, r)) for d in range(chips)]
    across_chip = [permutation(lambda i, r, e=e: (i ^ (2 * e), r)) for e in range(chips)]

    def move(value, pairs):
        return lax.ppermute(value, AXES, pairs)

    tie = lax.optimization_barrier
    wide = shaped((total, channels), F32)
    narrow = shaped((total, channels), B16)
    stat = shaped((2 * STAT, channels), F32)
    shifted = shaped((3, 2, (side // 2 + 2) * side, channels), B16)
    vec_rows = shaped((8, channels), F32)
    held_shifted = pltpu.VMEM(shifted.shape, B16)
    held_wide = pltpu.VMEM((total, channels), F32)
    held_narrow = pltpu.VMEM((total, channels), B16)
    loads, sends = pltpu.SemaphoreType.DMA((6,)), pltpu.SemaphoreType.DMA((SENDS,))
    near_first, near_second = row ^ (1 + core), row ^ (2 - core)
    quarters = [row, near_first, near_second, row ^ 3, row, near_second, near_first, row ^ 3]
    halves = [core] * 4 + [1 - core] * 4
    kind = lax.dynamic_index_in_dim(panel_kind, row, keepdims=False)
    slot_chip, slot_core = owner_slot // (2 * own), (owner_slot // own) % 2
    place = owner_slot % own + jnp.where(slot_core == core, 0, own)
    meta = jnp.stack(
        [kind, core]
        + [q * depth + h * block for q, h in zip(quarters, halves)]
        + [q * depth + core * block for q in (row, near_second, near_first, row ^ 3)]
        + [q * depth + (1 - core) * block for q in (row, near_first, near_second, row ^ 3)]
    ).astype(jnp.int32)
    away = chip ^ slot_chip
    third = jnp.where(away == 3, 2 * own, 0)
    meta = jnp.concatenate(
        [meta, jnp.minimum(away, 2), place + third, (place ^ own) + third]
    ).astype(jnp.int32)
    image = lax.all_to_all(image_in, "rows", 0, 0, tiled=True).reshape(total, channels)

    low = shaped((own, block, channels), B16)
    core_only = jnp.stack([jnp.zeros_like(core), core]).astype(jnp.int32)
    mine, send = call(
        cast_kernel, (low, low), [SSPEC, VSPEC], (VSPEC, VSPEC), [], (core_only, master), vmem=16
    )
    here = jnp.concatenate([mine, move(send, to_core)], axis=0)

    arrived = [here] + [move(here, across_chip[e]) for e in range(1, chips)]
    hb_one, stats_one = call(
        functools.partial(first_kernel, side),
        (shifted, stat),
        [SSPEC, VSPEC, VSPEC],
        (ASPEC, VSPEC),
        [held_shifted, sends],
        (meta, image, vec_master),
        moved=5 * total * channels * 2,
    )
    rounds = arrived[:2]
    if chips == 4:
        rounds.append(jnp.concatenate(arrived[2:], axis=0))
    pieces, before = [], None
    for e, part in enumerate(rounds):
        if e == 1:
            part, before, hb_one = tie((part, before, hb_one))
        elif e == 2:
            part, before = tie((part, before))
        near, far = move(part, to_first), move(part, to_second)
        if e == 2:
            near, far, pieces[PIECES + 3] = tie((near, far, pieces[PIECES + 3]))
        corner = move(near, to_second)
        before = [near, far] if e == 0 else [near, far, pieces[3]]
        held = [part, near, far, corner]
        pieces += held + [move(piece, to_core) for piece in held]
    out_grad, pieces[-5] = tie((out_grad, pieces[-5]))
    count = len(pieces)

    def weight_scratch(n):
        return [pltpu.VMEM((n, channels, channels), B16), pltpu.SemaphoreType.DMA((n, 8))]

    conv_flops = 2 * total * 9 * channels * channels
    conv_bytes = 9 * channels * channels * 2 + 8 * total * channels

    cotangent = lax.all_to_all(out_grad, "rows", 0, 0, tiled=True).reshape(total, channels)
    parts_of = lambda n, m: shaped((n, m, block, channels), B16)
    slots = pltpu.VMEM((4, TAP_SLOTS, block, channels), B16)
    part_scratch = [pltpu.VMEM((2, channels, channels), F32), slots, slots]
    part_sems = pltpu.SemaphoreType.DMA((TAP_SLOTS, 3))
    pixel_pairs = [pltpu.VMEM((total, total), F32)] + [pltpu.VMEM((total, total), B16)] * 2
    middle, stats_two, hb_two, residual, stats_three, normed, weights_two = call(
        functools.partial(conv_kernel, side, count),
        (wide, stat, shifted, wide, stat, narrow, shaped((9, channels, channels), B16)),
        [SSPEC, ASPEC, ASPEC, VSPEC] + [ASPEC] * count,
        (ASPEC, VSPEC, ASPEC, ASPEC, VSPEC, ASPEC, ASPEC),
        weight_scratch(9)
        + weight_scratch(9)
        + [held_shifted, held_wide, held_narrow, held_wide, held_narrow, loads, sends],
        [meta, hb_one, image, vec_master] + pieces,
        flops=2 * conv_flops,
        moved=conv_bytes,
    )
    (block_out, d_residual, d_middle_two, eb_two, keep_a, near_a, pair_a, rows_attn) = call(
        functools.partial(attention_kernel, side, count),
        (narrow, wide, narrow, shifted, parts_of(4, 4), parts_of(2, 4), parts_of(2, 4), vec_rows),
        [SSPEC, ASPEC, VSPEC, ASPEC, ASPEC, VSPEC] + [ASPEC] * count,
        (ASPEC,) * 7 + (VSPEC,),
        weight_scratch(4)
        + [held_wide, held_narrow]
        + [held_narrow] * 3
        + pixel_pairs
        + [held_narrow] * 6
        + [held_wide, held_narrow, held_wide, held_narrow, held_shifted]
        + part_scratch
        + [loads, sends, part_sems],
        [meta, residual, stats_three, normed, cotangent, vec_master] + pieces,
        flops=4 * conv_flops,
        moved=2 * conv_bytes,
    )

    def tap_grads(hb, grad):
        return call(
            functools.partial(tap_kernel, side),
            (parts_of(4, 9), parts_of(2, 9), parts_of(2, 9)),
            [SSPEC, ASPEC, ASPEC],
            (ASPEC,) * 3,
            [held_shifted, held_narrow] + part_scratch + [loads, part_sems],
            (meta, hb, grad),
            flops=conv_flops,
            moved=conv_bytes,
        )

    def added(*terms):
        return sum((v.astype(F32) for v in terms[1:]), terms[0].astype(F32)).astype(B16)

    chip_groups = [list(range(c, imgs, 2)) for c in range(2)]

    def pair_of(keep, got):
        return added(keep[2:4], got[1])

    def quarter_of(keep, got, arrived, k):
        return added(keep[k], got[0][k], arrived[k])

    def from_core(near, pair):
        return move(near, to_core), move(pair, to_core)

    got_attn = from_core(near_a, pair_a)
    d_middle_one, rows_two = call(
        functools.partial(back_kernel, side, False, 1),
        (narrow, vec_rows),
        [SSPEC, ASPEC, ASPEC, VSPEC, VSPEC] + [ASPEC],
        (ASPEC, VSPEC),
        weight_scratch(9)
        + [held_shifted, held_wide, held_wide, held_narrow, loads, sends],
        [meta, eb_two, middle, stats_two, vec_master, weights_two],
        flops=conv_flops,
        moved=conv_bytes,
    )
    got_attn, d_middle_two, d_middle_one = tie((got_attn, d_middle_two, d_middle_one))
    pair_attn, d_middle_two = tie((pair_of(keep_a, got_attn), d_middle_two))
    arrived_attn = move(pair_attn, to_first)
    keep_two, near_two, pair_two = tap_grads(hb_two, d_middle_two)
    got_two = from_core(near_two, pair_two)
    send_attn = quarter_of(keep_a, got_attn, arrived_attn, 1)
    send_attn, near_two, d_middle_one = tie((send_attn, near_two, d_middle_one))
    quarter_attn = move(send_attn, to_second)
    keep_one, near_one, pair_one = tap_grads(hb_one, d_middle_one)
    got_one = from_core(near_one, pair_one)
    got_two, near_one = tie((got_two, near_one))
    pair_two = pair_of(keep_two, got_two)
    arrived_two = move(pair_two, to_first)
    pair_one = pair_of(keep_one, got_one)
    pair_two, pair_one, d_middle_one = tie((pair_two, pair_one, d_middle_one))
    arrived_one = move(pair_one, to_first)
    d_image, rows_one = call(
        functools.partial(back_kernel, side, True, count),
        (narrow, vec_rows),
        [SSPEC, ASPEC, ASPEC, VSPEC, VSPEC, ASPEC] + [ASPEC] * count,
        (ASPEC, VSPEC),
        weight_scratch(9)
        + [held_shifted, held_narrow, held_wide, held_narrow, held_wide, loads, sends],
        [meta, d_middle_one, image, stats_one, vec_master, d_residual] + pieces,
        flops=conv_flops,
        moved=conv_bytes,
    )
    arrived_two, d_image = tie((arrived_two, d_image))
    send_two = quarter_of(keep_two, got_two, arrived_two, 1)
    send_two, rows_one = tie((send_two, rows_one))
    quarter_two = move(send_two, to_second)
    vec_grads = jnp.concatenate([rows_one[0:2], rows_two[2:3], rows_two[0:2], rows_attn[0:6]])
    vec_grads = vec_grads + move(vec_grads, to_core)
    if chips == 4:
        far = [move(vec_grads, across_chip[e]) for e in range(1, 4)]
        vec_grads = (vec_grads + far[0]) + (far[1] + far[2])
    elif chips == 2:
        vec_grads = vec_grads + move(vec_grads, across_chip[1])
    quarter_one = move(quarter_of(keep_one, got_one, arrived_one, 1), to_second)
    sum_two = added(quarter_of(keep_two, got_two, arrived_two, 0), quarter_two)
    sum_attn = added(quarter_of(keep_a, got_attn, arrived_attn, 0), quarter_attn)
    quarter_one, sum_two, sum_attn, vec_grads = tie((quarter_one, sum_two, sum_attn, vec_grads))
    slots_shape = shaped((chips * 2 * own, block, channels), B16)
    one = pl.BlockSpec((1, 9, block, channels), lambda t: (0, 0, 0, 0))
    slot_terms = call(
        slot_kernel,
        slots_shape,
        [SSPEC, one, one, one, one] + [pl.BlockSpec(v.shape, lambda t: (0, 0, 0)) for v in (sum_two, sum_attn)],
        pl.BlockSpec(slots_shape.shape, lambda t: (0, 0, 0)),
        [],
        [owner_slot, keep_one, got_one[0], arrived_one, quarter_one[None], sum_two, sum_attn],
        grid=(1,),
        vmem=24,
    )
    by_chip = lax.all_to_all(
        slot_terms, "imgs", 0, 0, tiled=True, axis_index_groups=chip_groups
    ).reshape(chips, 2 * own, block, channels)

    def slots_of(which):
        terms = lax.dynamic_slice_in_dim(by_chip, which * own, own, axis=1)
        return added(*[terms[d] for d in range(chips)])

    slot_terms, vec_grads, d_image = tie((slot_terms, vec_grads, d_image))
    near = [move(vec_grads, to_near[k]) for k in range(1, 4)]
    vec_grads = (vec_grads + near[0]) + (near[1] + near[2])
    strips = jnp.stack([block_out, d_image]).reshape(2, 4, side // 4, side, channels)
    strip = lambda k: lax.dynamic_index_in_dim(strips, row ^ k, axis=1, keepdims=False)
    strips = [strip(0)] + [move(strip(k), to_near[k]) for k in range(1, 4)]
    odd, high = row % 2 == 1, row >= 2
    strips = [jnp.where(odd, strips[k ^ 1], strips[k]) for k in range(4)]
    strips = [jnp.where(high, strips[k ^ 2], strips[k]) for k in range(4)]
    block_out = jnp.stack([strip[0] for strip in strips])
    input_grad = jnp.stack([strip[1] for strip in strips])

    send = slots_of(1 - core)
    by_chip, block_out, input_grad, vec_grads = tie((by_chip, block_out, input_grad, vec_grads))
    mine, other = slots_of(core), move(send, to_core)
    deep = pl.BlockSpec((1, depth, channels), lambda t: (t, 0, 0))
    flat = pl.BlockSpec((1, block, channels), lambda t: (t, 0, 0))
    slot_shape = shaped(master.shape, F32)
    new_first, new_second, new_master = call(
        adam_kernel,
        (slot_shape,) * 3,
        [SSPEC, deep, deep, deep, flat, flat],
        (deep,) * 3,
        [pltpu.VMEM((depth, channels), F32)],
        (meta, master, first_moment, second_moment, mine, other),
        moved=6 * own * depth * channels * 4,
        grid=(own,),
        vmem=16,
    )
    vec_results = adam_update(vec_master, vec_first, vec_second, vec_grads, VEC_RATE)
    return (block_out, input_grad, new_first, new_second, new_master) + vec_results


def on_slice(*args):
    image_in = args[0]
    panels, row_count, col_count, channels = image_in.shape
    rows, imgs = lax.axis_size("rows"), lax.axis_size("imgs")
    chips = imgs // 2
    whole_panels = (
        rows == 4
        and panels == rows
        and row_count * rows == col_count == 32
        and channels == 512
        and args[4].shape[0] == 4
        and imgs == 2 * chips
        and args[2].shape[0] == MATS
        and chips in (1, 2, 4)
    )
    return on_panel(*args) if whole_panels else on_device(*args)


def solution(mesh):
    in_specs = (
        P("imgs", "rows", None, None),
        P("imgs"),
        P(),
        P("imgs", "rows", None, None),
        P("imgs", "rows", None),
        P("imgs", "rows", None),
        P("imgs", "rows", None),
        P(),
        P(),
        P(),
    )
    out_specs = (
        P("imgs", "rows", None, None),
        P("imgs", "rows", None, None),
        P("imgs", "rows", None),
        P("imgs", "rows", None),
        P("imgs", "rows", None),
        P(),
        P(),
        P(),
    )
    return jax.shard_map(
        on_slice, mesh=mesh, in_specs=in_specs, out_specs=out_specs, check_vma=False
    )
```

```python
import functools
import math

import jax
import jax.numpy as jnp
from jax import lax
from jax.experimental import pallas as pl
from jax.experimental.pallas import tpu as pltpu
from jax.sharding import PartitionSpec as P

GROUPS = 32
MATS = 22
STEP = 5


EXACT_PRECISION = lax.Precision.HIGHEST
NORM_EPS = 1e-06
LEARN_RATE = 0.05
VEC_RATE = 0.2
BETA_ONE = 0.5
BETA_TWO = 0.5
ADAM_EPS = 1e-08
WEIGHT_DECAY = 0.01
MASK_FILL = -1000000000.0


def extended(cells, sides, width):
    for axis, dim in sides:
        count = lax.axis_size(axis)
        ends = count - 1
        head = lax.slice_in_dim(cells, 0, width, axis=dim)
        tail = lax.slice_in_dim(cells, cells.shape[dim] - width, cells.shape[dim], axis=dim)
        cells = jnp.concatenate(
            [
                lax.ppermute(tail, axis, [(i, (i + 1) % count) for i in range(ends)]),
                cells,
                lax.ppermute(head, axis, [((i + 1) % count, i) for i in range(ends)]),
            ],
            axis=dim,
        )
    return cells


def panel_ids(kind_list, row_index, col_index, panel_side):
    row_grid = row_index[None, :, None]
    col_grid = col_index[None, None, :]
    kind_grid = kind_list[:, None, None]
    half_side = panel_side // 2
    part_side = 3 * panel_side // 4
    inside = (row_grid >= 0) & (row_grid < panel_side) & (col_grid >= 0) & (col_grid < panel_side)
    quarter = 2 * (row_grid >= half_side).astype(jnp.int32) + (col_grid >= half_side).astype(
        jnp.int32
    )
    zero_grid = jnp.zeros_like(quarter)
    corner = jnp.where((row_grid < part_side) & (col_grid < part_side), zero_grid, zero_grid - 1)
    labels = jnp.where(
        kind_grid == 0,
        zero_grid,
        jnp.where(kind_grid == 1, corner, jnp.where(kind_grid == 2, quarter, zero_grid - 1)),
    )
    return jnp.where(inside & (labels >= 0), labels, -1)


def spread_pix(onehot, per_group):
    return jnp.einsum("prwi,pig->prwg", onehot, per_group, precision=EXACT_PRECISION)


def group_stats(value_rows, onehot, counts):
    panel_count, row_count, col_count, channel_count = value_rows.shape
    grouped = value_rows.reshape(panel_count, row_count, col_count, GROUPS, channel_count // GROUPS)
    first_sums = lax.psum(
        jnp.einsum("prwi,prwgc->pig", onehot, grouped, precision=EXACT_PRECISION), "rows"
    )
    group_mean = first_sums / counts[:, :, None]
    centred = grouped - spread_pix(onehot, group_mean)[..., None]
    square_sums = jnp.einsum(
        "prwi,prwgc->pig", onehot, centred * centred, precision=EXACT_PRECISION
    )
    spread = lax.psum(square_sums, "rows") / counts[:, :, None]
    scale_pix = spread_pix(onehot, lax.rsqrt(spread + NORM_EPS))
    normal_val = (centred * scale_pix[..., None]).reshape(value_rows.shape)
    return (normal_val, scale_pix)


def group_back(gradient, normal_val, scale_pix, gain_row, onehot, counts):
    panel_count, row_count, col_count, channel_count = gradient.shape
    grad_gain = jnp.sum(gradient * normal_val, axis=(0, 1, 2))
    grad_shift = jnp.sum(gradient, axis=(0, 1, 2))
    scaled = (gradient * gain_row).reshape(
        panel_count, row_count, col_count, GROUPS, channel_count // GROUPS
    )
    normal_grp = normal_val.reshape(scaled.shape)
    plain_sums = jnp.einsum("prwi,prwgc->pig", onehot, scaled, precision=EXACT_PRECISION)
    cross_sums = jnp.einsum(
        "prwi,prwgc->pig", onehot, scaled * normal_grp, precision=EXACT_PRECISION
    )
    plain_sums, cross_sums = lax.psum((plain_sums, cross_sums), "rows")
    plain_pix = spread_pix(onehot, plain_sums / counts[:, :, None])
    cross_pix = spread_pix(onehot, cross_sums / counts[:, :, None])
    result = scale_pix[..., None] * (
        scaled - plain_pix[..., None] - normal_grp * cross_pix[..., None]
    )
    return (result.reshape(gradient.shape), grad_gain, grad_shift)


def silu_slope(pre_act):
    sigmoid_val = jax.nn.sigmoid(pre_act)
    return sigmoid_val * (1.0 + pre_act * (1.0 - sigmoid_val))


def conv_forward(hidden, weight_cat, tap_masks):
    panel_count, row_count, col_count, channel_count = hidden.shape
    padded = extended(hidden, (("rows", 1),), 1)
    padded = jnp.pad(padded, ((0, 0), (0, 0), (1, 1), (0, 0)))
    columns = jnp.concatenate(
        [
            padded[
                :,
                tap_index // 3 : tap_index // 3 + row_count,
                tap_index % 3 : tap_index % 3 + col_count,
                :,
            ]
            * tap_masks[tap_index]
            for tap_index in range(9)
        ],
        axis=-1,
    )
    columns = columns.reshape(-1, 9 * channel_count)
    result = jnp.dot(columns, weight_cat, preferred_element_type=jnp.float32)
    return (result.reshape(hidden.shape), columns)


def conv_backward(gradient, columns, weight_cat, tap_masks):
    panel_count, row_count, col_count, channel_count = gradient.shape
    grad_flat = gradient.reshape(-1, channel_count)
    weight_grad = jnp.einsum("mk,mc->kc", columns, grad_flat, preferred_element_type=jnp.float32)
    col_grads = jnp.einsum("mc,kc->mk", grad_flat, weight_cat, preferred_element_type=jnp.float32)
    col_grads = col_grads.reshape(panel_count, row_count, col_count, 9, channel_count)
    padded_grad = jnp.zeros((panel_count, row_count + 2, col_count + 2, channel_count), jnp.float32)
    for tap_index in range(9):
        tap_row = tap_index // 3
        tap_col = tap_index % 3
        padded_grad = padded_grad.at[
            :, tap_row : tap_row + row_count, tap_col : tap_col + col_count, :
        ].add(col_grads[:, :, :, tap_index, :] * tap_masks[tap_index])
    padded_grad = padded_grad[:, :, 1 : col_count + 1, :]
    edge_rows = jnp.concatenate(
        [padded_grad[:, 0:1], padded_grad[:, row_count + 1 : row_count + 2]], axis=1
    )
    arrived = extended(edge_rows.astype(jnp.bfloat16), (("rows", 1),), 1).astype(edge_rows.dtype)
    inner = padded_grad[:, 1 : row_count + 1]
    inner = inner.at[:, 0].add(arrived[:, 0])
    inner = inner.at[:, row_count - 1].add(arrived[:, 3])
    return (inner, weight_grad)


def adam_update(weight, first_old, second, gradient, step_rate):
    new_first = BETA_ONE * first_old + (1.0 - BETA_ONE) * gradient
    new_second = BETA_TWO * second + (1.0 - BETA_TWO) * gradient * gradient
    first_hat = new_first / (1.0 - BETA_ONE**STEP)
    second_hat = new_second / (1.0 - BETA_TWO**STEP)
    new_weight = weight - step_rate * (
        first_hat / (jnp.sqrt(second_hat) + ADAM_EPS) + WEIGHT_DECAY * weight
    )
    return (new_first, new_second, new_weight)


def on_device(
    image_in,
    panel_kind,
    owner_slot,
    out_grad,
    master,
    first_moment,
    second_moment,
    vec_master,
    vec_first,
    vec_second,
):
    panel_count, row_count, col_count, channel_count = image_in.shape
    height_all = row_count * lax.axis_size("rows")
    group_width = channel_count // GROUPS
    pixel_count = panel_count * row_count * col_count
    local_pix = row_count * col_count
    slot_total = master.shape[0] * lax.axis_size("imgs")
    inv_root = 1.0 / math.sqrt(channel_count)
    placing = owner_slot[None, :] == jnp.arange(slot_total, dtype=jnp.int32)[:, None]
    slot_weights = lax.all_gather(master.astype(jnp.bfloat16), "imgs", axis=0, tiled=True)
    picked = jnp.einsum(
        "sm,sij->mij",
        placing.astype(jnp.bfloat16),
        slot_weights,
        preferred_element_type=jnp.float32,
    ).astype(jnp.bfloat16)
    weights = lax.all_gather(picked, "rows", axis=1, tiled=True)
    conv_first = weights[0:9].reshape(9 * channel_count, channel_count)
    conv_second = weights[9:18].reshape(9 * channel_count, channel_count)
    attn_in = jnp.concatenate([weights[18], weights[19], weights[20]], axis=1)
    attn_out = weights[21]
    first_row = lax.axis_index("rows") * row_count
    col_range = jnp.arange(col_count, dtype=jnp.int32)
    labels = panel_ids(
        panel_kind, first_row + jnp.arange(row_count, dtype=jnp.int32), col_range, height_all
    )
    outer_labels = panel_ids(
        panel_kind,
        first_row + jnp.arange(-1, row_count + 1, dtype=jnp.int32),
        jnp.arange(-1, col_count + 1, dtype=jnp.int32),
        height_all,
    )
    whole_labels = panel_ids(
        panel_kind, jnp.arange(height_all, dtype=jnp.int32), col_range, height_all
    )
    label_range = jnp.arange(4, dtype=jnp.int32)
    onehot = (labels[..., None] == label_range).astype(jnp.float32)
    validity = (labels >= 0).astype(jnp.float32)[..., None]
    counts = jnp.maximum(
        jnp.sum((whole_labels[..., None] == label_range).astype(jnp.float32), axis=(1, 2))
        * group_width,
        1.0,
    )
    tap_masks = [
        (
            (
                outer_labels[
                    :,
                    tap_index // 3 : tap_index // 3 + row_count,
                    tap_index % 3 : tap_index % 3 + col_count,
                ]
                == labels
            )
            & (labels >= 0)
        ).astype(jnp.bfloat16)[..., None]
        for tap_index in range(9)
    ]
    image_vals = image_in.astype(jnp.float32)
    normal_one, scale_one = group_stats(image_vals, onehot, counts)
    pre_one = normal_one * vec_master[0] + vec_master[1]
    hidden_one = jax.nn.silu(pre_one).astype(jnp.bfloat16)
    conv_out, columns_one = conv_forward(hidden_one, conv_first, tap_masks)
    middle = conv_out + vec_master[2]
    normal_two, scale_two = group_stats(middle, onehot, counts)
    pre_two = normal_two * vec_master[3] + vec_master[4]
    hidden_two = jax.nn.silu(pre_two).astype(jnp.bfloat16)
    conv_out_two, columns_two = conv_forward(hidden_two, conv_second, tap_masks)
    residual = image_vals + conv_out_two + vec_master[5]
    normal_three, scale_three = group_stats(residual, onehot, counts)
    normed = (
        (normal_three * vec_master[6] + vec_master[7])
        .astype(jnp.bfloat16)
        .reshape(pixel_count, channel_count)
    )
    qkv_vals = jnp.dot(normed, attn_in, preferred_element_type=jnp.float32)
    query_matrix = (
        (qkv_vals[:, :channel_count] + vec_master[8])
        .astype(jnp.bfloat16)
        .reshape(panel_count, local_pix, channel_count)
    )
    key_loc = (
        qkv_vals[:, channel_count : 2 * channel_count]
        .astype(jnp.bfloat16)
        .reshape(panel_count, row_count, col_count, channel_count)
    )
    values_loc = (
        (qkv_vals[:, 2 * channel_count :] + vec_master[9])
        .astype(jnp.bfloat16)
        .reshape(panel_count, row_count, col_count, channel_count)
    )
    keys_all, values_all = (
        lax.all_gather(key_loc, "rows", axis=1, tiled=True),
        lax.all_gather(values_loc, "rows", axis=1, tiled=True),
    )
    keys_all = keys_all.reshape(panel_count, height_all * col_count, channel_count)
    values_all = values_all.reshape(panel_count, height_all * col_count, channel_count)
    query_labels = labels.reshape(panel_count, -1)
    key_labels = whole_labels.reshape(panel_count, -1)
    same_image = (query_labels[:, :, None] == key_labels[:, None, :]) & (
        key_labels[:, None, :] >= 0
    )
    attention_scores = (
        jnp.einsum("pqc,pkc->pqk", query_matrix, keys_all, preferred_element_type=jnp.float32)
        * inv_root
    )
    attention_scores = jnp.where(same_image, attention_scores, MASK_FILL)
    row_max = jnp.max(attention_scores, axis=-1, keepdims=True)
    exp_scores = jnp.exp(attention_scores - row_max)
    exp_total = jnp.sum(exp_scores, axis=-1, keepdims=True)
    softmax_weights = exp_scores / exp_total
    log_total = row_max[..., 0] + jnp.log(exp_total[..., 0])
    attended_values = jnp.einsum(
        "pqk,pkc->pqc",
        softmax_weights.astype(jnp.bfloat16),
        values_all,
        preferred_element_type=jnp.float32,
    ).astype(jnp.bfloat16)
    attended_values = attended_values.reshape(pixel_count, channel_count)
    projected = (
        jnp.dot(attended_values, attn_out, preferred_element_type=jnp.float32) + vec_master[10]
    ).reshape(image_in.shape)
    block_out = ((residual + projected) * validity).astype(jnp.bfloat16)
    grad_out = out_grad.astype(jnp.float32) * validity
    grad_flat = grad_out.astype(jnp.bfloat16).reshape(pixel_count, channel_count)
    grad_proj = jnp.einsum(
        "mc,md->cd", attended_values, grad_flat, preferred_element_type=jnp.float32
    )
    bias_proj = jnp.sum(grad_out, axis=(0, 1, 2))
    d_attended = jnp.einsum(
        "md,cd->mc", grad_flat, attn_out, preferred_element_type=jnp.float32
    ).astype(jnp.bfloat16)
    d_attended = d_attended.reshape(panel_count, local_pix, channel_count)
    again_scores = (
        jnp.einsum("pqc,pkc->pqk", query_matrix, keys_all, preferred_element_type=jnp.float32)
        * inv_root
    )
    again_scores = jnp.where(same_image, again_scores, MASK_FILL)
    again_soft = jnp.exp(again_scores - log_total[..., None])
    d_soft = jnp.einsum("pqc,pkc->pqk", d_attended, values_all, preferred_element_type=jnp.float32)
    row_delta = jnp.sum(d_soft * again_soft, axis=-1)
    d_scores = (again_soft * (d_soft - row_delta[..., None])).astype(jnp.bfloat16)
    d_queries = (
        jnp.einsum("pqk,pkc->pqc", d_scores, keys_all, preferred_element_type=jnp.float32)
        * inv_root
    ).astype(jnp.bfloat16)
    d_key_all = (
        jnp.einsum("pqk,pqc->pkc", d_scores, query_matrix, preferred_element_type=jnp.float32)
        * inv_root
    )
    d_value_all = jnp.einsum(
        "pqk,pqc->pkc",
        again_soft.astype(jnp.bfloat16),
        d_attended,
        preferred_element_type=jnp.float32,
    )
    d_key_all = d_key_all.reshape(panel_count, height_all, col_count, channel_count)
    d_value_all = d_value_all.reshape(panel_count, height_all, col_count, channel_count)
    d_keys, d_values = (
        lax.psum_scatter(
            d_key_all.astype(jnp.bfloat16), "rows", scatter_dimension=1, tiled=True
        ).astype(jnp.float32),
        lax.psum_scatter(
            d_value_all.astype(jnp.bfloat16), "rows", scatter_dimension=1, tiled=True
        ).astype(jnp.float32),
    )
    d_keys = d_keys.reshape(pixel_count, channel_count).astype(jnp.bfloat16)
    d_values = d_values.reshape(pixel_count, channel_count).astype(jnp.bfloat16)
    d_queries = d_queries.reshape(pixel_count, channel_count)
    d_qkv = jnp.concatenate([d_queries, d_keys, d_values], axis=1)
    grad_qkv = jnp.einsum("mc,md->cd", normed, d_qkv, preferred_element_type=jnp.float32)
    bias_query = jnp.sum(d_queries, axis=0, dtype=jnp.float32)
    bias_value = jnp.sum(d_values, axis=0, dtype=jnp.float32)
    d_normed = jnp.einsum("md,cd->mc", d_qkv, attn_in, preferred_element_type=jnp.float32).reshape(
        image_in.shape
    )
    d_three, gain_three, shift_three = group_back(
        d_normed, normal_three, scale_three, vec_master[6], onehot, counts
    )
    d_residual = grad_out + d_three
    d_middle_two = d_residual.astype(jnp.bfloat16)
    bias_two = jnp.sum(d_middle_two, axis=(0, 1, 2), dtype=jnp.float32)
    d_hidden_two, grad_conv_two = conv_backward(d_middle_two, columns_two, conv_second, tap_masks)
    d_middle, gain_two, shift_two = group_back(
        d_hidden_two * silu_slope(pre_two), normal_two, scale_two, vec_master[3], onehot, counts
    )
    d_middle_one = d_middle.astype(jnp.bfloat16)
    bias_one = jnp.sum(d_middle_one, axis=(0, 1, 2), dtype=jnp.float32)
    d_hidden_one, grad_conv_one = conv_backward(d_middle_one, columns_one, conv_first, tap_masks)
    d_input, gain_one, shift_one = group_back(
        d_hidden_one * silu_slope(pre_one), normal_one, scale_one, vec_master[0], onehot, counts
    )
    input_grad = (d_residual + d_input).astype(jnp.bfloat16)
    vec_grads = jnp.stack(
        [
            gain_one,
            shift_one,
            bias_one,
            gain_two,
            shift_two,
            bias_two,
            gain_three,
            shift_three,
            bias_query,
            bias_value,
            bias_proj,
        ]
    )
    vec_grads = lax.psum(vec_grads, ("imgs", "rows"))
    mat_grads = jnp.concatenate(
        [
            grad_conv_one.reshape(9, channel_count, channel_count),
            grad_conv_two.reshape(9, channel_count, channel_count),
            grad_qkv[:, :channel_count][None],
            grad_qkv[:, channel_count : 2 * channel_count][None],
            grad_qkv[:, 2 * channel_count :][None],
            grad_proj[None],
        ],
        axis=0,
    )
    row_grads = lax.psum_scatter(
        mat_grads.astype(jnp.bfloat16), "rows", scatter_dimension=1, tiled=True
    ).astype(jnp.float32)
    slot_terms = jnp.einsum(
        "sm,mij->sij", placing.astype(jnp.float32), row_grads, precision=EXACT_PRECISION
    )
    owned_grads = lax.psum_scatter(
        slot_terms.astype(jnp.bfloat16), "imgs", scatter_dimension=0, tiled=True
    ).astype(jnp.float32)
    new_first, new_second, new_master = adam_update(
        master, first_moment, second_moment, owned_grads, LEARN_RATE
    )
    vec_first_new, vec_second_new, vec_master_new = adam_update(
        vec_master, vec_first, vec_second, vec_grads, VEC_RATE
    )
    return (
        block_out,
        input_grad,
        new_first,
        new_second,
        new_master,
        vec_first_new,
        vec_second_new,
        vec_master_new,
    )


F32 = jnp.float32
B16 = jnp.bfloat16
AXES = ("imgs", "rows")
NN = (((1,), (0,)), ((), ()))
NT = (((1,), (1,)), ((), ()))
TN = (((0,), (0,)), ((), ()))
VSPEC = pl.BlockSpec(memory_space=pltpu.VMEM)
SSPEC = pl.BlockSpec(memory_space=pltpu.SMEM)
ASPEC = pl.BlockSpec(memory_space=pl.ANY)
STAT = 16
M_KIND, M_CORE, M_OFF, M_KEEP, M_SEND, M_FROM = 0, 1, 2, 10, 14, 18
LANES = 128


def dot(left, right, dims):
    return lax.dot_general(left, right, dims, preferred_element_type=F32)


def shaped(shape, dtype):
    return jax.ShapeDtypeStruct(shape, dtype)


def call(body, outs, in_specs, out_specs, scratch, args, flops=0, moved=0, grid=None, vmem=58):
    extra = {} if grid is None else {"grid": grid}
    return pl.pallas_call(
        body,
        out_shape=outs,
        in_specs=in_specs,
        out_specs=out_specs,
        scratch_shapes=scratch,
        compiler_params=pltpu.CompilerParams(vmem_limit_bytes=vmem * 2**20),
        cost_estimate=pl.CostEstimate(flops=flops, bytes_accessed=moved, transcendentals=0),
        **extra,
    )(*args)


class Panel:
    def __init__(self, kind, side, channels):
        self.kind, self.side, self.channels = kind, side, channels
        self.half = side // 2
        self.width = channels // GROUPS
        part = 3 * side // 4
        self.limit = jnp.where(kind == 3, 0, jnp.where(kind == 1, part, side))
        pixels = jnp.where(
            kind == 2, self.half * self.half, jnp.where(kind == 1, part * part, side * side)
        )
        count = jnp.where(kind == 3, 1, pixels * self.width)
        self.inverse = 1.0 / count.astype(F32)
        self.four = jnp.where(kind == 2, 1.0, 0.0).astype(F32)
        self.cut = jnp.where(kind == 2, self.half, -1)

    def columns(self):
        return lax.broadcasted_iota(jnp.int32, (self.side, self.channels), 0)

    def mask(self, columns, i):
        return columns < jnp.where(i < self.limit, self.limit, 0)

    def rows(self, i):
        return pl.ds(pl.multiple_of(i * self.side, self.side), self.side)

    def same_group(self):
        shift = self.width.bit_length() - 1
        shape = (LANES, LANES)
        left = lax.broadcasted_iota(jnp.int32, shape, 0) >> shift
        right = lax.broadcasted_iota(jnp.int32, shape, 1) >> shift
        return jnp.where(left == right, 1.0, 0.0).astype(B16)

    def loop(self, body, init, after=None):
        found = []
        for top in range(2):
            found.append(
                lax.fori_loop(
                    0,
                    self.half,
                    lambda t, carry, top=top: body(top * self.half + t, top, carry),
                    init,
                    unroll=2,
                )
            )
            if after is not None:
                after(top)
        return found

    def spread(self, stat, top):
        shape = (self.half, self.channels)
        return jnp.concatenate(
            [
                jnp.broadcast_to(stat[2 * top : 2 * top + 1], shape),
                jnp.broadcast_to(stat[2 * top + 1 : 2 * top + 2], shape),
            ],
            axis=0,
        )

    def quadrants(self, upper, lower):
        parts = []
        for acc in (upper, lower):
            for left in range(2):
                parts.append(
                    jnp.sum(acc[left * self.half : (left + 1) * self.half], axis=0, keepdims=True)
                )
        parts.append(jnp.zeros((STAT - 4, self.channels), F32))
        return jnp.concatenate(parts, axis=0)

    def over_images(self, sums):
        total = jnp.sum(sums, axis=0, keepdims=True)
        return sums * self.four + total * (1.0 - self.four)

    def over_groups(self, sums, same):
        high = sums.astype(B16)
        rest = sums - high.astype(F32)
        middle = rest.astype(B16)
        low = (rest - middle.astype(F32)).astype(B16)
        cuts = range(0, self.channels, LANES)
        stacked = jnp.concatenate(
            [part[:, c : c + LANES] for part in (high, middle, low) for c in cuts], axis=0
        )
        found = dot(stacked, same, NN)
        third = len(cuts) * STAT
        found = found[0:third] + found[third : 2 * third] + found[2 * third :]
        return jnp.concatenate(
            [found[k * STAT : (k + 1) * STAT] for k in range(len(cuts))], axis=1
        )

    def reduced(self, sums, same):
        return self.over_groups(self.over_images(sums), same) * self.inverse

    def zero(self):
        return jnp.zeros((self.side, self.channels), F32)


def norm_stats(panel, load, same):
    columns = panel.columns()

    def add_plain(i, top, carry):
        return carry + jnp.where(panel.mask(columns, i), load(i), 0.0)

    mean = panel.reduced(panel.quadrants(*panel.loop(add_plain, panel.zero())), same)
    means = [panel.spread(mean, top) for top in range(2)]

    def add_square(i, top, carry):
        centred = load(i) - means[top]
        return carry + jnp.where(panel.mask(columns, i), centred * centred, 0.0)

    spread = panel.reduced(panel.quadrants(*panel.loop(add_square, panel.zero())), same)
    return mean, lax.rsqrt(spread + NORM_EPS)


def store_shifted(panel, hb, i, top, row, columns):
    side = panel.side
    place = pl.ds(pl.multiple_of((i - top * panel.half + 1) * side, side), side)
    before = pltpu.roll(row, 1, 0)
    after = pltpu.roll(row, side - 1, 0)
    from_left = (columns != 0) & (columns != panel.cut)
    from_right = (columns != side - 1) & (columns != panel.cut - 1)
    hb[0, top, place, :] = jnp.where(from_left, before, 0.0).astype(B16)
    hb[1, top, place, :] = row.astype(B16)
    hb[2, top, place, :] = jnp.where(from_right, after, 0.0).astype(B16)


def store_edges(panel, hb):
    side, half = panel.side, panel.half
    joined = 1.0 - panel.four
    blank = jnp.zeros((side, panel.channels), B16)
    for b in range(3):
        hb[b, 0, 0:side, :] = blank
        hb[b, 1, (half + 1) * side : (half + 2) * side, :] = blank
        upper = hb[b, 0, half * side : (half + 1) * side, :].astype(F32) * joined
        lower = hb[b, 1, side : 2 * side, :].astype(F32) * joined
        hb[b, 1, 0:side, :] = upper.astype(B16)
        hb[b, 0, (half + 1) * side : (half + 2) * side, :] = lower.astype(B16)


def silu_row(panel, load, columns, mean, rstd, gain, shift, i):
    mask = panel.mask(columns, i)
    normal = jnp.where(mask, (load(i) - mean) * rstd, 0.0)
    pre = normal * gain + shift
    half = 0.5 * pre
    return jnp.where(mask, half + half * jnp.tanh(half), 0.0)


def silu_shifted(panel, load, mean, rstd, gain, shift, hb, sender, out):
    columns = panel.columns()
    means = [panel.spread(mean, top) for top in range(2)]
    rstds = [panel.spread(rstd, top) for top in range(2)]

    def step(i, top, carry):
        row = silu_row(panel, load, columns, means[top], rstds[top], gain, shift, i)
        store_shifted(panel, hb, i, top, row, columns)
        return carry

    def after(top):
        if top == 1:
            store_edges(panel, hb)
        if sender is not None:
            send_shifted(panel, sender, hb, out, top)

    panel.loop(step, 0, after)


PIECES = 8
SENDS = 32


class Sender:
    def __init__(self, sems):
        self.sems, self.copies = sems, []

    def send(self, source, target):
        copy = pltpu.make_async_copy(source, target, self.sems.at[len(self.copies)])
        copy.start()
        self.copies.append(copy)

    def finish(self):
        for copy in self.copies:
            copy.wait()


def fetch(source, target, sem):
    copy = pltpu.make_async_copy(source, target, sem)
    copy.start()
    return copy


def send_shifted(panel, sender, hb, out, top):
    side, rows = panel.side, panel.half * panel.side
    for b in range(3):
        if top == 0:
            sender.send(hb.at[b, 0, pl.ds(side, rows), :], out.at[b, 0, pl.ds(side, rows), :])
        else:
            for start in (0, rows + side):
                place = pl.ds(start, side)
                sender.send(hb.at[b, 0, place, :], out.at[b, 0, place, :])
            sender.send(hb.at[b, 1], out.at[b, 1])


def send_half(panel, sender, source, out, top):
    rows = panel.half * panel.side
    place = pl.ds(top * rows, rows)
    sender.send(source.at[place, :], out.at[place, :])


def weight_copies(meta, pieces, first, held, sems, m):
    block = pieces[0].shape[1]
    slot = meta[M_FROM + MATS + first + m]
    other_slot = meta[M_FROM + 2 * MATS + first + m]
    copies = []
    for t in range(8):
        source = pieces[t].at[slot if t < 4 else other_slot]
        place = pl.ds(pl.multiple_of(meta[M_OFF + t], block), block)
        copies.append(pltpu.make_async_copy(source, held.at[m, place, :], sems.at[m, t]))
    return copies


class Whole:
    def __init__(self, matrices, held, sems):
        self.matrices, self.held, self.sems, self.copies = matrices, held, sems, {}

    def start(self, order):
        for m in order:
            self.copies[m] = fetch(self.matrices.at[m], self.held.at[m], self.sems.at[m, 0])

    def wait(self, m):
        self.copies[m].wait()


class Weights:
    def __init__(self, meta, pieces, first, held, sems):
        self.meta, self.pieces, self.first, self.held, self.sems = meta, pieces, first, held, sems

    def start(self, order):
        for m in order:
            for e in range(len(self.pieces) // PIECES):

                @pl.when(self.meta[M_FROM + self.first + m] == e)
                def _(e=e, m=m):
                    group = self.pieces[PIECES * e : PIECES * (e + 1)]
                    for copy in weight_copies(
                        self.meta, group, self.first, self.held, self.sems, m
                    ):
                        copy.start()

    def wait(self, m):
        block = self.pieces[0].shape[1]
        for t in range(PIECES):
            target = self.held.at[m, pl.ds(0, block), :]
            pltpu.make_async_copy(self.pieces[t].at[0], target, self.sems.at[m, t]).wait()


def start_taps(weights, shifted, hb, sems, flip):
    loads = []
    order = [tap for tap, _, _ in tap_order(flip)]
    for col in range(3):
        if shifted is not None:
            loads.append(fetch(shifted.at[col], hb.at[col], sems.at[col]))
        weights.start(order[3 * col : 3 * col + 3])
    return loads


def tap_order(flip):
    order = []
    for col in range(3):
        for row in range(3):
            a, b = (2 - row, 2 - col) if flip else (row, col)
            order.append((3 * a + b, row, col))
    return order


def conv_taps(panel, hb, loads, weights, top, dims, flip):
    side, pixels = panel.side, panel.half * panel.side
    total = jnp.zeros((pixels, panel.channels), F32)
    for tap, row, col in tap_order(flip):
        if top == 0:
            if row == 0 and loads is not None:
                loads[col].wait()
            weights.wait(tap)
        total = total + dot(
            hb[col, top, row * side : row * side + pixels, :], weights.held[tap], dims
        )
    return total


def cast_kernel(meta, master, mine, send):
    block = mine.shape[1]
    for out, half in ((mine, meta[M_CORE]), (send, 1 - meta[M_CORE])):
        place = pl.ds(pl.multiple_of(half * block, block), block)
        out[...] = master[:, place, :].astype(B16)


def first_kernel(side, meta, image, vec, hb_out, stats, hb, out_sems):
    panel = Panel(meta[M_KIND], side, image.shape[1])
    sender = Sender(out_sems)

    def load(i):
        return image[panel.rows(i), :].astype(F32)

    mean, rstd = norm_stats(panel, load, panel.same_group())
    stats[0:STAT, :] = mean
    stats[STAT:, :] = rstd
    silu_shifted(panel, load, mean, rstd, vec[0:1, :], vec[1:2, :], hb, sender, hb_out)
    sender.finish()


def norm_back(panel, load, stats, gain, same, gradient, emit, extra, after):
    columns = panel.columns()
    means = [panel.spread(stats[0:STAT], top) for top in range(2)]
    rstds = [panel.spread(stats[STAT:], top) for top in range(2)]

    def normal_of(i, top, mask):
        return jnp.where(mask, (load(i) - means[top]) * rstds[top], 0.0)

    def add(i, top, carry):
        mask = panel.mask(columns, i)
        normal = normal_of(i, top, mask)
        grad = gradient(i, mask, normal)
        return carry[0] + grad, carry[1] + grad * normal

    upper, lower = panel.loop(add, (panel.zero(), panel.zero()))
    plain = panel.quadrants(upper[0], lower[0])
    cross = panel.quadrants(upper[1], lower[1])
    plain_mean = panel.reduced(plain * gain, same)
    cross_mean = panel.reduced(cross * gain, same)
    plains = [panel.spread(plain_mean, top) for top in range(2)]
    crosses = [panel.spread(cross_mean, top) for top in range(2)]

    def finish(i, top, carry):
        mask = panel.mask(columns, i)
        normal = normal_of(i, top, mask)
        scaled = gradient(i, mask, None) * gain
        value = rstds[top] * (scaled - plains[top] - normal * crosses[top])
        return emit(i, top, jnp.where(mask, value, 0.0), carry, columns)

    found = panel.loop(finish, extra, after)
    grad_gain = jnp.sum(cross, axis=0, keepdims=True)
    grad_shift = jnp.sum(plain, axis=0, keepdims=True)
    return grad_gain, grad_shift, found


def store_parts(meta, staged, keep, send, m):
    block = keep.shape[2]
    for k in range(4):
        keep[k, m] = staged[pl.ds(pl.multiple_of(meta[M_KEEP + k], block), block), :].astype(B16)
        send[k, m] = staged[pl.ds(pl.multiple_of(meta[M_SEND + k], block), block), :].astype(B16)


TAP_SLOTS = 3


class Parts:
    def __init__(self, meta, staged, keep, send, targets, sems):
        self.meta, self.staged, self.keep, self.send = meta, staged, keep, send
        self.targets, self.sems, self.flying = targets, sems, []

    def put(self, value, m):
        n = len(self.flying)
        slot, staged = n % TAP_SLOTS, self.staged.at[n % 2]
        staged[...] = value
        if n >= TAP_SLOTS:
            for copy in self.flying[n - TAP_SLOTS]:
                copy.wait()
        store_parts(self.meta, staged, self.keep, self.send, slot)
        sources = (
            self.keep.at[:, slot],
            self.send.at[pl.ds(0, 2), slot],
            self.send.at[pl.ds(2, 2), slot],
        )
        self.flying.append(
            [
                fetch(source, target.at[:, m], self.sems.at[slot, k])
                for k, (source, target) in enumerate(zip(sources, self.targets))
            ]
        )

    def finish(self):
        for copies in self.flying[-TAP_SLOTS:]:
            for copy in copies:
                copy.wait()


def tap_grads_of(side, hb, loads, grad, parts):
    pixels = side * side // 2
    for tap, row, col in tap_order(False):
        if row == 0 and loads is not None:
            loads[col].wait()
        start = row * side
        parts.put(
            dot(hb[col, 0, start : start + pixels, :], grad[0:pixels, :], TN)
            + dot(hb[col, 1, start : start + pixels, :], grad[pixels:, :], TN),
            tap,
        )


def tap_kernel(side, meta, hb_in, grad_in, keep_to, near_to, pair_to, *refs):
    hb, grad, staged, keep, send, in_sems, out_sems = refs
    first = fetch(grad_in, grad, in_sems.at[3])
    loads = [fetch(hb_in.at[b], hb.at[b], in_sems.at[b]) for b in range(3)]
    first.wait()
    parts = Parts(meta, staged, keep, send, (keep_to, near_to, pair_to), out_sems)
    tap_grads_of(side, hb, loads, grad, parts)
    parts.finish()


def conv_kernel(side, count, meta, hb_in, image_in, vec, *refs):
    pieces, refs = refs[:count], refs[count:]
    middle_to, stats_two, hb_to, residual_to, stats, normed_to, weights_to = refs[:7]
    held_one, sems_one, held_two, sems_two, hb, middle, image, residual, normed, in_sems, out_sems = refs[7:]
    channels = residual.shape[1]
    panel = Panel(meta[M_KIND], side, channels)
    first = Weights(meta, pieces, 0, held_one, sems_one)
    second = Weights(meta, pieces, 9, held_two, sems_two)
    loads = start_taps(first, hb_in, hb, in_sems, False)
    sender = Sender(out_sems)
    same = panel.same_group()
    pixels = panel.half * side
    for top in range(2):
        middle[top * pixels : (top + 1) * pixels, :] = (
            conv_taps(panel, hb, loads, first, top, NN, False) + vec[2:3, :]
        )
        send_half(panel, sender, middle, middle_to, top)
        if top == 0:
            image_load = fetch(image_in, image, in_sems.at[3])
            start_taps(second, None, None, None, False)

    def middle_load(i):
        return middle[panel.rows(i), :]

    mean, rstd = norm_stats(panel, middle_load, same)
    stats_two[0:STAT, :] = mean
    stats_two[STAT:, :] = rstd
    silu_shifted(panel, middle_load, mean, rstd, vec[3:4, :], vec[4:5, :], hb, sender, hb_to)
    image_load.wait()
    for top in range(2):
        span = slice(top * pixels, (top + 1) * pixels)
        residual[span, :] = (
            image[span, :].astype(F32)
            + conv_taps(panel, hb, None, second, top, NN, False)
            + vec[5:6, :]
        )
        if top == 0:
            sender.send(held_two, weights_to)
        send_half(panel, sender, residual, residual_to, top)

    def residual_load(i):
        return residual[panel.rows(i), :]

    mean, rstd = norm_stats(panel, residual_load, same)
    stats[0:STAT, :] = mean
    stats[STAT:, :] = rstd
    columns = panel.columns()
    means = [panel.spread(mean, top) for top in range(2)]
    rstds = [panel.spread(rstd, top) for top in range(2)]

    def step(i, top, carry):
        value = (residual_load(i) - means[top]) * rstds[top]
        normal = jnp.where(panel.mask(columns, i), value, 0.0)
        normed[panel.rows(i), :] = (normal * vec[6:7, :] + vec[7:8, :]).astype(B16)
        return carry

    panel.loop(step, 0, lambda top: send_half(panel, sender, normed, normed_to, top))
    sender.finish()


def attention_kernel(side, count, meta, residual_in, stats, normed_in, grad_in, vec, *refs):
    pieces, refs = refs[:count], refs[count:]
    (block_to, d_residual_to, grad_to, eb_to, keep_to, near_to, pair_to, rows_out) = refs[:8]
    (held_attn, sems_attn, residual, normed, queries, keys, values, soft_low, d_scores,
     attended, d_attended, d_queries, d_keys, d_values, gout, d_normed, block_out, d_residual,
     d_middle, eb, staged, keep, send, in_sems, out_sems, part_sems) = refs[8:]
    channels = residual.shape[1]
    panel = Panel(meta[M_KIND], side, channels)
    normed_load = fetch(normed_in, normed, in_sems.at[3])
    third = Weights(meta, pieces, 18, held_attn, sems_attn)
    third.start(range(4))
    grad_load = fetch(grad_in, gout, in_sems.at[4])
    residual_copy = fetch(residual_in, residual, in_sems.at[5])
    sender = Sender(out_sems)
    parts = Parts(meta, staged, keep, send, (keep_to, near_to, pair_to), part_sems)
    same = panel.same_group()

    def residual_load(i):
        return residual[panel.rows(i), :]

    normed_load.wait()
    total = side * side
    block = total // 4
    inv_root = 1.0 / math.sqrt(channels)
    shift = side.bit_length() - 1

    def labels(pixel):
        i, j = pixel >> shift, pixel & (side - 1)
        quarter = jnp.where(i >= panel.half, 2, 0) + jnp.where(j >= panel.half, 1, 0)
        four = jnp.where(panel.kind == 2, 1, 0)
        lab = quarter * four
        return jnp.where((i < panel.limit) & (j < panel.limit), lab, -1)

    key_labels = labels(lax.broadcasted_iota(jnp.int32, (1, total), 1))

    def block_labels(n):
        return labels(lax.broadcasted_iota(jnp.int32, (block, 1), 0) + n * block)

    for m in range(4):
        third.wait(m)
    for n in range(4):
        span = slice(n * block, (n + 1) * block)
        rows = normed[span, :]
        queries[span, :] = (dot(rows, held_attn[0], NN) + vec[8:9, :]).astype(B16)
        keys[span, :] = dot(rows, held_attn[1], NN).astype(B16)
        values[span, :] = (dot(rows, held_attn[2], NN) + vec[9:10, :]).astype(B16)
    gout_sum = jnp.zeros((1, channels), F32)
    grad_load.wait()
    residual_copy.wait()
    for n in range(4):
        span = slice(n * block, (n + 1) * block)
        lab = block_labels(n)
        scores = dot(queries[span, :], keys[...], NT) * inv_root
        scores = jnp.where((lab == key_labels) & (key_labels >= 0), scores, MASK_FILL)
        top = jnp.max(scores, axis=-1, keepdims=True)
        grown = jnp.exp(scores - top)
        chances = grown * (1.0 / jnp.sum(grown, axis=-1, keepdims=True))
        soft_low[span, :] = chances.astype(B16)
        attended[span, :] = dot(soft_low[span, :], values[...], NN).astype(B16)
        projected = dot(attended[span, :], held_attn[3], NN) + vec[10:11, :]
        valid = lab >= 0
        block_out[span, :] = jnp.where(valid, residual[span, :] + projected, 0.0).astype(B16)
        grad = jnp.where(valid, gout[span, :].astype(F32), 0.0)
        gout_sum = gout_sum + jnp.sum(grad, axis=0, keepdims=True)
        gout[span, :] = grad.astype(B16)
        d_attended[span, :] = dot(gout[span, :], held_attn[3], NT).astype(B16)
    sender.send(block_out, block_to)
    for n in range(4):
        span = slice(n * block, (n + 1) * block)
        d_soft = dot(d_attended[span, :], values[...], NT)
        chances = soft_low[span, :].astype(F32)
        delta = jnp.sum(d_soft * chances, axis=-1, keepdims=True)
        d_scores[span, :] = (chances * (d_soft - delta)).astype(B16)
        d_queries[span, :] = (dot(d_scores[span, :], keys[...], NN) * inv_root).astype(B16)
    d_keys[...] = (dot(d_scores[...], queries[...], TN) * inv_root).astype(B16)
    d_values[...] = dot(soft_low[...], d_attended[...], TN).astype(B16)
    pairs = ((normed, d_queries), (normed, d_keys), (normed, d_values), (attended, gout))
    for m, (left, right) in enumerate(pairs):
        parts.put(dot(left[...], right[...], TN), m)
    for n in range(4):
        span = slice(n * block, (n + 1) * block)
        d_normed[span, :] = (
            dot(d_queries[span, :], held_attn[0], NT)
            + dot(d_keys[span, :], held_attn[1], NT)
            + dot(d_values[span, :], held_attn[2], NT)
        )

    def gradient(i, mask, normal):
        return jnp.where(mask, d_normed[panel.rows(i), :], 0.0)

    def emit(i, top, value, carry, columns):
        place = panel.rows(i)
        full = gout[place, :].astype(F32) + value
        d_residual[place, :] = full
        low = full.astype(B16)
        d_middle[place, :] = low
        row = low.astype(F32)
        store_shifted(panel, eb, i, top, row, columns)
        return (
            carry[0] + row,
            carry[1] + d_queries[place, :].astype(F32),
            carry[2] + d_values[place, :].astype(F32),
        )

    def after(top):
        send_half(panel, sender, d_residual, d_residual_to, top)
        send_half(panel, sender, d_middle, grad_to, top)
        if top == 1:
            store_edges(panel, eb)
        send_shifted(panel, sender, eb, eb_to, top)

    zero = panel.zero()
    grad_gain, grad_shift, found = norm_back(
        panel, residual_load, stats, vec[6:7, :], same, gradient, emit, (zero, zero, zero), after
    )
    sums = [jnp.sum(found[0][k] + found[1][k], axis=0, keepdims=True) for k in range(3)]
    rows_out[0:1, :] = sums[0]
    rows_out[1:2, :] = grad_gain
    rows_out[2:3, :] = grad_shift
    rows_out[3:4, :] = sums[1]
    rows_out[4:5, :] = sums[2]
    rows_out[5:6, :] = gout_sum
    rows_out[6:8, :] = jnp.zeros((2, channels), F32)
    parts.finish()
    sender.finish()


def back_kernel(side, last, count, meta, eb_in, source_in, stats, vec, *refs):
    if last:
        residual_in, pieces, refs = refs[0], refs[1 : 1 + count], refs[1 + count :]
        out_to, rows_out, held, sems, eb, source, slope, out, d_residual, in_sems, out_sems = refs
        first = 0
    else:
        pieces, refs = refs[:count], refs[count:]
        out_to, rows_out, held, sems, eb, source, slope, out, in_sems, out_sems = refs
        first = 3
    panel = Panel(meta[M_KIND], side, source.shape[1])
    if last:
        given = fetch(eb_in, out, in_sems.at[0])
        weights, loads = Weights(meta, pieces, 0, held, sems), None
        start_taps(weights, None, None, None, True)
    else:
        weights = Whole(pieces[0], held, sems)
        loads = start_taps(weights, eb_in, eb, in_sems, True)
    later = [fetch(source_in, source, in_sems.at[3])]
    if last:
        later.append(fetch(residual_in, d_residual, in_sems.at[4]))
    sender = Sender(out_sems)
    same = panel.same_group()
    gain, shift = vec[first : first + 1, :], vec[first + 1 : first + 2, :]
    if last:
        columns = panel.columns()
        given.wait()

        def widen(i, top, carry):
            row = out[panel.rows(i), :].astype(F32)
            store_shifted(panel, eb, i, top, row, columns)
            return carry

        panel.loop(widen, 0)
        store_edges(panel, eb)
    pixels = panel.half * side
    for top in range(2):
        slope[top * pixels : (top + 1) * pixels, :] = conv_taps(
            panel, eb, loads, weights, top, NT, True
        )
    for copy in later:
        copy.wait()

    def load(i):
        return source[panel.rows(i), :].astype(F32)

    def gradient(i, mask, normal):
        place = panel.rows(i)
        if normal is None:
            return slope[place, :]
        pre = normal * gain + shift
        sig = 0.5 + 0.5 * jnp.tanh(0.5 * pre)
        value = jnp.where(mask, slope[place, :] * (sig * (1.0 + pre * (1.0 - sig))), 0.0)
        slope[place, :] = value
        return value

    def emit(i, top, value, carry, columns):
        place = panel.rows(i)
        if last:
            out[place, :] = (d_residual[place, :] + value).astype(B16)
            return carry
        low = value.astype(B16)
        out[place, :] = low
        return carry + low.astype(F32)

    def after(top):
        send_half(panel, sender, out, out_to, top)

    grad_gain, grad_shift, found = norm_back(
        panel, load, stats, gain, same, gradient, emit, 0 if last else panel.zero(), after
    )
    channels = panel.channels
    rows_out[0:1, :] = grad_gain
    rows_out[1:2, :] = grad_shift
    if last:
        rows_out[2:8, :] = jnp.zeros((6, channels), F32)
    else:
        rows_out[2:3, :] = jnp.sum(found[0] + found[1], axis=0, keepdims=True)
        rows_out[3:8, :] = jnp.zeros((5, channels), F32)
    sender.finish()


def slot_kernel(owner, *refs):
    terms, second, third, out = refs[:4], refs[4], refs[5], refs[6]
    out[...] = jnp.zeros(out.shape, out.dtype)
    for m in range(MATS):
        if m < 9:
            total = terms[0][0, m].astype(F32)
            for term in terms[1:]:
                total = total + term[0, m].astype(F32)
            out[owner[m]] = total.astype(out.dtype)
        else:
            out[owner[m]] = second[m - 9] if m < 18 else third[m - 18]


def adam_kernel(meta, master, first, second, mine, other, new_first, new_second, new_master, grad):
    block = mine.shape[1]
    core = meta[M_CORE]
    grad[pl.ds(pl.multiple_of(core * block, block), block), :] = mine[0].astype(F32)
    grad[pl.ds(pl.multiple_of((1 - core) * block, block), block), :] = other[0].astype(F32)
    results = adam_update(master[0], first[0], second[0], grad[...], LEARN_RATE)
    new_first[0], new_second[0], new_master[0] = results


def on_panel(
    image_in,
    panel_kind,
    owner_slot,
    out_grad,
    master,
    first_moment,
    second_moment,
    vec_master,
    vec_first,
    vec_second,
):
    side, channels = image_in.shape[2], image_in.shape[3]
    imgs = lax.axis_size("imgs")
    chips = imgs // 2
    own, depth = master.shape[0], master.shape[1]
    block = depth // 2
    total = side * side
    group, row = lax.axis_index("imgs"), lax.axis_index("rows")
    core, chip = group % 2, group // 2

    def permutation(target):
        pairs = []
        for i in range(imgs):
            for r in range(4):
                to_i, to_r = target(i, r)
                pairs.append((i * 4 + r, to_i * 4 + to_r))
        return pairs

    to_core = permutation(lambda i, r: (i ^ 1, r))
    to_near = [permutation(lambda i, r, k=k: (i, r ^ k)) for k in range(4)]
    to_first = permutation(lambda i, r: (i, r ^ (1 + i % 2)))
    to_second = permutation(lambda i, r: (i, r ^ (2 - i % 2)))
    to_chip = [permutation(lambda i, r, d=d: ((i + 2 * d) % imgs, r)) for d in range(chips)]
    across_chip = [permutation(lambda i, r, e=e: (i ^ (2 * e), r)) for e in range(chips)]

    def move(value, pairs):
        return lax.ppermute(value, AXES, pairs)

    tie = lax.optimization_barrier
    wide = shaped((total, channels), F32)
    narrow = shaped((total, channels), B16)
    stat = shaped((2 * STAT, channels), F32)
    shifted = shaped((3, 2, (side // 2 + 2) * side, channels), B16)
    vec_rows = shaped((8, channels), F32)
    held_shifted = pltpu.VMEM(shifted.shape, B16)
    held_wide = pltpu.VMEM((total, channels), F32)
    held_narrow = pltpu.VMEM((total, channels), B16)
    loads, sends = pltpu.SemaphoreType.DMA((6,)), pltpu.SemaphoreType.DMA((SENDS,))
    near_first, near_second = row ^ (1 + core), row ^ (2 - core)
    quarters = [row, near_first, near_second, row ^ 3, row, near_second, near_first, row ^ 3]
    halves = [core] * 4 + [1 - core] * 4
    kind = lax.dynamic_index_in_dim(panel_kind, row, keepdims=False)
    slot_chip, slot_core = owner_slot // (2 * own), (owner_slot // own) % 2
    place = owner_slot % own + jnp.where(slot_core == core, 0, own)
    meta = jnp.stack(
        [kind, core]
        + [q * depth + h * block for q, h in zip(quarters, halves)]
        + [q * depth + core * block for q in (row, near_second, near_first, row ^ 3)]
        + [q * depth + (1 - core) * block for q in (row, near_first, near_second, row ^ 3)]
    ).astype(jnp.int32)
    away = chip ^ slot_chip
    third = jnp.where(away == 3, 2 * own, 0)
    meta = jnp.concatenate(
        [meta, jnp.minimum(away, 2), place + third, (place ^ own) + third]
    ).astype(jnp.int32)
    image = lax.all_to_all(image_in, "rows", 0, 0, tiled=True).reshape(total, channels)

    low = shaped((own, block, channels), B16)
    core_only = jnp.stack([jnp.zeros_like(core), core]).astype(jnp.int32)
    mine, send = call(
        cast_kernel, (low, low), [SSPEC, VSPEC], (VSPEC, VSPEC), [], (core_only, master), vmem=16
    )
    here = jnp.concatenate([mine, move(send, to_core)], axis=0)

    arrived = [here] + [move(here, across_chip[e]) for e in range(1, chips)]
    hb_one, stats_one = call(
        functools.partial(first_kernel, side),
        (shifted, stat),
        [SSPEC, VSPEC, VSPEC],
        (ASPEC, VSPEC),
        [held_shifted, sends],
        (meta, image, vec_master),
        moved=5 * total * channels * 2,
    )
    rounds = arrived[:2]
    if chips == 4:
        rounds.append(jnp.concatenate(arrived[2:], axis=0))
    pieces, before = [], None
    for e, part in enumerate(rounds):
        if e == 1:
            part, before, hb_one = tie((part, before, hb_one))
        elif e == 2:
            part, before = tie((part, before))
        near, far = move(part, to_first), move(part, to_second)
        if e == 2:
            near, far, pieces[PIECES + 3] = tie((near, far, pieces[PIECES + 3]))
        corner = move(near, to_second)
        before = [near, far] if e == 0 else [near, far, pieces[3]]
        held = [part, near, far, corner]
        pieces += held + [move(piece, to_core) for piece in held]
    out_grad, pieces[-5] = tie((out_grad, pieces[-5]))
    count = len(pieces)

    def weight_scratch(n):
        return [pltpu.VMEM((n, channels, channels), B16), pltpu.SemaphoreType.DMA((n, 8))]

    conv_flops = 2 * total * 9 * channels * channels
    conv_bytes = 9 * channels * channels * 2 + 8 * total * channels

    cotangent = lax.all_to_all(out_grad, "rows", 0, 0, tiled=True).reshape(total, channels)
    parts_of = lambda n, m: shaped((n, m, block, channels), B16)
    slots = pltpu.VMEM((4, TAP_SLOTS, block, channels), B16)
    part_scratch = [pltpu.VMEM((2, channels, channels), F32), slots, slots]
    part_sems = pltpu.SemaphoreType.DMA((TAP_SLOTS, 3))
    pixel_pairs = [pltpu.VMEM((total, total), B16)] * 2
    middle, stats_two, hb_two, residual, stats_three, normed, weights_two = call(
        functools.partial(conv_kernel, side, count),
        (wide, stat, shifted, wide, stat, narrow, shaped((9, channels, channels), B16)),
        [SSPEC, ASPEC, ASPEC, VSPEC] + [ASPEC] * count,
        (ASPEC, VSPEC, ASPEC, ASPEC, VSPEC, ASPEC, ASPEC),
        weight_scratch(9)
        + weight_scratch(9)
        + [held_shifted, held_wide, held_narrow, held_wide, held_narrow, loads, sends],
        [meta, hb_one, image, vec_master] + pieces,
        flops=2 * conv_flops,
        moved=conv_bytes,
    )
    (block_out, d_residual, d_middle_two, eb_two, keep_a, near_a, pair_a, rows_attn) = call(
        functools.partial(attention_kernel, side, count),
        (narrow, wide, narrow, shifted, parts_of(4, 4), parts_of(2, 4), parts_of(2, 4), vec_rows),
        [SSPEC, ASPEC, VSPEC, ASPEC, ASPEC, VSPEC] + [ASPEC] * count,
        (ASPEC,) * 7 + (VSPEC,),
        weight_scratch(4)
        + [held_wide, held_narrow]
        + [held_narrow] * 3
        + pixel_pairs
        + [held_narrow] * 6
        + [held_wide, held_narrow, held_wide, held_narrow, held_shifted]
        + part_scratch
        + [loads, sends, part_sems],
        [meta, residual, stats_three, normed, cotangent, vec_master] + pieces,
        flops=4 * conv_flops,
        moved=2 * conv_bytes,
    )

    def tap_grads(hb, grad):
        return call(
            functools.partial(tap_kernel, side),
            (parts_of(4, 9), parts_of(2, 9), parts_of(2, 9)),
            [SSPEC, ASPEC, ASPEC],
            (ASPEC,) * 3,
            [held_shifted, held_narrow] + part_scratch + [loads, part_sems],
            (meta, hb, grad),
            flops=conv_flops,
            moved=conv_bytes,
        )

    def added(*terms):
        return sum((v.astype(F32) for v in terms[1:]), terms[0].astype(F32)).astype(B16)

    chip_groups = [list(range(c, imgs, 2)) for c in range(2)]

    def pair_of(keep, got):
        return added(keep[2:4], got[1])

    def quarter_of(keep, got, arrived, k):
        return added(keep[k], got[0][k], arrived[k])

    def from_core(near, pair):
        return move(near, to_core), move(pair, to_core)

    got_attn = from_core(near_a, pair_a)
    d_middle_one, rows_two = call(
        functools.partial(back_kernel, side, False, 1),
        (narrow, vec_rows),
        [SSPEC, ASPEC, ASPEC, VSPEC, VSPEC] + [ASPEC],
        (ASPEC, VSPEC),
        weight_scratch(9)
        + [held_shifted, held_wide, held_wide, held_narrow, loads, sends],
        [meta, eb_two, middle, stats_two, vec_master, weights_two],
        flops=conv_flops,
        moved=conv_bytes,
    )
    got_attn, d_middle_two, d_middle_one = tie((got_attn, d_middle_two, d_middle_one))
    pair_attn, d_middle_two = tie((pair_of(keep_a, got_attn), d_middle_two))
    arrived_attn = move(pair_attn, to_first)
    keep_two, near_two, pair_two = tap_grads(hb_two, d_middle_two)
    got_two = from_core(near_two, pair_two)
    send_attn = quarter_of(keep_a, got_attn, arrived_attn, 1)
    send_attn, near_two, d_middle_one = tie((send_attn, near_two, d_middle_one))
    quarter_attn = move(send_attn, to_second)
    keep_one, near_one, pair_one = tap_grads(hb_one, d_middle_one)
    got_one = from_core(near_one, pair_one)
    got_two, near_one = tie((got_two, near_one))
    pair_two = pair_of(keep_two, got_two)
    arrived_two = move(pair_two, to_first)
    pair_one = pair_of(keep_one, got_one)
    pair_two, pair_one, d_middle_one = tie((pair_two, pair_one, d_middle_one))
    arrived_one = move(pair_one, to_first)
    d_image, rows_one = call(
        functools.partial(back_kernel, side, True, count),
        (narrow, vec_rows),
        [SSPEC, ASPEC, ASPEC, VSPEC, VSPEC, ASPEC] + [ASPEC] * count,
        (ASPEC, VSPEC),
        weight_scratch(9)
        + [held_shifted, held_narrow, held_wide, held_narrow, held_wide, loads, sends],
        [meta, d_middle_one, image, stats_one, vec_master, d_residual] + pieces,
        flops=conv_flops,
        moved=conv_bytes,
    )
    arrived_two, d_image = tie((arrived_two, d_image))
    send_two = quarter_of(keep_two, got_two, arrived_two, 1)
    send_two, rows_one = tie((send_two, rows_one))
    quarter_two = move(send_two, to_second)
    vec_grads = jnp.concatenate([rows_one[0:2], rows_two[2:3], rows_two[0:2], rows_attn[0:6]])
    vec_grads = vec_grads + move(vec_grads, to_core)
    if chips == 4:
        far = [move(vec_grads, across_chip[e]) for e in range(1, 4)]
        vec_grads = (vec_grads + far[0]) + (far[1] + far[2])
    elif chips == 2:
        vec_grads = vec_grads + move(vec_grads, across_chip[1])
    quarter_one = move(quarter_of(keep_one, got_one, arrived_one, 1), to_second)
    sum_two = added(quarter_of(keep_two, got_two, arrived_two, 0), quarter_two)
    sum_attn = added(quarter_of(keep_a, got_attn, arrived_attn, 0), quarter_attn)
    quarter_one, sum_two, sum_attn, vec_grads = tie((quarter_one, sum_two, sum_attn, vec_grads))
    slots_shape = shaped((chips * 2 * own, block, channels), B16)
    one = pl.BlockSpec((1, 9, block, channels), lambda t: (0, 0, 0, 0))
    slot_terms = call(
        slot_kernel,
        slots_shape,
        [SSPEC, one, one, one, one] + [pl.BlockSpec(v.shape, lambda t: (0, 0, 0)) for v in (sum_two, sum_attn)],
        pl.BlockSpec(slots_shape.shape, lambda t: (0, 0, 0)),
        [],
        [owner_slot, keep_one, got_one[0], arrived_one, quarter_one[None], sum_two, sum_attn],
        grid=(1,),
        vmem=24,
    )
    by_chip = lax.all_to_all(
        slot_terms, "imgs", 0, 0, tiled=True, axis_index_groups=chip_groups
    ).reshape(chips, 2 * own, block, channels)

    def slots_of(which):
        terms = lax.dynamic_slice_in_dim(by_chip, which * own, own, axis=1)
        return added(*[terms[d] for d in range(chips)])

    slot_terms, vec_grads, d_image = tie((slot_terms, vec_grads, d_image))
    near = [move(vec_grads, to_near[k]) for k in range(1, 4)]
    vec_grads = (vec_grads + near[0]) + (near[1] + near[2])
    strips = jnp.stack([block_out, d_image]).reshape(2, 4, side // 4, side, channels)
    strip = lambda k: lax.dynamic_index_in_dim(strips, row ^ k, axis=1, keepdims=False)
    strips = [strip(0)] + [move(strip(k), to_near[k]) for k in range(1, 4)]
    odd, high = row % 2 == 1, row >= 2
    strips = [jnp.where(odd, strips[k ^ 1], strips[k]) for k in range(4)]
    strips = [jnp.where(high, strips[k ^ 2], strips[k]) for k in range(4)]
    block_out = jnp.stack([strip[0] for strip in strips])
    input_grad = jnp.stack([strip[1] for strip in strips])

    send = slots_of(1 - core)
    by_chip, block_out, input_grad, vec_grads = tie((by_chip, block_out, input_grad, vec_grads))
    mine, other = slots_of(core), move(send, to_core)
    deep = pl.BlockSpec((1, depth, channels), lambda t: (t, 0, 0))
    flat = pl.BlockSpec((1, block, channels), lambda t: (t, 0, 0))
    slot_shape = shaped(master.shape, F32)
    new_first, new_second, new_master = call(
        adam_kernel,
        (slot_shape,) * 3,
        [SSPEC, deep, deep, deep, flat, flat],
        (deep,) * 3,
        [pltpu.VMEM((depth, channels), F32)],
        (meta, master, first_moment, second_moment, mine, other),
        moved=6 * own * depth * channels * 4,
        grid=(own,),
        vmem=16,
    )
    vec_results = adam_update(vec_master, vec_first, vec_second, vec_grads, VEC_RATE)
    return (block_out, input_grad, new_first, new_second, new_master) + vec_results


def on_slice(*args):
    image_in = args[0]
    panels, row_count, col_count, channels = image_in.shape
    rows, imgs = lax.axis_size("rows"), lax.axis_size("imgs")
    chips = imgs // 2
    whole_panels = (
        rows == 4
        and panels == rows
        and row_count * rows == col_count == 32
        and channels == 512
        and args[4].shape[0] == 4
        and imgs == 2 * chips
        and args[2].shape[0] == MATS
        and chips in (1, 2, 4)
    )
    return on_panel(*args) if whole_panels else on_device(*args)


def solution(mesh):
    in_specs = (
        P("imgs", "rows", None, None),
        P("imgs"),
        P(),
        P("imgs", "rows", None, None),
        P("imgs", "rows", None),
        P("imgs", "rows", None),
        P("imgs", "rows", None),
        P(),
        P(),
        P(),
    )
    out_specs = (
        P("imgs", "rows", None, None),
        P("imgs", "rows", None, None),
        P("imgs", "rows", None),
        P("imgs", "rows", None),
        P("imgs", "rows", None),
        P(),
        P(),
        P(),
    )
    return jax.shard_map(
        on_slice, mesh=mesh, in_specs=in_specs, out_specs=out_specs, check_vma=False
    )
```
